32 devices in a mesh: blk: 8 (over y, x, core), ulysses: 4 (over z).
Axes of the slice: x: 2, y: 2, z: 4, core: 2. Of those that a mesh axis runs over, the one named last changes fastest.
Arguments:
- queries: bfloat16 [4096, 2048], P(('blk', 'ulysses')), may hold values from -6 to 6
- key_states: bfloat16 [4096, 512], P(('blk', 'ulysses')), may hold values from -6 to 6
- value_states: bfloat16 [4096, 512], P(('blk', 'ulysses')), may hold values from -6 to 6
- attn_out: bfloat16 [4096, 2048], P(('blk', 'ulysses')), may hold values from -6 to 6
- grad_out: bfloat16 [4096, 2048], P(('blk', 'ulysses')), may hold values from -6 to 6
- log_sums: float32 [4096, 32], P(('blk', 'ulysses')), may hold values from 2 to 4
- owners: int32 [16], replicated, may hold values from 0 to 15, as said below
Outputs:
- grad_query: bfloat16 [4096, 2048], P(('blk', 'ulysses'))
- grad_key: bfloat16 [4096, 512], P(('blk', 'ulysses'))
- grad_value: bfloat16 [4096, 512], P(('blk', 'ulysses'))
The draws below stay inside these ranges and needn't reach their ends.
Inputs may be any that keep to these rules, and one draw needn't show every extreme that they name: `owners`: every value 0 to 15 appears exactly once; each sequence block holds one half-block below 8 and the half-block 2 * 8 - 1 minus it.
All inputs are finite; a program needn't handle non-finite values.
Results may differ from the reference program's by a relative error of at most 0.0049.
Values may be sent and summed in bfloat16 or wider, within the bound.
No kernel may reach another device: no remote copies, remote signals or barrier semaphores. Data moves between devices by JAX's collectives and lax.ppermute only.
A program may use at most 64 MiB of HBM per device.

```python
import math
import jax
import jax.numpy as jnp
from jax import lax

HEADS = 32
KV_HEADS = 8
HEAD_DIM = 64
TOK_DEV = 128
SEQ = 4096
N_BLK = 8
N_ULYSSES = 4


def draw_owners(key, part):
    first_key = jax.random.fold_in(key, 11)
    second_key = jax.random.fold_in(key, 23)
    lower = jax.random.permutation(first_key, N_BLK).astype(jnp.int32)
    flipped = jax.random.randint(second_key, (N_BLK,), 0, 2).astype(jnp.int32)
    upper = (2 * N_BLK - 1 - lower).astype(jnp.int32)
    leading = jnp.where(flipped == 1, upper, lower)
    trailing = jnp.where(flipped == 1, lower, upper)
    return jnp.stack([leading, trailing], axis=1).reshape(-1).astype(jnp.int32)


def steps_of(key, dims, split, least, high):
    loudness, own = 1.0, jax.random.fold_in(key, 6)
    for axis_at, blocks in split:
        draws = jnp.exp(jax.random.uniform(jax.random.fold_in(own, axis_at), (blocks,), jnp.float32, least / len(split), high / len(split)))
        loudness = loudness * jnp.repeat(draws, dims[axis_at] // blocks).reshape([-1 if axis == axis_at else 1 for axis in range(len(dims))])
    return loudness


def bell_draw(rng, dims, spread, most, pieces=(), kind=jnp.bfloat16):
    entries = spread * jax.random.normal(rng, dims, jnp.float32)
    if pieces:
        entries = entries * steps_of(rng, dims, pieces, -0.22, 0.18)
    return jnp.clip(entries, -most, most).astype(kind)


def setup_inputs(seed: int = 0) -> dict:
    keys = jax.random.split(jax.random.key(seed), 8)
    return {
        "queries": bell_draw(keys[0], (SEQ, HEADS * HEAD_DIM), 1.0, 6.0, ((0, 32),)),
        "key_states": bell_draw(keys[1], (SEQ, KV_HEADS * HEAD_DIM), 1.0, 6.0, ((0, 32),)),
        "value_states": bell_draw(keys[2], (SEQ, KV_HEADS * HEAD_DIM), 1.0, 6.0, ((0, 32),)),
        "attn_out": bell_draw(keys[3], (SEQ, HEADS * HEAD_DIM), 1.0, 6.0, ((0, 32),)),
        "grad_out": bell_draw(keys[4], (SEQ, HEADS * HEAD_DIM), 1.0, 6.0, ((0, 32),)),
        "log_sums": jnp.clip(2.0 + 2.0 * jax.random.uniform(keys[5], (SEQ, HEADS), jnp.float32) ** steps_of(keys[5], (SEQ, HEADS), ((0, 32),), -0.2, 0.2), 2.0, 4.0),
        "owners": draw_owners(jax.random.fold_in(keys[7], 71), 0),
    }


def block_grads(query_blk, grad_blk, key_blk, value_blk, sums_blk, delta_blk, query_pos, key_pos):
    wide = jnp.float32
    factor = 1.0 / math.sqrt(HEAD_DIM)
    scores = jnp.einsum('qhgd,khd->hgqk', query_blk.astype(wide), key_blk.astype(wide)) * factor
    sums_t = jnp.transpose(sums_blk, (1, 2, 0))[..., None]
    delta_t = jnp.transpose(delta_blk, (1, 2, 0))[..., None]
    visible = query_pos[:, None] >= key_pos[None, :]
    probs = jnp.where(visible, jnp.exp(scores - sums_t), 0.0)
    probs_b = probs.astype(jnp.bfloat16)
    grad_value = jnp.einsum('hgqk,qhgd->khd', probs_b.astype(wide), grad_blk.astype(wide))
    dprobs = jnp.einsum('qhgd,khd->hgqk', grad_blk.astype(wide), value_blk.astype(wide))
    dscores = (probs * (dprobs - delta_t) * factor).astype(jnp.bfloat16)
    grad_query = jnp.einsum('hgqk,khd->qhgd', dscores.astype(wide), key_blk.astype(wide))
    grad_key = jnp.einsum('hgqk,qhgd->khd', dscores.astype(wide), query_blk.astype(wide))
    count = query_blk.shape[0]
    return (grad_query.astype(jnp.bfloat16).reshape(count, -1), grad_key.astype(jnp.bfloat16).reshape(count, -1), grad_value.astype(jnp.bfloat16).reshape(count, -1))

def select_rank(array, index):
    return lax.dynamic_index_in_dim(array, index, 0, keepdims=False)

def reference(queries, key_states, value_states, attn_out, grad_out, log_sums, owners):
    group_tok = TOK_DEV * N_ULYSSES
    half = group_tok // 2
    group = HEADS // KV_HEADS
    delta = lax.optimization_barrier(jnp.sum((grad_out.astype(jnp.float32) * attn_out.astype(jnp.float32)).reshape(-1, HEADS, HEAD_DIM), axis=2))
    query_shape = (N_BLK, group_tok, KV_HEADS, group, HEAD_DIM)
    query_all = queries.reshape(query_shape)
    grad_all = grad_out.reshape(query_shape)
    key_all = key_states.reshape(N_BLK, group_tok, KV_HEADS, HEAD_DIM)
    value_all = value_states.reshape(N_BLK, group_tok, KV_HEADS, HEAD_DIM)
    sums_all = log_sums.reshape(N_BLK, group_tok, KV_HEADS, group)
    delta_all = delta.reshape(N_BLK, group_tok, KV_HEADS, group)
    offsets = jnp.arange(group_tok, dtype=jnp.int32)

    def one_rank(rank):
        before = (rank - 1) % N_BLK
        query_pos = jnp.take(owners, 2 * rank + offsets // half) * half + offsets % half
        key_pos = jnp.take(owners, 2 * before + offsets // half) * half + offsets % half
        return block_grads(select_rank(query_all, rank), select_rank(grad_all, rank), select_rank(key_all, before), select_rank(value_all, before), select_rank(sums_all, rank), select_rank(delta_all, rank), query_pos, key_pos)
    grad_query, grad_key, grad_value = lax.map(one_rank, jnp.arange(N_BLK, dtype=jnp.int32))
    grad_query = grad_query.reshape(-1, HEADS * HEAD_DIM)
    grad_key = jnp.roll(grad_key, -1, axis=0).reshape(-1, KV_HEADS * HEAD_DIM)
    grad_value = jnp.roll(grad_value, -1, axis=0).reshape(-1, KV_HEADS * HEAD_DIM)
    return (grad_query, grad_key, grad_value)
```

```python
import functools
import math

import jax
import jax.numpy as jnp
from jax import lax
from jax.experimental import pallas as pl
from jax.experimental.pallas import tpu as pltpu
from jax.sharding import PartitionSpec as P

HEAD_DIM = 64
LOG2E = math.log2(math.e)
BF16 = jnp.bfloat16
F32 = jnp.float32
VMEM = pl.BlockSpec(memory_space=pltpu.VMEM)
SMEM = pl.BlockSpec(memory_space=pltpu.SMEM)


def dot(a, b, a_dim, b_dim):
    return lax.dot_general(
        a, b, (((a_dim,), (b_dim,)), ((), ())), preferred_element_type=F32
    )


def pack_kernel(flags, q, do, k, v, q_send, do_send, kv_same, kv_other):
    half = q_send.shape[1]
    part = k.shape[1] // 2

    def write(mine):
        other = 1 - mine
        q_send[...] = q[:, other * half : (other + 1) * half]
        do_send[...] = do[:, other * half : (other + 1) * half]
        kv_same[:, :part] = k[:, mine * part : (mine + 1) * part]
        kv_same[:, part:] = v[:, mine * part : (mine + 1) * part]
        kv_other[:, :part] = k[:, other * part : (other + 1) * part]
        kv_other[:, part:] = v[:, other * part : (other + 1) * part]

    @pl.when(flags[0] == 0)
    def _():
        write(0)

    @pl.when(flags[0] == 1)
    def _():
        write(1)


def stats_kernel(flags, do, o, sums, stat_own, stat_send):
    tokens, width = do.shape
    heads = sums.shape[1]
    prod = do[...].astype(F32) * o[...].astype(F32)
    high = prod.astype(BF16)
    low = (prod - high.astype(F32)).astype(BF16)
    row = lax.broadcasted_iota(jnp.int32, (heads, width), 0)
    col = lax.broadcasted_iota(jnp.int32, (heads, width), 1)
    pick = jnp.where(col // HEAD_DIM == row, 1.0, 0.0).astype(BF16)
    delta = dot(pick, high, 1, 1) + dot(pick, low, 1, 1)
    lse = jnp.transpose(sums[...]) * LOG2E
    n = heads // 2

    def write(mine):
        other = 1 - mine
        stat_own[:n, :] = lse[mine * n : (mine + 1) * n, :]
        stat_own[n:, :] = delta[mine * n : (mine + 1) * n, :]
        stat_send[:n, :] = lse[other * n : (other + 1) * n, :]
        stat_send[n:, :] = delta[other * n : (other + 1) * n, :]

    @pl.when(flags[0] == 0)
    def _():
        write(0)

    @pl.when(flags[0] == 1)
    def _():
        write(1)


def grads_kernel(shards, flags, q, do, q_in, do_in, st, st_in, *rest):
    kv = rest[:shards]
    dq_own, dq_send = rest[shards : shards + 2]
    dkv = rest[shards + 2 : 2 * shards + 2]
    dq_acc = rest[2 * shards + 2]
    tok = q.shape[0]
    heads = st.shape[0] // 2
    kv_heads = kv[0].shape[1] // 2 // HEAD_DIM
    group = heads // kv_heads
    side = shards // 2
    keys = side * tok
    part = kv_heads * HEAD_DIM
    factor = 1.0 / math.sqrt(HEAD_DIM)
    mine = flags[0]
    width = 2 * HEAD_DIM
    dq_acc[...] = jnp.zeros_like(dq_acc)

    def spread(block, odd):
        one = block[:, HEAD_DIM:] if odd else block[:, :HEAD_DIM]
        zero = jnp.zeros_like(one)
        return jnp.concatenate(
            [jnp.concatenate([one, zero], 1), jnp.concatenate([zero, one], 1)], 0
        )

    def fold(wide, odd):
        top, low = wide[:keys], wide[keys:]
        if odd:
            return pltpu.roll(top, HEAD_DIM, 1) + low
        return top + pltpu.roll(low, HEAD_DIM, 1)

    def one_side(near):
        members = range(side) if near else range(side, shards)
        base = pl.multiple_of(mine * (heads * HEAD_DIM), heads * HEAD_DIM)
        for pair in range(kv_heads // 2):
            k_cols = slice(pair * width, (pair + 1) * width)
            v_cols = slice(part + pair * width, part + (pair + 1) * width)
            k_two = jnp.concatenate([kv[m][:, k_cols] for m in members], 0)
            v_two = jnp.concatenate([kv[m][:, v_cols] for m in members], 0)
            folded_k, folded_v = [], []
            for odd in range(2):
                kv_head = 2 * pair + odd
                k_wide, v_wide = spread(k_two, odd), spread(v_two, odd)
                k_turned = jnp.transpose(k_wide)
                dk, dv = None, None
                for t in range(group // 2):
                    head = kv_head * group + 2 * t
                    at = head * HEAD_DIM
                    cols = pl.ds(pl.multiple_of(base + at, width), width)
                    q_two = jnp.concatenate([q[:, cols], q_in[:, at : at + width]], 0)
                    do_two = jnp.concatenate([do[:, cols], do_in[:, at : at + width]], 0)
                    scores = dot(k_wide, q_two, 1, 1)
                    dprobs = dot(v_wide, do_two, 1, 1)

                    def rows(first):
                        lines = [
                            jnp.concatenate(
                                [st[first + i : first + i + 1, :], st_in[first + i : first + i + 1, :]], 1
                            )
                            for i in range(2)
                        ]
                        return lines

                    lse, delta = rows(head), rows(heads + head)
                    probs_b, dscores = [], []
                    for i in range(2):
                        s = scores[i * keys : (i + 1) * keys]
                        d = dprobs[i * keys : (i + 1) * keys]
                        p = jnp.exp2(s * (factor * LOG2E) - lse[i])
                        probs_b.append(p.astype(BF16))
                        dscores.append((p * (d - delta[i])).astype(BF16))
                    probs_b = jnp.concatenate(probs_b, 0)
                    dscores = jnp.concatenate(dscores, 0)
                    dv_t = dot(probs_b, do_two, 1, 0)
                    dk_t = dot(dscores, q_two, 1, 0)
                    dv = dv_t if dv is None else dv + dv_t
                    dk = dk_t if dk is None else dk + dk_t
                    turned = dot(k_turned, dscores, 1, 0)
                    dq_acc[at : at + width, :] += turned
                folded_k.append(fold(dk, odd))
                folded_v.append(fold(dv, odd))
            lane = lax.broadcasted_iota(jnp.int32, (keys, width), 1)
            dk = (jnp.where(lane < HEAD_DIM, folded_k[0], folded_k[1]) * factor).astype(BF16)
            dv = jnp.where(lane < HEAD_DIM, folded_v[0], folded_v[1]).astype(BF16)
            for i, m in enumerate(members):
                dkv[m][:, k_cols] = dk[i * tok : (i + 1) * tok]
                dkv[m][:, v_cols] = dv[i * tok : (i + 1) * tok]

    def one_side_or_zero(near):
        seen = flags[1] if near else flags[2]

        @pl.when(seen != 0)
        def _():
            one_side(near)

        @pl.when(seen == 0)
        def _():
            for m in range(side) if near else range(side, shards):
                dkv[m][...] = jnp.zeros_like(dkv[m])

    one_side_or_zero(True)
    one_side_or_zero(False)
    for at in range(0, heads * HEAD_DIM, width):
        out = jnp.transpose(dq_acc[at : at + width, :]) * factor
        out = out.astype(BF16)
        dq_own[:, at : at + width] = out[:tok]
        dq_send[:, at : at + width] = out[tok:]


def join_kernel(shards, flags, dq_own, dq_back, *rest):
    back = rest[:shards]
    gq, gk, gv = rest[shards:]
    half = dq_own.shape[1]
    part = gk.shape[1] // 2

    def write(mine):
        other = 1 - mine
        gq[:, mine * half : (mine + 1) * half] = dq_own[...]
        gq[:, other * half : (other + 1) * half] = dq_back[...]
        for parity in range(2):
            total = back[parity][...].astype(F32)
            for m in range(parity + 2, shards, 2):
                total = total + back[m][...].astype(F32)
            total = total.astype(BF16)
            place = mine if parity == 0 else other
            gk[:, place * part : (place + 1) * part] = total[:, :part]
            gv[:, place * part : (place + 1) * part] = total[:, part:]

    @pl.when(flags[0] == 0)
    def _():
        write(0)

    @pl.when(flags[0] == 1)
    def _():
        write(1)


def per_device(queries, key_states, value_states, attn_out, grad_out, log_sums, owners):
    n_blk, n_uly = lax.axis_size("blk"), lax.axis_size("ulysses")
    tok, width = queries.shape
    heads = log_sums.shape[1]
    kv_width = key_states.shape[1]
    half = width // 2
    rank, z = lax.axis_index("blk"), lax.axis_index("ulysses")
    before = (rank - 1) % n_blk
    side = z // (n_uly // 2)
    mine_q = owners[2 * rank + side]
    near = mine_q > owners[2 * before + side]
    far = mine_q > owners[2 * before + 1 - side]
    flags = jnp.stack([z % 2, near.astype(jnp.int32), far.astype(jnp.int32)]).astype(jnp.int32)

    def move(value, step, flip):
        pairs = []
        for b in range(n_blk):
            for u in range(n_uly):
                target = ((b + step) % n_blk) * n_uly + (u ^ flip)
                pairs.append((b * n_uly + u, target))
        return lax.ppermute(value, ("blk", "ulysses"), pairs)

    def shape(*dims, dtype=BF16):
        return jax.ShapeDtypeStruct(dims, dtype)

    q_send, do_send, kv_same, kv_other = pl.pallas_call(
        pack_kernel,
        out_shape=[shape(tok, half), shape(tok, half), shape(tok, kv_width), shape(tok, kv_width)],
        in_specs=[SMEM] + [VMEM] * 4,
        out_specs=[VMEM] * 4,
        name="pack",
    )(flags, queries, grad_out, key_states, value_states)
    q_in, do_in = move(q_send, 0, 1), move(do_send, 0, 1)
    kv = [move(kv_same if d % 2 == 0 else kv_other, 1, d) for d in range(n_uly)]
    stat_own, stat_send = pl.pallas_call(
        stats_kernel,
        out_shape=[shape(heads, tok, dtype=F32)] * 2,
        in_specs=[SMEM] + [VMEM] * 3,
        out_specs=[VMEM] * 2,
        name="stats",
    )(flags, grad_out, attn_out, log_sums)
    stat_in = move(stat_send, 0, 1)
    outs = pl.pallas_call(
        functools.partial(grads_kernel, n_uly),
        out_shape=[shape(tok, half)] * 2 + [shape(tok, kv_width)] * n_uly,
        in_specs=[SMEM] + [VMEM] * (6 + n_uly),
        out_specs=[VMEM] * (2 + n_uly),
        scratch_shapes=[pltpu.VMEM((half, 2 * tok), F32)],
        compiler_params=pltpu.CompilerParams(vmem_limit_bytes=40 * 1024 * 1024),
        name="grads",
    )(flags, queries, grad_out, q_in, do_in, stat_own, stat_in, *kv)
    dq_own, dq_send, dkv = outs[0], outs[1], outs[2:]
    back = [move(dkv[d], -1, d) for d in range(n_uly)]
    dq_back = move(dq_send, 0, 1)
    return tuple(
        pl.pallas_call(
            functools.partial(join_kernel, n_uly),
            out_shape=[shape(tok, width), shape(tok, kv_width), shape(tok, kv_width)],
            in_specs=[SMEM] + [VMEM] * (2 + n_uly),
            out_specs=[VMEM] * 3,
            name="join",
        )(flags, dq_own, dq_back, *back)
    )


def solution(mesh):
    rows = P(("blk", "ulysses"), None)
    return jax.shard_map(
        per_device,
        mesh=mesh,
        in_specs=(rows, rows, rows, rows, rows, rows, P()),
        out_specs=(rows, rows, rows),
        check_vma=False,
    )
```

```python
import functools
import math

import jax
import jax.numpy as jnp
from jax import lax
from jax.experimental import pallas as pl
from jax.experimental.pallas import tpu as pltpu
from jax.sharding import PartitionSpec as P

HEAD_DIM = 64
LOG2E = math.log2(math.e)
BF16 = jnp.bfloat16
F32 = jnp.float32
VMEM = pl.BlockSpec(memory_space=pltpu.VMEM)
SMEM = pl.BlockSpec(memory_space=pltpu.SMEM)


def dot(a, b, a_dim, b_dim):
    return lax.dot_general(
        a, b, (((a_dim,), (b_dim,)), ((), ())), preferred_element_type=F32
    )


def parity():
    return lax.rem(lax.axis_index("ulysses"), 2)


def by_parity(write):
    for mine in range(2):

        @pl.when(parity() == mine)
        def _():
            write(mine, 1 - mine)


def pack_kernel(q, do, o, k, v, sums, qd_send, kv_same, kv_other, stat_own):
    tokens, width = do.shape
    heads = sums.shape[0]
    half = width // 2
    part = k.shape[1] // 2
    n = heads // 2
    prod = do[...].astype(F32) * o[...].astype(F32)
    high = prod.astype(BF16)
    low = (prod - high.astype(F32)).astype(BF16)
    row = lax.broadcasted_iota(jnp.int32, (heads, width), 0)
    col = lax.broadcasted_iota(jnp.int32, (heads, width), 1)
    pick = jnp.where(col // HEAD_DIM == row, 1.0, 0.0).astype(BF16)
    delta = dot(pick, high, 1, 1) + dot(pick, low, 1, 1)
    lse = sums[...] * LOG2E

    def write(mine, other):
        qd_send[:, :half] = q[:, other * half : (other + 1) * half]
        qd_send[:, half:width] = do[:, other * half : (other + 1) * half]
        kv_same[:, :part] = k[:, mine * part : (mine + 1) * part]
        kv_same[:, part:] = v[:, mine * part : (mine + 1) * part]
        kv_other[:, :part] = k[:, other * part : (other + 1) * part]
        kv_other[:, part:] = v[:, other * part : (other + 1) * part]
        stat_own[:n, :] = lse[mine * n : (mine + 1) * n, :]
        stat_own[n:, :] = delta[mine * n : (mine + 1) * n, :]
        left = jnp.concatenate([x[other * n : (other + 1) * n, :] for x in (lse, delta)], 0)
        terms = []
        for _ in range(3):
            term = left.astype(BF16).astype(F32)
            left = left - term
            terms.append(term)
        terms.append(jnp.zeros((128 - 6 * n, tokens), F32))
        qd_send[:, width:] = jnp.transpose(jnp.concatenate(terms, 0)).astype(BF16)

    by_parity(write)


def grads_kernel(shards, owners, q, do, qd_in, st, *rest):
    kv = rest[:shards]
    dq_own, dq_send = rest[shards : shards + 2]
    dkv = rest[shards + 2 : 2 * shards + 2]
    dq_acc = rest[2 * shards + 2]
    tok = q.shape[0]
    heads = st.shape[0] // 2
    kv_heads = kv[0].shape[1] // 2 // HEAD_DIM
    group = heads // kv_heads
    side = shards // 2
    keys = side * tok
    part = kv_heads * HEAD_DIM
    factor = 1.0 / math.sqrt(HEAD_DIM)
    mine = parity()
    width = 2 * HEAD_DIM
    half = heads * HEAD_DIM
    terms = jnp.transpose(qd_in[:, 2 * half :].astype(F32))
    n = 2 * heads
    st_two = jnp.concatenate([st[...], terms[:n] + terms[n : 2 * n] + terms[2 * n : 3 * n]], 1)
    rank, z = lax.axis_index("blk"), lax.axis_index("ulysses")
    n_blk = lax.axis_size("blk")
    before = lax.rem(rank + n_blk - 1, n_blk)
    place = lax.div(z, side)
    mine_q = owners[2 * rank + place]
    near_seen = mine_q > owners[2 * before + place]
    far_seen = mine_q > owners[2 * before + 1 - place]
    dq_acc[...] = jnp.zeros_like(dq_acc)

    def spread(block, odd):
        one = block[:, HEAD_DIM:] if odd else block[:, :HEAD_DIM]
        zero = jnp.zeros_like(one)
        return jnp.concatenate(
            [jnp.concatenate([one, zero], 1), jnp.concatenate([zero, one], 1)], 0
        )

    def fold(wide, odd):
        top, low = wide[:keys], wide[keys:]
        if odd:
            return pltpu.roll(top, HEAD_DIM, 1) + low
        return top + pltpu.roll(low, HEAD_DIM, 1)

    def one_side(near):
        members = range(side) if near else range(side, shards)
        base = pl.multiple_of(mine * half, half)
        for pair in range(kv_heads // 2):
            k_cols = slice(pair * width, (pair + 1) * width)
            v_cols = slice(part + pair * width, part + (pair + 1) * width)
            k_two = jnp.concatenate([kv[m][:, k_cols] for m in members], 0)
            v_two = jnp.concatenate([kv[m][:, v_cols] for m in members], 0)
            folded_k, folded_v = [], []
            for odd in range(2):
                kv_head = 2 * pair + odd
                k_wide, v_wide = spread(k_two, odd), spread(v_two, odd)
                k_turned = jnp.transpose(k_wide)
                dk, dv = None, None
                for t in range(group // 2):
                    head = kv_head * group + 2 * t
                    at = head * HEAD_DIM
                    cols = pl.ds(pl.multiple_of(base + at, width), width)
                    q_two = jnp.concatenate([q[:, cols], qd_in[:, at : at + width]], 0)
                    do_two = jnp.concatenate([do[:, cols], qd_in[:, half + at : half + at + width]], 0)
                    scores = dot(k_wide, q_two, 1, 1)
                    dprobs = dot(v_wide, do_two, 1, 1)

                    lse = [st_two[head + i : head + i + 1] for i in range(2)]
                    delta = [st_two[heads + head + i : heads + head + i + 1] for i in range(2)]
                    probs_b, dscores = [], []
                    for i in range(2):
                        s = scores[i * keys : (i + 1) * keys]
                        d = dprobs[i * keys : (i + 1) * keys]
                        p = jnp.exp2(s * (factor * LOG2E) - lse[i])
                        probs_b.append(p.astype(BF16))
                        dscores.append((p * (d - delta[i])).astype(BF16))
                    probs_b = jnp.concatenate(probs_b, 0)
                    dscores = jnp.concatenate(dscores, 0)
                    dv_t = dot(probs_b, do_two, 1, 0)
                    dk_t = dot(dscores, q_two, 1, 0)
                    dv = dv_t if dv is None else dv + dv_t
                    dk = dk_t if dk is None else dk + dk_t
                    turned = dot(k_turned, dscores, 1, 0)
                    dq_acc[at : at + width, :] += turned
                folded_k.append(fold(dk, odd))
                folded_v.append(fold(dv, odd))
            lane = lax.broadcasted_iota(jnp.int32, (keys, width), 1)
            dk = (jnp.where(lane < HEAD_DIM, folded_k[0], folded_k[1]) * factor).astype(BF16)
            dv = jnp.where(lane < HEAD_DIM, folded_v[0], folded_v[1]).astype(BF16)
            for i, m in enumerate(members):
                dkv[m][:, k_cols] = dk[i * tok : (i + 1) * tok]
                dkv[m][:, v_cols] = dv[i * tok : (i + 1) * tok]

    def one_side_or_zero(near):
        seen = near_seen if near else far_seen

        @pl.when(seen)
        def _():
            one_side(near)

        @pl.when(jnp.logical_not(seen))
        def _():
            for m in range(side) if near else range(side, shards):
                dkv[m][...] = jnp.zeros_like(dkv[m])

    one_side_or_zero(True)
    one_side_or_zero(False)
    for at in range(0, heads * HEAD_DIM, width):
        out = jnp.transpose(dq_acc[at : at + width, :]) * factor
        out = out.astype(BF16)
        dq_own[:, at : at + width] = out[:tok]
        dq_send[:, at : at + width] = out[tok:]


def join_kernel(shards, dq_own, dq_back, *rest):
    back = rest[:shards]
    gq, gk, gv = rest[shards:]
    half = dq_own.shape[1]
    part = gk.shape[1] // 2

    def write(mine, other):
        gq[:, mine * half : (mine + 1) * half] = dq_own[...]
        gq[:, other * half : (other + 1) * half] = dq_back[...]
        for parity in range(2):
            total = back[parity][...].astype(F32)
            for m in range(parity + 2, shards, 2):
                total = total + back[m][...].astype(F32)
            total = total.astype(BF16)
            place = mine if parity == 0 else other
            gk[:, place * part : (place + 1) * part] = total[:, :part]
            gv[:, place * part : (place + 1) * part] = total[:, part:]

    by_parity(write)


def limit(mib):
    return pltpu.CompilerParams(vmem_limit_bytes=mib * 1024 * 1024)


def per_device(queries, key_states, value_states, attn_out, grad_out, log_sums, owners):
    n_blk, n_uly = lax.axis_size("blk"), lax.axis_size("ulysses")
    tok, width = queries.shape
    heads = log_sums.shape[1]
    kv_width = key_states.shape[1]
    half = width // 2
    def move(value, step, flip):
        pairs = []
        for b in range(n_blk):
            for u in range(n_uly):
                target = ((b + step) % n_blk) * n_uly + (u ^ flip)
                pairs.append((b * n_uly + u, target))
        return lax.ppermute(value, ("blk", "ulysses"), pairs)

    def shape(*dims, dtype=BF16):
        return jax.ShapeDtypeStruct(dims, dtype)

    qd_send, kv_same, kv_other, stat_own = pl.pallas_call(
        pack_kernel,
        out_shape=[
            shape(tok, width + 128),
            shape(tok, kv_width),
            shape(tok, kv_width),
            shape(heads, tok, dtype=F32),
        ],
        in_specs=[VMEM] * 6,
        out_specs=[VMEM] * 4,
        compiler_params=limit(16),
        name="pack",
    )(queries, grad_out, attn_out, key_states, value_states, jnp.transpose(log_sums))
    qd_in = move(qd_send, 0, 1)
    kv = [move(kv_same if d % 2 == 0 else kv_other, 1, d) for d in range(n_uly)]
    outs = pl.pallas_call(
        functools.partial(grads_kernel, n_uly),
        out_shape=[shape(tok, half)] * 2 + [shape(tok, kv_width)] * n_uly,
        in_specs=[SMEM] + [VMEM] * (4 + n_uly),
        out_specs=[VMEM] * (2 + n_uly),
        scratch_shapes=[pltpu.VMEM((half, 2 * tok), F32)],
        compiler_params=limit(32),
        name="grads",
    )(owners, queries, grad_out, qd_in, stat_own, *kv)
    dq_own, dq_send, dkv = outs[0], outs[1], outs[2:]
    back = [move(dkv[d], -1, d) for d in range(n_uly)]
    dq_back = move(dq_send, 0, 1)
    return tuple(
        pl.pallas_call(
            functools.partial(join_kernel, n_uly),
            out_shape=[shape(tok, width), shape(tok, kv_width), shape(tok, kv_width)],
            in_specs=[VMEM] * (2 + n_uly),
            out_specs=[VMEM] * 3,
            compiler_params=limit(8),
            name="join",
        )(dq_own, dq_back, *back)
    )


def solution(mesh):
    rows = P(("blk", "ulysses"), None)
    return jax.shard_map(
        per_device,
        mesh=mesh,
        in_specs=(rows, rows, rows, rows, rows, rows, P()),
        out_specs=(rows, rows, rows),
        check_vma=False,
    )
```

```python
import functools
import math

import jax
import jax.numpy as jnp
from jax import lax
from jax.experimental import pallas as pl
from jax.experimental.pallas import tpu as pltpu
from jax.sharding import PartitionSpec as P

HEAD_DIM = 64
LANES = 128
PACK_MIB = 60
LOG2E = math.log2(math.e)
BF16 = jnp.bfloat16
F32 = jnp.float32
VMEM = pl.BlockSpec(memory_space=pltpu.VMEM)
SMEM = pl.BlockSpec(memory_space=pltpu.SMEM)
HBM = pl.BlockSpec(memory_space=pltpu.HBM)


def dot(a, b, a_dim, b_dim):
    return lax.dot_general(
        a, b, (((a_dim,), (b_dim,)), ((), ())), preferred_element_type=F32
    )


def parity():
    return lax.rem(lax.axis_index("ulysses"), 2)


def by_parity(write):
    for mine in range(2):

        @pl.when(parity() == mine)
        def _():
            write(mine, 1 - mine)


def columns(which, size):
    return pl.ds(pl.multiple_of(which * size, size), size)


def pack_kv_kernel(k, v, kv_same, kv_other, sems):
    part = k.shape[1] // 2
    mine = parity()
    copies = []
    for i, source in enumerate((k, v)):
        for j, (target, which) in enumerate(((kv_same, mine), (kv_other, 1 - mine))):
            copies.append(
                pltpu.make_async_copy(
                    source.at[:, columns(which, part)],
                    target.at[:, i * part : (i + 1) * part],
                    sems.at[2 * i + j],
                )
            )
    for copy in copies:
        copy.start()
    for copy in copies:
        copy.wait()


def pack_q_kernel(q, do, o, sums, qd_send, stat_own, do_all, o_all, sums_all, stat_send, sems):
    tokens, width = do.shape
    heads = sums.shape[0]
    half = width // 2
    n = heads // 2
    other = 1 - parity()
    pairs = [
        (do, do_all),
        (o, o_all),
        (sums, sums_all),
        (q.at[:, columns(other, half)], qd_send.at[:, :half]),
        (do.at[:, columns(other, half)], qd_send.at[:, half:width]),
    ]
    copies = [pltpu.make_async_copy(a, b, sems.at[i]) for i, (a, b) in enumerate(pairs)]
    last = pltpu.make_async_copy(stat_send, qd_send.at[:, width:], sems.at[5])
    for copy in copies:
        copy.start()
    row = lax.broadcasted_iota(jnp.int32, (heads, width), 0)
    col = lax.broadcasted_iota(jnp.int32, (heads, width), 1)
    pick = jnp.where(col // HEAD_DIM == row, 1.0, 0.0).astype(BF16)
    for copy in copies[:3]:
        copy.wait()
    prod = do_all[...].astype(F32) * o_all[...].astype(F32)
    high = prod.astype(BF16)
    low = (prod - high.astype(F32)).astype(BF16)
    delta = dot(pick, high, 1, 1) + dot(pick, low, 1, 1)
    lse = sums_all[...] * LOG2E

    def write(mine, other):
        stat_own[:n, :] = lse[mine * n : (mine + 1) * n, :]
        stat_own[n:, :] = delta[mine * n : (mine + 1) * n, :]
        left = jnp.concatenate([x[other * n : (other + 1) * n, :] for x in (lse, delta)], 0)
        terms = []
        for _ in range(3):
            term = left.astype(BF16).astype(F32)
            left = left - term
            terms.append(term)
        terms.append(jnp.zeros((LANES - 6 * n, tokens), F32))
        stat_send[...] = jnp.transpose(jnp.concatenate(terms, 0)).astype(BF16)

    by_parity(write)
    last.start()
    for copy in [*copies[3:], last]:
        copy.wait()


def stack_heads(load, first, group):
    blocks = []
    for pair in range(group // 2):
        two = load((first + 2 * pair) * HEAD_DIM, 2 * HEAD_DIM)
        blocks += [two[:, :HEAD_DIM], two[:, HEAD_DIM:]]
    return jnp.concatenate(blocks, 0)


def stack_stats(stats, first, group):
    return jnp.concatenate([stats[first + g : first + g + 1] for g in range(group)], 1)


def head_grads(q, do, lse, delta, k, v):
    scores = dot(k, q, 1, 1)
    dprobs = dot(v, do, 1, 1)
    probs = jnp.exp2(scores * (LOG2E / math.sqrt(HEAD_DIM)) - lse)
    dscores = (probs * (dprobs - delta)).astype(BF16)
    dv = dot(probs.astype(BF16), do, 1, 0)
    dk = dot(dscores, q, 1, 0)
    dq = dot(k, dscores, 0, 0)
    return dk, dv, dq


def side_grads(load_q, load_do, stats, kv, put):
    heads = stats.shape[0] // 2
    part = kv[0].shape[1] // 2
    kv_heads = part // HEAD_DIM
    group = heads // kv_heads
    width = 2 * HEAD_DIM
    for pair in range(kv_heads // 2):
        at = pair * width
        k_two = jnp.concatenate([ref[:, at : at + width] for ref in kv], 0)
        v_two = jnp.concatenate([ref[:, part + at : part + at + width] for ref in kv], 0)
        dks, dvs = [], []
        for odd in range(2):
            first = (2 * pair + odd) * group
            lanes = slice(odd * HEAD_DIM, (odd + 1) * HEAD_DIM)
            dk, dv, dq = head_grads(
                stack_heads(load_q, first, group),
                stack_heads(load_do, first, group),
                stack_stats(stats, first, group),
                stack_stats(stats, heads + first, group),
                k_two[:, lanes],
                v_two[:, lanes],
            )
            dks.append(dk)
            dvs.append(dv)
            put_dq = dq
            put(first, put_dq)
        put.store(at, part, jnp.concatenate(dks, 1), jnp.concatenate(dvs, 1))


class Put:
    def __init__(self, dq_acc, group, store):
        self.dq_acc, self.group, self.store = dq_acc, group, store

    def __call__(self, first, dq):
        tok = self.dq_acc.shape[1]
        for g in range(self.group):
            rows = slice((first + g) * HEAD_DIM, (first + g + 1) * HEAD_DIM)
            self.dq_acc[rows, :] += dq[:, g * tok : (g + 1) * tok]


def write_dq(dq_acc, dq_out):
    factor = 1.0 / math.sqrt(HEAD_DIM)
    for at in range(0, dq_acc.shape[0], LANES):
        dq_out[:, at : at + LANES] = (jnp.transpose(dq_acc[at : at + LANES, :]) * factor).astype(BF16)


def seen_sides(owners, shards):
    rank, z = lax.axis_index("blk"), lax.axis_index("ulysses")
    n_blk = lax.axis_size("blk")
    before = lax.rem(rank + n_blk - 1, n_blk)
    place = lax.div(z, shards // 2)
    mine = owners[2 * rank + place]
    return mine > owners[2 * before + place], mine > owners[2 * before + 1 - place]


def own_kernel(shards, owners, q, do, stats, *rest):
    kv = rest[:shards]
    dq_own = rest[shards]
    accs = rest[shards + 1 : shards + 3]
    dq_acc = rest[shards + 3]
    heads = stats.shape[0] // 2
    half = heads * HEAD_DIM
    group = 2 * heads * HEAD_DIM // kv[0].shape[1]
    mine = parity()
    side = shards // 2
    dq_acc[...] = jnp.zeros_like(dq_acc)

    def from_half(ref):
        def load(at, size):
            return ref[:, pl.ds(pl.multiple_of(mine * half + at, size), size)]

        return load

    def one(which):
        acc = accs[which]

        def store(at, part, dk, dv):
            acc[:, at : at + dk.shape[1]] = dk
            acc[:, part + at : part + at + dv.shape[1]] = dv

        side_grads(
            from_half(q),
            from_half(do),
            stats[...],
            kv[which * side : (which + 1) * side],
            Put(dq_acc, group, store),
        )

    for which, seen in enumerate(seen_sides(owners, shards)):
        pl.when(seen)(functools.partial(one, which))
    write_dq(dq_acc, dq_own)


def partner_kernel(shards, which, owners, qd_in, acc, *rest):
    side = shards // 2
    kv = rest[:side]
    rest = rest[side:]
    dq_before = None
    if which == 0:
        dq_before, rest = rest[0], rest[1:]
    dkv = rest[:side]
    dq_out = rest[side]
    dq_acc = dq_out if which == 1 else rest[side + 1]
    tok = qd_in.shape[0]
    half = (qd_in.shape[1] - LANES) // 2
    n = 2 * half // HEAD_DIM
    group = 2 * half // kv[0].shape[1]
    seen = seen_sides(owners, shards)[which]
    dq_acc[...] = jnp.zeros_like(dq_acc) if dq_before is None else dq_before[...]
    factor = 1.0 / math.sqrt(HEAD_DIM)

    @pl.when(seen)
    def _():
        terms = jnp.transpose(qd_in[:, 2 * half :].astype(F32))
        stats = terms[:n] + terms[n : 2 * n] + terms[2 * n : 3 * n]

        def store(at, part, dk, dv):
            k_at = slice(at, at + dk.shape[1])
            v_at = slice(part + at, part + at + dv.shape[1])
            dk = ((dk + acc[:, k_at]) * factor).astype(BF16)
            dv = (dv + acc[:, v_at]).astype(BF16)
            for m in range(side):
                dkv[m][:, k_at] = dk[m * tok : (m + 1) * tok]
                dkv[m][:, v_at] = dv[m * tok : (m + 1) * tok]

        side_grads(
            lambda at, size: qd_in[:, at : at + size],
            lambda at, size: qd_in[:, half + at : half + at + size],
            stats,
            kv,
            Put(dq_acc, group, store),
        )

    @pl.when(jnp.logical_not(seen))
    def _():
        for m in range(side):
            dkv[m][...] = jnp.zeros_like(dkv[m])

    if which == 0:
        write_dq(dq_acc, dq_out)


def join_far_kernel(shards, *refs):
    back, out = refs[: shards // 2], refs[shards // 2 :]
    for odd in range(2):
        total = back[odd][...].astype(F32)
        for m in range(odd + 2, shards // 2, 2):
            total = total + back[m][...].astype(F32)
        out[odd][...] = total


def join_kernel(shards, dq_own, dq_back, *rest):
    back, far = rest[: shards // 2], rest[shards // 2 : shards // 2 + 2]
    gq, gk, gv = rest[shards // 2 + 2 :]
    half = dq_own.shape[1]
    part = gk.shape[1] // 2

    def write(mine, other):
        gq[:, mine * half : (mine + 1) * half] = dq_own[...]
        gq[:, other * half : (other + 1) * half] = dq_back[...]
        for odd in range(2):
            total = far[odd][...]
            for m in range(odd, shards // 2, 2):
                total = total + back[m][...].astype(F32)
            total = total.astype(BF16)
            place = mine if odd == 0 else other
            gk[:, place * part : (place + 1) * part] = total[:, :part]
            gv[:, place * part : (place + 1) * part] = total[:, part:]

    by_parity(write)


def limit(mib):
    return pltpu.CompilerParams(vmem_limit_bytes=mib * 1024 * 1024)


def per_device(queries, key_states, value_states, attn_out, grad_out, log_sums, owners):
    n_blk, n_uly = lax.axis_size("blk"), lax.axis_size("ulysses")
    tok, width = queries.shape
    heads = log_sums.shape[1]
    kv_width = key_states.shape[1]
    half = width // 2
    side = n_uly // 2

    def move(value, step, flip):
        pairs = []
        for b in range(n_blk):
            for u in range(n_uly):
                target = ((b + step) % n_blk) * n_uly + (u ^ flip)
                pairs.append((b * n_uly + u, target))
        return lax.ppermute(value, ("blk", "ulysses"), pairs)

    def shape(*dims, dtype=BF16):
        return jax.ShapeDtypeStruct(dims, dtype)

    cover = pl.CostEstimate(flops=1 << 38, bytes_accessed=1 << 20, transcendentals=0)

    kv_same, kv_other = pl.pallas_call(
        pack_kv_kernel,
        out_shape=[shape(tok, kv_width)] * 2,
        in_specs=[HBM] * 2,
        out_specs=[HBM] * 2,
        scratch_shapes=[pltpu.SemaphoreType.DMA((4,))],
        compiler_params=limit(PACK_MIB),
        name="pack_kv",
    )(key_states, value_states)
    kv = [move(kv_same if d % 2 == 0 else kv_other, 1, d) for d in range(n_uly)]
    qd_send, stat_own = pl.pallas_call(
        pack_q_kernel,
        out_shape=[shape(tok, width + LANES), shape(heads, tok, dtype=F32)],
        in_specs=[HBM] * 4,
        out_specs=[HBM, VMEM],
        scratch_shapes=[
            pltpu.VMEM((tok, width), BF16),
            pltpu.VMEM((tok, width), BF16),
            pltpu.VMEM((heads, tok), F32),
            pltpu.VMEM((tok, LANES), BF16),
            pltpu.SemaphoreType.DMA((6,)),
        ],
        compiler_params=limit(PACK_MIB),
        name="pack_q",
    )(queries, grad_out, attn_out, jnp.transpose(log_sums))
    qd_in = move(qd_send, 0, 1)
    dq_own, acc_near, acc_far = pl.pallas_call(
        functools.partial(own_kernel, n_uly),
        out_shape=[shape(tok, half)] + [shape(side * tok, kv_width, dtype=F32)] * 2,
        in_specs=[SMEM] + [VMEM] * (3 + n_uly),
        out_specs=[VMEM] * 3,
        scratch_shapes=[pltpu.VMEM((half, tok), F32)],
        compiler_params=limit(32),
        cost_estimate=cover,
        name="own",
    )(owners, queries, grad_out, stat_own, *kv)
    *dkv_far, dq_far = pl.pallas_call(
        functools.partial(partner_kernel, n_uly, 1),
        out_shape=[shape(tok, kv_width)] * side + [shape(half, tok, dtype=F32)],
        in_specs=[SMEM] + [VMEM] * (2 + side),
        out_specs=[VMEM] * (side + 1),
        compiler_params=limit(32),
        name="far",
    )(owners, qd_in, acc_far, *kv[side:])
    back_far = [move(x, -1, side + d) for d, x in enumerate(dkv_far)]
    *dkv_near, dq_send = pl.pallas_call(
        functools.partial(partner_kernel, n_uly, 0),
        out_shape=[shape(tok, kv_width)] * side + [shape(tok, half)],
        in_specs=[SMEM] + [VMEM] * (3 + side),
        out_specs=[VMEM] * (side + 1),
        scratch_shapes=[pltpu.VMEM((half, tok), F32)],
        compiler_params=limit(32),
        name="near",
    )(owners, qd_in, acc_near, *kv[:side], dq_far)
    back_near = [move(x, -1, d) for d, x in enumerate(dkv_near)]
    dq_back = move(dq_send, 0, 1)
    far = pl.pallas_call(
        functools.partial(join_far_kernel, n_uly),
        out_shape=[shape(tok, kv_width, dtype=F32)] * 2,
        in_specs=[VMEM] * side,
        out_specs=[VMEM] * 2,
        compiler_params=limit(8),
        cost_estimate=cover,
        name="join_far",
    )(*back_far)
    return tuple(
        pl.pallas_call(
            functools.partial(join_kernel, n_uly),
            out_shape=[shape(tok, width), shape(tok, kv_width), shape(tok, kv_width)],
            in_specs=[VMEM] * (4 + side),
            out_specs=[VMEM] * 3,
            compiler_params=limit(8),
            name="join",
        )(dq_own, dq_back, *back_near, *far)
    )


def solution(mesh):
    rows = P(("blk", "ulysses"), None)
    return jax.shard_map(
        per_device,
        mesh=mesh,
        in_specs=(rows, rows, rows, rows, rows, rows, P()),
        out_specs=(rows, rows, rows),
        check_vma=False,
    )
```

```python
import functools
import math

import jax
import jax.numpy as jnp
from jax import lax
from jax.experimental import pallas as pl
from jax.experimental.pallas import tpu as pltpu
from jax.sharding import PartitionSpec as P

HEAD_DIM = 64
LANES = 128
PACK_MIB = 60
LOG2E = math.log2(math.e)
BF16 = jnp.bfloat16
F32 = jnp.float32
VMEM = pl.BlockSpec(memory_space=pltpu.VMEM)
SMEM = pl.BlockSpec(memory_space=pltpu.SMEM)


def dot(a, b, a_dim, b_dim):
    return lax.dot_general(
        a, b, (((a_dim,), (b_dim,)), ((), ())), preferred_element_type=F32
    )


def parity():
    return lax.rem(lax.axis_index("ulysses"), 2)


def by_parity(write):
    for mine in range(2):

        @pl.when(parity() == mine)
        def _():
            write(mine, 1 - mine)


def pack_kv_kernel(k, v, kv_same, kv_other):
    part = k.shape[1] // 2

    def write(mine, other):
        for out, which in ((kv_same, mine), (kv_other, other)):
            out[:, :part] = k[:, which * part : (which + 1) * part]
            out[:, part:] = v[:, which * part : (which + 1) * part]

    by_parity(write)


def pack_q_kernel(q, do, o, sums, qd_send, stat_own):
    tokens, width = do.shape
    heads = sums.shape[0]
    half = width // 2
    n = heads // 2
    row = lax.broadcasted_iota(jnp.int32, (heads, width), 0)
    col = lax.broadcasted_iota(jnp.int32, (heads, width), 1)
    pick = jnp.where(col // HEAD_DIM == row, 1.0, 0.0).astype(BF16)
    prod = do[...].astype(F32) * o[...].astype(F32)
    high = prod.astype(BF16)
    low = (prod - high.astype(F32)).astype(BF16)
    delta = dot(pick, high, 1, 1) + dot(pick, low, 1, 1)
    lse = sums[...] * LOG2E

    def write(mine, other):
        qd_send[:, :half] = q[:, other * half : (other + 1) * half]
        qd_send[:, half:width] = do[:, other * half : (other + 1) * half]
        stat_own[:n, :] = lse[mine * n : (mine + 1) * n, :]
        stat_own[n:, :] = delta[mine * n : (mine + 1) * n, :]
        left = jnp.concatenate([x[other * n : (other + 1) * n, :] for x in (lse, delta)], 0)
        terms = []
        for _ in range(3):
            term = left.astype(BF16).astype(F32)
            left = left - term
            terms.append(term)
        terms.append(jnp.zeros((LANES - 6 * n, tokens), F32))
        qd_send[:, width:] = jnp.transpose(jnp.concatenate(terms, 0)).astype(BF16)

    by_parity(write)


def stack_heads(load, first, group):
    blocks = []
    for pair in range(group // 2):
        two = load((first + 2 * pair) * HEAD_DIM, 2 * HEAD_DIM)
        blocks += [two[:, :HEAD_DIM], two[:, HEAD_DIM:]]
    return jnp.concatenate(blocks, 0)


def stack_stats(stats, first, group):
    return jnp.concatenate([stats[first + g : first + g + 1] for g in range(group)], 1)


def head_grads(q, do, lse, delta, k, v):
    scores = dot(k, q, 1, 1)
    dprobs = dot(v, do, 1, 1)
    probs = jnp.exp2(scores * (LOG2E / math.sqrt(HEAD_DIM)) - lse)
    dscores = (probs * (dprobs - delta)).astype(BF16)
    dv = dot(probs.astype(BF16), do, 1, 0)
    dk = dot(dscores, q, 1, 0)
    dq = dot(k, dscores, 0, 0)
    return dk, dv, dq


def side_grads(load_q, load_do, stats, kv, put):
    heads = stats.shape[0] // 2
    part = kv[0].shape[1] // 2
    kv_heads = part // HEAD_DIM
    group = heads // kv_heads
    width = 2 * HEAD_DIM
    for pair in range(kv_heads // 2):
        at = pair * width
        k_two = jnp.concatenate([ref[:, at : at + width] for ref in kv], 0)
        v_two = jnp.concatenate([ref[:, part + at : part + at + width] for ref in kv], 0)
        dks, dvs = [], []
        for odd in range(2):
            first = (2 * pair + odd) * group
            lanes = slice(odd * HEAD_DIM, (odd + 1) * HEAD_DIM)
            dk, dv, dq = head_grads(
                stack_heads(load_q, first, group),
                stack_heads(load_do, first, group),
                stack_stats(stats, first, group),
                stack_stats(stats, heads + first, group),
                k_two[:, lanes],
                v_two[:, lanes],
            )
            dks.append(dk)
            dvs.append(dv)
            put_dq = dq
            put(first, put_dq)
        put.store(at, part, jnp.concatenate(dks, 1), jnp.concatenate(dvs, 1))


class Put:
    def __init__(self, dq_acc, group, store):
        self.dq_acc, self.group, self.store = dq_acc, group, store

    def __call__(self, first, dq):
        tok = self.dq_acc.shape[1]
        for g in range(self.group):
            rows = slice((first + g) * HEAD_DIM, (first + g + 1) * HEAD_DIM)
            self.dq_acc[rows, :] += dq[:, g * tok : (g + 1) * tok]


def write_dq(dq_acc, dq_out):
    factor = 1.0 / math.sqrt(HEAD_DIM)
    for at in range(0, dq_acc.shape[0], LANES):
        dq_out[:, at : at + LANES] = (jnp.transpose(dq_acc[at : at + LANES, :]) * factor).astype(BF16)


def seen_sides(owners, shards):
    rank, z = lax.axis_index("blk"), lax.axis_index("ulysses")
    n_blk = lax.axis_size("blk")
    before = lax.rem(rank + n_blk - 1, n_blk)
    place = lax.div(z, shards // 2)
    mine = owners[2 * rank + place]
    return mine > owners[2 * before + place], mine > owners[2 * before + 1 - place]


def own_kernel(shards, owners, q, do, stats, *rest):
    kv = rest[:shards]
    dq_own = rest[shards]
    accs = rest[shards + 1 : shards + 3]
    dq_acc = rest[shards + 3]
    heads = stats.shape[0] // 2
    half = heads * HEAD_DIM
    group = 2 * heads * HEAD_DIM // kv[0].shape[1]
    mine = parity()
    side = shards // 2
    dq_acc[...] = jnp.zeros_like(dq_acc)

    def from_half(ref):
        def load(at, size):
            return ref[:, pl.ds(pl.multiple_of(mine * half + at, size), size)]

        return load

    def one(which):
        acc = accs[which]

        def store(at, part, dk, dv):
            acc[:, at : at + dk.shape[1]] = dk
            acc[:, part + at : part + at + dv.shape[1]] = dv

        side_grads(
            from_half(q),
            from_half(do),
            stats[...],
            kv[which * side : (which + 1) * side],
            Put(dq_acc, group, store),
        )

    for which, seen in enumerate(seen_sides(owners, shards)):
        pl.when(seen)(functools.partial(one, which))
    write_dq(dq_acc, dq_own)


def partner_kernel(shards, which, owners, qd_in, acc, *rest):
    side = shards // 2
    kv = rest[:side]
    rest = rest[side:]
    dq_before = None
    if which == 0:
        dq_before, rest = rest[0], rest[1:]
    dkv = rest[:side]
    dq_out = rest[side]
    dq_acc = dq_out if which == 1 else rest[side + 1]
    tok = qd_in.shape[0]
    half = (qd_in.shape[1] - LANES) // 2
    n = 2 * half // HEAD_DIM
    group = 2 * half // kv[0].shape[1]
    seen = seen_sides(owners, shards)[which]
    dq_acc[...] = jnp.zeros_like(dq_acc) if dq_before is None else dq_before[...]
    factor = 1.0 / math.sqrt(HEAD_DIM)

    @pl.when(seen)
    def _():
        terms = jnp.transpose(qd_in[:, 2 * half :].astype(F32))
        stats = terms[:n] + terms[n : 2 * n] + terms[2 * n : 3 * n]

        def store(at, part, dk, dv):
            k_at = slice(at, at + dk.shape[1])
            v_at = slice(part + at, part + at + dv.shape[1])
            dk = ((dk + acc[:, k_at]) * factor).astype(BF16)
            dv = (dv + acc[:, v_at]).astype(BF16)
            for m in range(side):
                dkv[m][:, k_at] = dk[m * tok : (m + 1) * tok]
                dkv[m][:, v_at] = dv[m * tok : (m + 1) * tok]

        side_grads(
            lambda at, size: qd_in[:, at : at + size],
            lambda at, size: qd_in[:, half + at : half + at + size],
            stats,
            kv,
            Put(dq_acc, group, store),
        )

    @pl.when(jnp.logical_not(seen))
    def _():
        for m in range(side):
            dkv[m][...] = jnp.zeros_like(dkv[m])

    if which == 0:
        write_dq(dq_acc, dq_out)


def join_far_kernel(shards, *refs):
    back, out = refs[: shards // 2], refs[shards // 2 :]
    for odd in range(2):
        total = back[odd][...].astype(F32)
        for m in range(odd + 2, shards // 2, 2):
            total = total + back[m][...].astype(F32)
        out[odd][...] = total


def join_kernel(shards, dq_own, dq_back, *rest):
    back, far = rest[: shards // 2], rest[shards // 2 : shards // 2 + 2]
    gq, gk, gv = rest[shards // 2 + 2 :]
    half = dq_own.shape[1]
    part = gk.shape[1] // 2

    def write(mine, other):
        gq[:, mine * half : (mine + 1) * half] = dq_own[...]
        gq[:, other * half : (other + 1) * half] = dq_back[...]
        for odd in range(2):
            total = far[odd][...]
            for m in range(odd, shards // 2, 2):
                total = total + back[m][...].astype(F32)
            total = total.astype(BF16)
            place = mine if odd == 0 else other
            gk[:, place * part : (place + 1) * part] = total[:, :part]
            gv[:, place * part : (place + 1) * part] = total[:, part:]

    by_parity(write)


def limit(mib):
    return pltpu.CompilerParams(vmem_limit_bytes=mib * 1024 * 1024)


def per_device(queries, key_states, value_states, attn_out, grad_out, log_sums, owners):
    n_blk, n_uly = lax.axis_size("blk"), lax.axis_size("ulysses")
    tok, width = queries.shape
    heads = log_sums.shape[1]
    kv_width = key_states.shape[1]
    half = width // 2
    side = n_uly // 2

    def move(value, step, flip):
        pairs = []
        for b in range(n_blk):
            for u in range(n_uly):
                target = ((b + step) % n_blk) * n_uly + (u ^ flip)
                pairs.append((b * n_uly + u, target))
        return lax.ppermute(value, ("blk", "ulysses"), pairs)

    def shape(*dims, dtype=BF16):
        return jax.ShapeDtypeStruct(dims, dtype)

    cover = pl.CostEstimate(flops=1 << 34, bytes_accessed=1 << 20, transcendentals=0)

    kv_same, kv_other = pl.pallas_call(
        pack_kv_kernel,
        out_shape=[shape(tok, kv_width)] * 2,
        in_specs=[VMEM] * 2,
        out_specs=[VMEM] * 2,
        compiler_params=limit(PACK_MIB),
        name="pack_kv",
    )(key_states, value_states)
    kv = [move(kv_same if d % 2 == 0 else kv_other, 1, d) for d in range(n_uly)]
    qd_send, stat_own = pl.pallas_call(
        pack_q_kernel,
        out_shape=[shape(tok, width + LANES), shape(heads, tok, dtype=F32)],
        in_specs=[VMEM] * 4,
        out_specs=[VMEM] * 2,
        compiler_params=limit(PACK_MIB),
        name="pack_q",
    )(queries, grad_out, attn_out, jnp.transpose(log_sums))
    qd_in = move(qd_send, 0, 1)
    dq_own, acc_near, acc_far = pl.pallas_call(
        functools.partial(own_kernel, n_uly),
        out_shape=[shape(tok, half)] + [shape(side * tok, kv_width, dtype=F32)] * 2,
        in_specs=[SMEM] + [VMEM] * (3 + n_uly),
        out_specs=[VMEM] * 3,
        scratch_shapes=[pltpu.VMEM((half, tok), F32)],
        compiler_params=limit(32),
        cost_estimate=cover,
        name="own",
    )(owners, queries, grad_out, stat_own, *kv)
    *dkv_far, dq_far = pl.pallas_call(
        functools.partial(partner_kernel, n_uly, 1),
        out_shape=[shape(tok, kv_width)] * side + [shape(half, tok, dtype=F32)],
        in_specs=[SMEM] + [VMEM] * (2 + side),
        out_specs=[VMEM] * (side + 1),
        compiler_params=limit(32),
        name="far",
    )(owners, qd_in, acc_far, *kv[side:])
    back_far = [move(x, -1, side + d) for d, x in enumerate(dkv_far)]
    *dkv_near, dq_send = pl.pallas_call(
        functools.partial(partner_kernel, n_uly, 0),
        out_shape=[shape(tok, kv_width)] * side + [shape(tok, half)],
        in_specs=[SMEM] + [VMEM] * (3 + side),
        out_specs=[VMEM] * (side + 1),
        scratch_shapes=[pltpu.VMEM((half, tok), F32)],
        compiler_params=limit(32),
        name="near",
    )(owners, qd_in, acc_near, *kv[:side], dq_far)
    back_near = [move(x, -1, d) for d, x in enumerate(dkv_near)]
    dq_back = move(dq_send, 0, 1)
    far = pl.pallas_call(
        functools.partial(join_far_kernel, n_uly),
        out_shape=[shape(tok, kv_width, dtype=F32)] * 2,
        in_specs=[VMEM] * side,
        out_specs=[VMEM] * 2,
        compiler_params=limit(8),
        cost_estimate=cover,
        name="join_far",
    )(*back_far)
    return tuple(
        pl.pallas_call(
            functools.partial(join_kernel, n_uly),
            out_shape=[shape(tok, width), shape(tok, kv_width), shape(tok, kv_width)],
            in_specs=[VMEM] * (4 + side),
            out_specs=[VMEM] * 3,
            compiler_params=limit(8),
            name="join",
        )(dq_own, dq_back, *back_near, *far)
    )


def solution(mesh):
    rows = P(("blk", "ulysses"), None)
    return jax.shard_map(
        per_device,
        mesh=mesh,
        in_specs=(rows, rows, rows, rows, rows, rows, P()),
        out_specs=(rows, rows, rows),
        check_vma=False,
    )
```

```python
import functools
import math

import jax
import jax.numpy as jnp
from jax import lax
from jax.experimental import pallas as pl
from jax.experimental.pallas import tpu as pltpu
from jax.sharding import PartitionSpec as P

HEAD_DIM = 64
LANES = 128
PACK_MIB = 60
LONG, SHORT = 1 << 34, 1 << 31
LOG2E = math.log2(math.e)
BF16 = jnp.bfloat16
F32 = jnp.float32
ANY = pl.BlockSpec(memory_space=pl.ANY)
VMEM = pl.BlockSpec(memory_space=pltpu.VMEM)
SMEM = pl.BlockSpec(memory_space=pltpu.SMEM)


def dot(a, b, a_dim, b_dim):
    return lax.dot_general(
        a, b, (((a_dim,), (b_dim,)), ((), ())), preferred_element_type=F32
    )


def parity():
    return lax.rem(lax.axis_index("ulysses"), 2)


def by_parity(write):
    for mine in range(2):

        @pl.when(parity() == mine)
        def _():
            write(mine, 1 - mine)


def pack_kv_kernel(k, v, *outs):
    part = k.shape[1] // 2

    def write(mine, other):
        for out, which in zip(outs, (mine, other, mine, other)):
            out[:, :part] = k[:, which * part : (which + 1) * part]
            out[:, part:] = v[:, which * part : (which + 1) * part]

    by_parity(write)


def pack_q_kernel(q, do, o, sums, near_in, near_in2, qd_send, stat_own, near_out, near_out2):
    tokens, width = do.shape
    heads = sums.shape[0]
    half = width // 2
    n = heads // 2
    row = lax.broadcasted_iota(jnp.int32, (heads, width), 0)
    col = lax.broadcasted_iota(jnp.int32, (heads, width), 1)
    pick = jnp.where(col // HEAD_DIM == row, 1.0, 0.0).astype(BF16)
    prod = do[...].astype(F32) * o[...].astype(F32)
    high = prod.astype(BF16)
    low = (prod - high.astype(F32)).astype(BF16)
    delta = dot(pick, high, 1, 1) + dot(pick, low, 1, 1)
    lse = sums[...] * LOG2E

    def write(mine, other):
        qd_send[:, :half] = q[:, other * half : (other + 1) * half]
        qd_send[:, half:width] = do[:, other * half : (other + 1) * half]
        stat_own[:n, :] = lse[mine * n : (mine + 1) * n, :]
        stat_own[n:, :] = delta[mine * n : (mine + 1) * n, :]
        left = jnp.concatenate([x[other * n : (other + 1) * n, :] for x in (lse, delta)], 0)
        terms = []
        for _ in range(3):
            term = left.astype(BF16).astype(F32)
            left = left - term
            terms.append(term)
        terms.append(jnp.zeros((LANES - 6 * n, tokens), F32))
        qd_send[:, width:] = jnp.transpose(jnp.concatenate(terms, 0)).astype(BF16)

    by_parity(write)


def stack_heads(load, first, group):
    blocks = []
    for pair in range(group // 2):
        two = load((first + 2 * pair) * HEAD_DIM, 2 * HEAD_DIM)
        blocks += [two[:, :HEAD_DIM], two[:, HEAD_DIM:]]
    return jnp.concatenate(blocks, 0)


def stack_stats(stats, first, group):
    return jnp.concatenate([stats[first + g : first + g + 1] for g in range(group)], 1)


def head_grads(q, do, lse, delta, k, v):
    scores = dot(k, q, 1, 1)
    dprobs = dot(v, do, 1, 1)
    probs = jnp.exp2(scores * (LOG2E / math.sqrt(HEAD_DIM)) - lse)
    dscores = (probs * (dprobs - delta)).astype(BF16)
    dv = dot(probs.astype(BF16), do, 1, 0)
    dk = dot(dscores, q, 1, 0)
    dq = dot(k, dscores, 0, 0)
    return dk, dv, dq


def side_grads(load_q, load_do, stats, kv, put):
    heads = stats.shape[0] // 2
    part = kv[0].shape[1] // 2
    kv_heads = part // HEAD_DIM
    group = heads // kv_heads
    width = 2 * HEAD_DIM
    for pair in range(kv_heads // 2):
        at = pair * width
        k_two = jnp.concatenate([ref[:, at : at + width] for ref in kv], 0)
        v_two = jnp.concatenate([ref[:, part + at : part + at + width] for ref in kv], 0)
        dks, dvs = [], []
        for odd in range(2):
            first = (2 * pair + odd) * group
            lanes = slice(odd * HEAD_DIM, (odd + 1) * HEAD_DIM)
            dk, dv, dq = head_grads(
                stack_heads(load_q, first, group),
                stack_heads(load_do, first, group),
                stack_stats(stats, first, group),
                stack_stats(stats, heads + first, group),
                k_two[:, lanes],
                v_two[:, lanes],
            )
            dks.append(dk)
            dvs.append(dv)
            put_dq = dq
            put(first, put_dq)
        put.store(at, part, jnp.concatenate(dks, 1), jnp.concatenate(dvs, 1))


class Put:
    def __init__(self, dq_acc, group, store):
        self.dq_acc, self.group, self.store = dq_acc, group, store

    def __call__(self, first, dq):
        tok = self.dq_acc.shape[1]
        for g in range(self.group):
            rows = slice((first + g) * HEAD_DIM, (first + g + 1) * HEAD_DIM)
            self.dq_acc[rows, :] += dq[:, g * tok : (g + 1) * tok]


def write_dq(dq_acc, dq_out):
    factor = 1.0 / math.sqrt(HEAD_DIM)
    for at in range(0, dq_acc.shape[0], LANES):
        dq_out[:, at : at + LANES] = (jnp.transpose(dq_acc[at : at + LANES, :]) * factor).astype(BF16)


def seen_sides(owners, shards):
    rank, z = lax.axis_index("blk"), lax.axis_index("ulysses")
    n_blk = lax.axis_size("blk")
    before = lax.rem(rank + n_blk - 1, n_blk)
    place = lax.div(z, shards // 2)
    mine = owners[2 * rank + place]
    return mine > owners[2 * before + place], mine > owners[2 * before + 1 - place]


def own_kernel(shards, which, owners, q, do, stats, *rest):
    side = shards // 2
    kv, rest = rest[:side], rest[side:]
    if which == 1:
        acc, dq_acc = rest
    else:
        dq_before, acc, dq_own, dq_acc = rest
    heads = stats.shape[0] // 2
    half = heads * HEAD_DIM
    group = 2 * half // kv[0].shape[1]
    mine = parity()
    dq_acc[...] = jnp.zeros_like(dq_acc) if which == 1 else dq_before[...]

    def from_half(ref):
        def load(at, size):
            return ref[:, pl.ds(pl.multiple_of(mine * half + at, size), size)]

        return load

    def store(at, part, dk, dv):
        acc[:, at : at + dk.shape[1]] = dk
        acc[:, part + at : part + at + dv.shape[1]] = dv

    @pl.when(seen_sides(owners, shards)[which])
    def _():
        side_grads(from_half(q), from_half(do), stats[...], kv, Put(dq_acc, group, store))

    if which == 0:
        write_dq(dq_acc, dq_own)


def partner_kernel(shards, which, owners, qd_in, acc, *rest):
    side = shards // 2
    kv = rest[:side]
    rest = rest[side:]
    dq_before = None
    if which == 0:
        dq_before, rest = rest[0], rest[1:]
    else:
        rest = rest[1:]
    dkv = rest[:side]
    dq_out = rest[side]
    dq_acc = dq_out if which == 1 else rest[side + 1]
    tok = qd_in.shape[0]
    half = (qd_in.shape[1] - LANES) // 2
    n = 2 * half // HEAD_DIM
    group = 2 * half // kv[0].shape[1]
    seen = seen_sides(owners, shards)[which]
    dq_acc[...] = jnp.zeros_like(dq_acc) if dq_before is None else dq_before[...]
    factor = 1.0 / math.sqrt(HEAD_DIM)

    @pl.when(seen)
    def _():
        terms = jnp.transpose(qd_in[:, 2 * half :].astype(F32))
        stats = terms[:n] + terms[n : 2 * n] + terms[2 * n : 3 * n]

        def store(at, part, dk, dv):
            k_at = slice(at, at + dk.shape[1])
            v_at = slice(part + at, part + at + dv.shape[1])
            dk = ((dk + acc[:, k_at]) * factor).astype(BF16)
            dv = (dv + acc[:, v_at]).astype(BF16)
            for m in range(side):
                dkv[m][:, k_at] = dk[m * tok : (m + 1) * tok]
                dkv[m][:, v_at] = dv[m * tok : (m + 1) * tok]

        side_grads(
            lambda at, size: qd_in[:, at : at + size],
            lambda at, size: qd_in[:, half + at : half + at + size],
            stats,
            kv,
            Put(dq_acc, group, store),
        )

    @pl.when(jnp.logical_not(seen))
    def _():
        for m in range(side):
            dkv[m][...] = jnp.zeros_like(dkv[m])

    if which == 0:
        write_dq(dq_acc, dq_out)


def join_far_kernel(shards, *refs):
    back, out = refs[: shards // 2], refs[shards // 2 :]
    for odd in range(2):
        total = back[odd][...].astype(F32)
        for m in range(odd + 2, shards // 2, 2):
            total = total + back[m][...].astype(F32)
        out[odd][...] = total


def join_kernel(shards, dq_own, dq_back, *rest):
    back, far = rest[: shards // 2], rest[shards // 2 : shards // 2 + 2]
    gq, gk, gv = rest[shards // 2 + 2 :]
    half = dq_own.shape[1]
    part = gk.shape[1] // 2

    def write(mine, other):
        gq[:, mine * half : (mine + 1) * half] = dq_own[...]
        gq[:, other * half : (other + 1) * half] = dq_back[...]
        for odd in range(2):
            total = far[odd][...]
            for m in range(odd, shards // 2, 2):
                total = total + back[m][...].astype(F32)
            total = total.astype(BF16)
            place = mine if odd == 0 else other
            gk[:, place * part : (place + 1) * part] = total[:, :part]
            gv[:, place * part : (place + 1) * part] = total[:, part:]

    by_parity(write)


def limit(mib):
    return pltpu.CompilerParams(vmem_limit_bytes=mib * 1024 * 1024)


def per_device(queries, key_states, value_states, attn_out, grad_out, log_sums, owners):
    n_blk, n_uly = lax.axis_size("blk"), lax.axis_size("ulysses")
    tok, width = queries.shape
    heads = log_sums.shape[1]
    kv_width = key_states.shape[1]
    half = width // 2
    side = n_uly // 2

    def move(value, step, flip):
        pairs = []
        for b in range(n_blk):
            for u in range(n_uly):
                target = ((b + step) % n_blk) * n_uly + (u ^ flip)
                pairs.append((b * n_uly + u, target))
        return lax.ppermute(value, ("blk", "ulysses"), pairs)

    def shape(*dims, dtype=BF16):
        return jax.ShapeDtypeStruct(dims, dtype)

    def cover(flops):
        return pl.CostEstimate(flops=flops, bytes_accessed=1 << 20, transcendentals=0)

    far_same, far_other, near_same, near_other = pl.pallas_call(
        pack_kv_kernel,
        out_shape=[shape(tok, kv_width)] * 4,
        in_specs=[VMEM] * 2,
        out_specs=[VMEM] * 4,
        compiler_params=limit(PACK_MIB),
        name="pack_kv",
    )(key_states, value_states)
    kv_far = [move(far_other if d % 2 else far_same, 1, d) for d in range(side, n_uly)]
    qd_send, stat_own, near_same, near_other = pl.pallas_call(
        pack_q_kernel,
        out_shape=[
            shape(tok, width + LANES),
            shape(heads, tok, dtype=F32),
            shape(tok, kv_width),
            shape(tok, kv_width),
        ],
        in_specs=[VMEM] * 4 + [ANY] * 2,
        out_specs=[VMEM] * 2 + [ANY] * 2,
        input_output_aliases={4: 2, 5: 3},
        compiler_params=limit(PACK_MIB),
        name="pack_q",
    )(queries, grad_out, attn_out, jnp.transpose(log_sums), near_same, near_other)
    kv_near = [move(near_other if d % 2 else near_same, 1, d) for d in range(side)]
    qd_in = move(qd_send, 0, 1)
    acc_far, dq_part = pl.pallas_call(
        functools.partial(own_kernel, n_uly, 1),
        out_shape=[shape(side * tok, kv_width, dtype=F32), shape(half, tok, dtype=F32)],
        in_specs=[SMEM] + [VMEM] * (3 + side),
        out_specs=[VMEM] * 2,
        compiler_params=limit(32),
        cost_estimate=cover(LONG),
        name="own_far",
    )(owners, queries, grad_out, stat_own, *kv_far)
    acc_near, dq_own = pl.pallas_call(
        functools.partial(own_kernel, n_uly, 0),
        out_shape=[shape(side * tok, kv_width, dtype=F32), shape(tok, half)],
        in_specs=[SMEM] + [VMEM] * (4 + side),
        out_specs=[VMEM] * 2,
        scratch_shapes=[pltpu.VMEM((half, tok), F32)],
        compiler_params=limit(32),
        cost_estimate=cover(SHORT),
        name="own_near",
    )(owners, queries, grad_out, stat_own, *kv_near, dq_part)
    *dkv_far, dq_far = pl.pallas_call(
        functools.partial(partner_kernel, n_uly, 1),
        out_shape=[shape(tok, kv_width)] * side + [shape(half, tok, dtype=F32)],
        in_specs=[SMEM] + [VMEM] * (2 + side) + [ANY],
        out_specs=[VMEM] * (side + 1),
        compiler_params=limit(32),
        name="far",
    )(owners, qd_in, acc_far, *kv_far, dq_own)
    back_far = [move(x, -1, side + d) for d, x in enumerate(dkv_far)]
    *dkv_near, dq_send = pl.pallas_call(
        functools.partial(partner_kernel, n_uly, 0),
        out_shape=[shape(tok, kv_width)] * side + [shape(tok, half)],
        in_specs=[SMEM] + [VMEM] * (3 + side),
        out_specs=[VMEM] * (side + 1),
        scratch_shapes=[pltpu.VMEM((half, tok), F32)],
        compiler_params=limit(32),
        name="near",
    )(owners, qd_in, acc_near, *kv_near, dq_far)
    back_near = [move(x, -1, d) for d, x in enumerate(dkv_near)]
    dq_back = move(dq_send, 0, 1)
    far = pl.pallas_call(
        functools.partial(join_far_kernel, n_uly),
        out_shape=[shape(tok, kv_width, dtype=F32)] * 2,
        in_specs=[VMEM] * side,
        out_specs=[VMEM] * 2,
        compiler_params=limit(8),
        cost_estimate=cover(LONG),
        name="join_far",
    )(*back_far)
    return tuple(
        pl.pallas_call(
            functools.partial(join_kernel, n_uly),
            out_shape=[shape(tok, width), shape(tok, kv_width), shape(tok, kv_width)],
            in_specs=[VMEM] * (4 + side),
            out_specs=[VMEM] * 3,
            compiler_params=limit(8),
            name="join",
        )(dq_own, dq_back, *back_near, *far)
    )


def solution(mesh):
    rows = P(("blk", "ulysses"), None)
    return jax.shard_map(
        per_device,
        mesh=mesh,
        in_specs=(rows, rows, rows, rows, rows, rows, P()),
        out_specs=(rows, rows, rows),
        check_vma=False,
    )
```

```python
import functools
import math

import jax
import jax.numpy as jnp
from jax import lax
from jax.experimental import pallas as pl
from jax.experimental.pallas import tpu as pltpu
from jax.sharding import PartitionSpec as P

HEAD_DIM = 64
LANES = 128
PACK_MIB = 60
LONG, SHORT = 1 << 34, 1 << 31
LOG2E = math.log2(math.e)
BF16 = jnp.bfloat16
F32 = jnp.float32
VMEM = pl.BlockSpec(memory_space=pltpu.VMEM)
SMEM = pl.BlockSpec(memory_space=pltpu.SMEM)


def dot(a, b, a_dim, b_dim):
    return lax.dot_general(
        a, b, (((a_dim,), (b_dim,)), ((), ())), preferred_element_type=F32
    )


def parity():
    return lax.rem(lax.axis_index("ulysses"), 2)


def by_parity(write):
    for mine in range(2):

        @pl.when(parity() == mine)
        def _():
            write(mine, 1 - mine)


def by_class(write):
    side = lax.div(lax.axis_index("ulysses"), lax.axis_size("ulysses") // 2)
    odd = lax.rem(lax.axis_index("blk") + side, 2)
    for which in range(2):

        @pl.when(odd == which)
        def _():
            write(which)


def in_turn(which, first, second):
    return [*first, *second] if which == 0 else [*second, *first]


def apart(which, refs, n_first):
    n_second = len(refs) - n_first
    if which == 0:
        return refs[:n_first], refs[n_first:]
    return refs[n_second:], refs[:n_second]


def pack_kernel(shards, owners, q, do, o, sums, k, v, *outs):
    side = shards // 2
    near_same, near_other, rest, stat_own, flags = outs[-5:]
    slots = outs[:-5]
    tokens, width = do.shape
    heads = sums.shape[0]
    half = width // 2
    part = k.shape[1] // 2
    n = heads // 2
    mine = parity()
    other = 1 - mine

    def cut(ref, which, size, at=0, wide=None):
        wide = size if wide is None else wide
        return ref[:, pl.ds(pl.multiple_of(which * size + at, wide), wide)]

    def put_keys(out, which):
        out[:, :part] = cut(k, which, part)
        out[:, part:] = cut(v, which, part)

    def put_rows(out, unit, at=0):
        out[:, at : at + part] = cut(q, other, half, unit * part, part)
        out[:, at + part : at + 2 * part] = cut(do, other, half, unit * part, part)

    n_mixed = len(slots) - side
    units = half // part

    def write(which):
        keys, rows = apart(which, slots, side)
        for d in range(side):
            put_keys(keys[d], mine if d % 2 == 0 else other)
        for unit in range(n_mixed):
            put_rows(rows[unit], unit)

    by_class(write)
    put_keys(near_same, mine)
    put_keys(near_other, other)
    for unit in range(n_mixed, units):
        put_rows(rest, unit, (unit - n_mixed) * 2 * part)

    row = lax.broadcasted_iota(jnp.int32, (heads, width), 0)
    col = lax.broadcasted_iota(jnp.int32, (heads, width), 1)
    pick = jnp.where(col // HEAD_DIM == row, 1.0, 0.0).astype(BF16)
    prod = do[...].astype(F32) * o[...].astype(F32)
    high = prod.astype(BF16)
    low = (prod - high.astype(F32)).astype(BF16)
    delta = dot(pick, high, 1, 1) + dot(pick, low, 1, 1)
    lse = sums[...] * LOG2E

    def write_stats(mine, other):
        stat_own[:n, :] = lse[mine * n : (mine + 1) * n, :]
        stat_own[n:, :] = delta[mine * n : (mine + 1) * n, :]
        left = jnp.concatenate([x[other * n : (other + 1) * n, :] for x in (lse, delta)], 0)
        terms = []
        for _ in range(3):
            term = left.astype(BF16).astype(F32)
            left = left - term
            terms.append(term)
        terms.append(jnp.zeros((LANES - 6 * n, tokens), F32))
        rest[:, rest.shape[1] - LANES :] = jnp.transpose(jnp.concatenate(terms, 0)).astype(BF16)

    by_parity(write_stats)
    near, far = seen_sides(owners, shards)
    line = lax.broadcasted_iota(jnp.int32, flags.shape, 0)
    flags[...] = jnp.where(line == 0, near.astype(jnp.int32), far.astype(jnp.int32))


def stack_heads(load, first, group):
    blocks = []
    for pair in range(group // 2):
        two = load((first + 2 * pair) * HEAD_DIM, 2 * HEAD_DIM)
        blocks += [two[:, :HEAD_DIM], two[:, HEAD_DIM:]]
    return jnp.concatenate(blocks, 0)


def stack_stats(stats, first, group):
    return jnp.concatenate([stats[first + g : first + g + 1] for g in range(group)], 1)


def head_grads(q, do, lse, delta, k, v):
    scores = dot(k, q, 1, 1)
    dprobs = dot(v, do, 1, 1)
    probs = jnp.exp2(scores * (LOG2E / math.sqrt(HEAD_DIM)) - lse)
    dscores = (probs * (dprobs - delta)).astype(BF16)
    dv = dot(probs.astype(BF16), do, 1, 0)
    dk = dot(dscores, q, 1, 0)
    dq = dot(k, dscores, 0, 0)
    return dk, dv, dq


def side_grads(load_q, load_do, stats, kv, put):
    heads = stats.shape[0] // 2
    part = kv.shape[1] // 2
    kv_heads = part // HEAD_DIM
    group = heads // kv_heads
    width = 2 * HEAD_DIM
    for pair in range(kv_heads // 2):
        at = pair * width
        k_two, v_two = kv[:, at : at + width], kv[:, part + at : part + at + width]
        dks, dvs = [], []
        for odd in range(2):
            first = (2 * pair + odd) * group
            lanes = slice(odd * HEAD_DIM, (odd + 1) * HEAD_DIM)
            dk, dv, dq = head_grads(
                stack_heads(load_q, first, group),
                stack_heads(load_do, first, group),
                stack_stats(stats, first, group),
                stack_stats(stats, heads + first, group),
                k_two[:, lanes],
                v_two[:, lanes],
            )
            dks.append(dk)
            dvs.append(dv)
            put(first, dq)
        put.store(at, part, jnp.concatenate(dks, 1), jnp.concatenate(dvs, 1))


class Put:
    def __init__(self, dq_acc, group, store):
        self.dq_acc, self.group, self.store = dq_acc, group, store

    def __call__(self, first, dq):
        tok = self.dq_acc.shape[1]
        for g in range(self.group):
            rows = slice((first + g) * HEAD_DIM, (first + g + 1) * HEAD_DIM)
            self.dq_acc[rows, :] += dq[:, g * tok : (g + 1) * tok]


def write_dq(dq_acc, outs):
    factor = 1.0 / math.sqrt(HEAD_DIM)
    rows = dq_acc.shape[0] // len(outs)
    for i, out in enumerate(outs):
        for at in range(0, rows, LANES):
            block = jnp.transpose(dq_acc[i * rows + at : i * rows + at + LANES, :])
            out[:, at : at + LANES] = (block * factor).astype(BF16)


def seen(flags, which):
    return jnp.max(flags[which : which + 1, :]) > 0


def seen_sides(owners, shards):
    rank, z = lax.axis_index("blk"), lax.axis_index("ulysses")
    n_blk = lax.axis_size("blk")
    before = lax.rem(rank + n_blk - 1, n_blk)
    place = lax.div(z, shards // 2)
    mine = owners[2 * rank + place]
    return mine > owners[2 * before + place], mine > owners[2 * before + 1 - place]


def own_rows(flags, which, q, do, stats, kv, acc, dq_acc):
    heads = stats.shape[0] // 2
    half = heads * HEAD_DIM
    group = 2 * half // kv.shape[1]
    mine = parity()

    def from_half(ref):
        def load(at, size):
            return ref[:, pl.ds(pl.multiple_of(mine * half + at, size), size)]

        return load

    def store(at, part, dk, dv):
        acc[:, at : at + dk.shape[1]] = dk
        acc[:, part + at : part + at + dv.shape[1]] = dv

    @pl.when(seen(flags, which))
    def _():
        side_grads(from_half(q), from_half(do), stats[...], kv, Put(dq_acc, group, store))


def own_far_kernel(shards, flags, q, do, stats, *rest):
    side = shards // 2
    slots = rest[:-4]
    kv, q_in, acc, dq_acc = rest[-4:]
    tok = q.shape[0]

    def sort(which):
        keys, rows = apart(which, slots, side)
        for d in range(side):
            kv[d * tok : (d + 1) * tok, :] = keys[d][...]
        for unit in range(len(rows)):
            q_in[unit * tok : (unit + 1) * tok, :] = rows[unit][...]

    by_class(sort)
    dq_acc[...] = jnp.zeros_like(dq_acc)
    own_rows(flags, 1, q, do, stats, kv, acc, dq_acc)


def own_near_kernel(shards, flags, q, do, stats, dq_before, *rest):
    side = shards // 2
    slots = rest[:side]
    kv, acc, dq_own, dq_acc = rest[side:]
    tok = q.shape[0]
    for d in range(side):
        kv[d * tok : (d + 1) * tok, :] = slots[d][...]
    dq_acc[...] = dq_before[...]
    own_rows(flags, 0, q, do, stats, kv, acc, dq_acc)
    write_dq(dq_acc, [dq_own])


def partner_rows(flags, which, q_in, rest, kv, acc, dkv, dq_acc):
    tok = rest.shape[0]
    n_mixed = q_in.shape[0] // tok
    unit_size = q_in.shape[1]
    part = unit_size // 2
    n = 2 * dq_acc.shape[0] // HEAD_DIM
    group = part // HEAD_DIM
    factor = 1.0 / math.sqrt(HEAD_DIM)

    def loader(offset):
        def load(at, size):
            unit, lane = at // part, at % part
            if unit < n_mixed:
                return q_in[unit * tok : (unit + 1) * tok, offset + lane : offset + lane + size]
            start = (unit - n_mixed) * unit_size + offset + lane
            return rest[:, start : start + size]

        return load

    @pl.when(seen(flags, which))
    def _():
        terms = jnp.transpose(rest[:, rest.shape[1] - LANES :].astype(F32))
        stats = terms[:n] + terms[n : 2 * n] + terms[2 * n : 3 * n]

        def store(at, part, dk, dv):
            k_at = slice(at, at + dk.shape[1])
            v_at = slice(part + at, part + at + dv.shape[1])
            dk = ((dk + acc[:, k_at]) * factor).astype(BF16)
            dv = (dv + acc[:, v_at]).astype(BF16)
            for m, out in enumerate(dkv):
                out[:, k_at] = dk[m * tok : (m + 1) * tok]
                out[:, v_at] = dv[m * tok : (m + 1) * tok]

        side_grads(loader(0), loader(part), stats, kv, Put(dq_acc, group, store))

    @pl.when(jnp.logical_not(seen(flags, which)))
    def _():
        for out in dkv:
            out[...] = jnp.zeros_like(out)


def partner_near_kernel(flags, q_in, rest, kv, acc, *outs):
    dq_acc = outs[-1]
    dq_acc[...] = jnp.zeros_like(dq_acc)
    partner_rows(flags, 0, q_in, rest, kv, acc, outs[:-1], dq_acc)


def partner_far_kernel(shards, flags, q_in, rest, kv, acc, dq_before, *outs):
    slots, dkv, dq_acc = outs[: -1 - shards // 2], outs[-1 - shards // 2 : -1], outs[-1]
    dq_acc[...] = dq_before[...]
    partner_rows(flags, 1, q_in, rest, kv, acc, dkv, dq_acc)

    def write(which):
        keys, rows = apart(which, slots, shards // 2)
        for out, ref in zip(keys, dkv):
            out[...] = ref[...]
        write_dq(dq_acc, rows)

    by_class(write)


def add_up(refs, parities):
    totals = []
    for odd in range(2):
        total = refs[odd][...].astype(F32)
        for m in range(odd + 2, parities, 2):
            total = total + refs[m][...].astype(F32)
        totals.append(total)
    return totals


def join_near_kernel(*refs):
    refs, outs = refs[:-2], refs[-2:]
    for out, total in zip(outs, add_up(refs, len(refs))):
        out[...] = total


def join_kernel(shards, dq_own, near_same, near_other, *rest):
    slots = rest[:-3]
    gq, gk, gv = rest[-3:]
    half = dq_own.shape[1]
    part = gk.shape[1] // 2

    def write_class(which):
        keys, rows = apart(which, slots, shards // 2)
        totals = [a[...] + b for a, b in zip((near_same, near_other), add_up(keys, len(keys)))]

        def write(mine, other):
            gq[:, mine * half : (mine + 1) * half] = dq_own[...]
            size = half // len(rows)
            for i, ref in enumerate(rows):
                gq[:, other * half + i * size : other * half + (i + 1) * size] = ref[...]
            for total, place in zip(totals, (mine, other)):
                gk[:, place * part : (place + 1) * part] = total[:, :part].astype(BF16)
                gv[:, place * part : (place + 1) * part] = total[:, part:].astype(BF16)

        by_parity(write)

    by_class(write_class)


def limit(mib):
    return pltpu.CompilerParams(vmem_limit_bytes=mib * 1024 * 1024)


def per_device(queries, key_states, value_states, attn_out, grad_out, log_sums, owners):
    n_blk, n_uly = lax.axis_size("blk"), lax.axis_size("ulysses")
    tok, width = queries.shape
    heads = log_sums.shape[1]
    kv_width = key_states.shape[1]
    half = width // 2
    side = n_uly // 2

    n_units = width // kv_width
    n_mixed = min(n_units, side)
    rest_width = (n_units - n_mixed) * kv_width + LANES

    def flips(first, second):
        return [in_turn(which, first, second) for which in range(2)]

    def move(value, *by_kind):
        pairs = []
        for b in range(n_blk):
            for u in range(n_uly):
                step, flip = by_kind[(b + u // side) % len(by_kind)]
                pairs.append((b * n_uly + u, ((b + step) % n_blk) * n_uly + (u ^ flip)))
        return lax.ppermute(value, ("blk", "ulysses"), pairs)

    def shape(*dims, dtype=BF16):
        return jax.ShapeDtypeStruct(dims, dtype)

    def cover(flops):
        return pl.CostEstimate(flops=flops, bytes_accessed=1 << 20, transcendentals=0)

    unit = shape(tok, kv_width)
    sides = shape(side * tok, kv_width)
    sides_wide = shape(side * tok, kv_width, dtype=F32)
    dq_wide = shape(half, tok, dtype=F32)
    *slots, near_same, near_other, rest, stat_own, flags = pl.pallas_call(
        functools.partial(pack_kernel, n_uly),
        out_shape=[unit] * (side + n_mixed + 2)
        + [
            shape(tok, rest_width),
            shape(heads, tok, dtype=F32),
            shape(8, LANES, dtype=jnp.int32),
        ],
        in_specs=[SMEM] + [VMEM] * 6,
        out_specs=[VMEM] * (side + n_mixed + 5),
        compiler_params=limit(PACK_MIB),
        name="pack",
    )(owners, queries, grad_out, attn_out, jnp.transpose(log_sums), key_states, value_states)
    turns = flips([(1, d) for d in range(side, n_uly)], [(0, 1)] * n_mixed)
    slots = [move(x, one, two) for x, one, two in zip(slots, *turns)]
    kv_near = [move(near_other if d % 2 else near_same, (1, d)) for d in range(side)]
    rest = move(rest, (0, 1))
    kv_far, q_in, acc_far, dq_part = pl.pallas_call(
        functools.partial(own_far_kernel, n_uly),
        out_shape=[sides, shape(n_mixed * tok, kv_width), sides_wide, dq_wide],
        in_specs=[VMEM] * (4 + side + n_mixed),
        out_specs=[VMEM] * 4,
        compiler_params=limit(32),
        cost_estimate=cover(SHORT),
        name="own_far",
    )(flags, queries, grad_out, stat_own, *slots)
    kv_near, acc_near, dq_own = pl.pallas_call(
        functools.partial(own_near_kernel, n_uly),
        out_shape=[sides, sides_wide, shape(tok, half)],
        in_specs=[VMEM] * (5 + side),
        out_specs=[VMEM] * 3,
        scratch_shapes=[pltpu.VMEM((half, tok), F32)],
        compiler_params=limit(32),
        cost_estimate=cover(SHORT),
        name="own_near",
    )(flags, queries, grad_out, stat_own, dq_part, *kv_near)
    *near, dq_part = pl.pallas_call(
        partner_near_kernel,
        out_shape=[unit] * side + [dq_wide],
        in_specs=[VMEM] * 5,
        out_specs=[VMEM] * (side + 1),
        compiler_params=limit(32),
        cost_estimate=cover(SHORT),
        name="near",
    )(flags, q_in, rest, kv_near, acc_near)
    near = [move(x, (-1, d)) for d, x in enumerate(near)]
    n_back = half // kv_width
    slots = pl.pallas_call(
        functools.partial(partner_far_kernel, n_uly),
        out_shape=[unit] * (side + n_back),
        in_specs=[VMEM] * 6,
        out_specs=[VMEM] * (side + n_back),
        scratch_shapes=[pltpu.VMEM((tok, kv_width), BF16)] * side + [pltpu.VMEM((half, tok), F32)],
        compiler_params=limit(32),
        cost_estimate=cover(SHORT),
        name="far",
    )(flags, q_in, rest, kv_far, acc_far, dq_part)
    turns = flips([(-1, d) for d in range(side, n_uly)], [(0, 1)] * n_back)
    slots = [move(x, one, two) for x, one, two in zip(slots, *turns)]
    near = pl.pallas_call(
        join_near_kernel,
        out_shape=[shape(tok, kv_width, dtype=F32)] * 2,
        in_specs=[VMEM] * side,
        out_specs=[VMEM] * 2,
        compiler_params=limit(8),
        cost_estimate=cover(LONG),
        name="join_near",
    )(*near)
    return tuple(
        pl.pallas_call(
            functools.partial(join_kernel, n_uly),
            out_shape=[shape(tok, width), shape(tok, kv_width), shape(tok, kv_width)],
            in_specs=[VMEM] * (3 + side + n_back),
            out_specs=[VMEM] * 3,
            compiler_params=limit(8),
            name="join",
        )(dq_own, *near, *slots)
    )


def solution(mesh):
    rows = P(("blk", "ulysses"), None)
    return jax.shard_map(
        per_device,
        mesh=mesh,
        in_specs=(rows, rows, rows, rows, rows, rows, P()),
        out_specs=(rows, rows, rows),
        check_vma=False,
    )
```

```python
import functools
import math

import jax
import jax.numpy as jnp
from jax import lax
from jax.experimental import pallas as pl
from jax.experimental.pallas import tpu as pltpu
from jax.sharding import PartitionSpec as P

HEAD_DIM = 64
LANES = 128
PACK_MIB = 60
SHORT = 1 << 31
LOG2E = math.log2(math.e)
BF16 = jnp.bfloat16
F32 = jnp.float32
VMEM = pl.BlockSpec(memory_space=pltpu.VMEM)
SMEM = pl.BlockSpec(memory_space=pltpu.SMEM)


def dot(a, b, a_dim, b_dim):
    return lax.dot_general(
        a, b, (((a_dim,), (b_dim,)), ((), ())), preferred_element_type=F32
    )


def parity():
    return lax.rem(lax.axis_index("ulysses"), 2)


def by_parity(write):
    for mine in range(2):

        @pl.when(parity() == mine)
        def _():
            write(mine, 1 - mine)


def by_class(write):
    side = lax.div(lax.axis_index("ulysses"), lax.axis_size("ulysses") // 2)
    odd = lax.rem(lax.axis_index("blk") + side, 2)
    for which in range(2):

        @pl.when(odd == which)
        def _():
            write(which)


def in_turn(which, first, second):
    return [*first, *second] if which == 0 else [*second, *first]


def apart(which, refs, n_first):
    n_second = len(refs) - n_first
    if which == 0:
        return refs[:n_first], refs[n_first:]
    return refs[n_second:], refs[:n_second]


def pack_kernel(side, n_mixed, owners, q, do, o, sums, k, v, *outs):
    near_same, near_other, *rest, stat_own, stat_send, flags = outs[side + n_mixed :]
    slots = outs[: side + n_mixed]
    tokens, width = do.shape
    heads = sums.shape[0]
    half = width // 2
    part = k.shape[1] // 2
    n = heads // 2
    mine = parity()
    other = 1 - mine

    def cut(ref, which, size, at=0, wide=None):
        wide = size if wide is None else wide
        return ref[:, pl.ds(pl.multiple_of(which * size + at, wide), wide)]

    def put_keys(out, which):
        out[:, :part] = cut(k, which, part)
        out[:, part:] = cut(v, which, part)

    def put_rows(out, unit, at=0):
        out[:, at : at + part] = cut(q, other, half, unit * part, part)
        out[:, at + part : at + 2 * part] = cut(do, other, half, unit * part, part)

    units = half // part

    def write(which):
        keys, rows = apart(which, slots, side)
        for d in range(side):
            put_keys(keys[d], mine if d % 2 == 0 else other)
        for unit in range(n_mixed):
            put_rows(rows[unit], unit)

    by_class(write)
    put_keys(near_same, mine)
    put_keys(near_other, other)
    for unit in range(n_mixed, units):
        put_rows(rest[0], unit, (unit - n_mixed) * 2 * part)

    row = lax.broadcasted_iota(jnp.int32, (heads, width), 0)
    col = lax.broadcasted_iota(jnp.int32, (heads, width), 1)
    pick = jnp.where(col // HEAD_DIM == row, 1.0, 0.0).astype(BF16)
    prod = do[...].astype(F32) * o[...].astype(F32)
    high = prod.astype(BF16)
    low = (prod - high.astype(F32)).astype(BF16)
    delta = dot(pick, high, 1, 1) + dot(pick, low, 1, 1)
    lse = sums[...] * LOG2E

    def write_stats(mine, other):
        stat_own[:n, :] = lse[mine * n : (mine + 1) * n, :]
        stat_own[n:, :] = delta[mine * n : (mine + 1) * n, :]
        stat_send[:n, :] = lse[other * n : (other + 1) * n, :]
        stat_send[n:, :] = delta[other * n : (other + 1) * n, :]

    by_parity(write_stats)
    near, far = seen_sides(owners, 2 * side)
    line = lax.broadcasted_iota(jnp.int32, flags.shape, 0)
    flags[...] = jnp.where(line == 0, near.astype(jnp.int32), far.astype(jnp.int32))


def stack_heads(load, first, group):
    blocks = []
    for pair in range(group // 2):
        two = load((first + 2 * pair) * HEAD_DIM, 2 * HEAD_DIM)
        blocks += [two[:, :HEAD_DIM], two[:, HEAD_DIM:]]
    return jnp.concatenate(blocks, 0)


def stack_stats(stats, first, group):
    return jnp.concatenate([stats[first + g : first + g + 1] for g in range(group)], 1)


def head_grads(q, do, lse, delta, k, v):
    scores = dot(k, q, 1, 1)
    dprobs = dot(v, do, 1, 1)
    probs = jnp.exp2(scores * (LOG2E / math.sqrt(HEAD_DIM)) - lse)
    dscores = (probs * (dprobs - delta)).astype(BF16)
    dv = dot(probs.astype(BF16), do, 1, 0)
    dk = dot(dscores, q, 1, 0)
    dq = dot(k, dscores, 0, 0)
    return dk, dv, dq


def side_grads(pairs, load_q, load_do, stats, kv, put):
    heads = stats.shape[0] // 2
    part = kv.shape[1] // 2
    kv_heads = part // HEAD_DIM
    group = heads // kv_heads
    width = 2 * HEAD_DIM
    for pair in pairs:
        at = pair * width
        k_two, v_two = kv[:, at : at + width], kv[:, part + at : part + at + width]
        dks, dvs = [], []
        for odd in range(2):
            first = (2 * pair + odd) * group
            lanes = slice(odd * HEAD_DIM, (odd + 1) * HEAD_DIM)
            dk, dv, dq = head_grads(
                stack_heads(load_q, first, group),
                stack_heads(load_do, first, group),
                stack_stats(stats, first, group),
                stack_stats(stats, heads + first, group),
                k_two[:, lanes],
                v_two[:, lanes],
            )
            dks.append(dk)
            dvs.append(dv)
            put(first, dq)
        put.store(at, jnp.concatenate(dks, 1), jnp.concatenate(dvs, 1))


class Put:
    def __init__(self, dq_acc, group, store):
        self.dq_acc, self.group, self.store = dq_acc, group, store

    def __call__(self, first, dq):
        tok = self.dq_acc.shape[1]
        for g in range(self.group):
            rows = slice((first + g) * HEAD_DIM, (first + g + 1) * HEAD_DIM)
            self.dq_acc[rows, :] += dq[:, g * tok : (g + 1) * tok]


def turned_dq(dq_acc, first, last):
    factor = 1.0 / math.sqrt(HEAD_DIM)
    blocks = [
        jnp.transpose(dq_acc[at : at + LANES, :])
        for at in range(first * HEAD_DIM, last * HEAD_DIM, LANES)
    ]
    return (jnp.concatenate(blocks, 1) * factor).astype(BF16)


def seen(flags, which):
    return jnp.max(flags[which : which + 1, :]) > 0


def seen_sides(owners, shards):
    rank, z = lax.axis_index("blk"), lax.axis_index("ulysses")
    n_blk = lax.axis_size("blk")
    before = lax.rem(rank + n_blk - 1, n_blk)
    place = lax.div(z, shards // 2)
    mine = owners[2 * rank + place]
    return mine > owners[2 * before + place], mine > owners[2 * before + 1 - place]


def own_rows(flags, which, q, do, stats, kv, acc, dq_acc):
    heads = stats.shape[0] // 2
    half = heads * HEAD_DIM
    part = kv.shape[1] // 2
    mine = parity()

    def from_half(ref):
        def load(at, size):
            return ref[:, pl.ds(pl.multiple_of(mine * half + at, size), size)]

        return load

    def store(at, dk, dv):
        acc[:, at : at + dk.shape[1]] = dk
        acc[:, part + at : part + at + dv.shape[1]] = dv

    @pl.when(seen(flags, which))
    def _():
        pairs = range(part // LANES)
        put = Put(dq_acc, half // part, store)
        side_grads(pairs, from_half(q), from_half(do), stats[...], kv, put)


def own_far_kernel(side, flags, q, do, stats, *rest):
    slots = rest[:-4]
    kv, q_in, acc, dq_acc = rest[-4:]
    tok = q.shape[0]

    def sort(which):
        keys, rows = apart(which, slots, side)
        for d in range(side):
            kv[d * tok : (d + 1) * tok, :] = keys[d][...]
        for unit in range(len(rows)):
            q_in[unit * tok : (unit + 1) * tok, :] = rows[unit][...]

    by_class(sort)
    dq_acc[...] = jnp.zeros_like(dq_acc)
    own_rows(flags, 1, q, do, stats, kv, acc, dq_acc)


def partner_rows(flags, which, pairs, load_q, load_do, stats, kv, acc, dq_acc, write):
    part = kv.shape[1] // 2
    factor = 1.0 / math.sqrt(HEAD_DIM)

    @pl.when(seen(flags, which))
    def _():
        def store(at, dk, dv):
            dk = (dk + acc[:, at : at + dk.shape[1]]) * factor
            dv = dv + acc[:, part + at : part + at + dv.shape[1]]
            write(at // LANES, dk.astype(BF16), dv.astype(BF16))

        side_grads(pairs, load_q, load_do, stats[...], kv, Put(dq_acc, part // HEAD_DIM, store))

    @pl.when(jnp.logical_not(seen(flags, which)))
    def _():
        for pair in pairs:
            zero = jnp.zeros((kv.shape[0], LANES), BF16)
            write(pair, zero, zero)


def early_kernel(side, flags, q, do, stats, stats_in, dq_before, kv_far, q_in, acc_far, *rest):
    slots = rest[:side]
    kv, acc, dq_own, near_done, far_done, dq_done, dq_acc = rest[side:]
    tok, part = q.shape[0], kv.shape[1] // 2
    heads = stats.shape[0] // 2
    for d in range(side):
        kv[d * tok : (d + 1) * tok, :] = slots[d][...]
    dq_acc[...] = dq_before[...]
    own_rows(flags, 0, q, do, stats, kv, acc, dq_acc)
    dq_own[...] = turned_dq(dq_acc, 0, heads)
    n_units = q_in.shape[0] // tok
    pairs = range(n_units // 2)
    dq_acc[...] = jnp.zeros_like(dq_acc)

    def loader(offset):
        def load(at, size):
            unit, lane = at // part, offset + at % part
            return q_in[unit * tok : (unit + 1) * tok, lane : lane + size]

        return load

    for which, keys, total, done in ((0, kv, acc, near_done), (1, kv_far, acc_far, far_done)):

        def write(pair, dk, dv, done=done):
            done[:, 2 * pair * LANES : (2 * pair + 1) * LANES] = dk
            done[:, (2 * pair + 1) * LANES : (2 * pair + 2) * LANES] = dv

        partner_rows(
            flags, which, pairs, loader(0), loader(part), stats_in, keys, total, dq_acc, write
        )
    dq_done[...] = turned_dq(dq_acc, 0, n_units * part // HEAD_DIM)


def late_kernel(side, flags, stats_in, near_kv, far_kv, near_acc, far_acc, near_done, far_done, dq_done, *rest):
    dq_acc = rest[-1]
    kv_width = near_kv.shape[1]
    part = kv_width // 2
    tok = dq_acc.shape[1]
    units = dq_acc.shape[0] // part
    early = dq_done.shape[1] // part
    rows = None
    if early < units:
        rows, rest = rest[0], rest[1:]
    near, slots = rest[:side], rest[side:-1]
    if rows is not None:
        dq_acc[...] = jnp.zeros_like(dq_acc)

    def loader(offset):
        def load(at, size):
            lane = (at // part - early) * kv_width + offset + at % part
            return rows[:, lane : lane + size]

        return load

    def send_back(outs, which, keys, total, done):
        def write(pair, dk, dv):
            for m, out in enumerate(outs):
                out[:, pair * LANES : (pair + 1) * LANES] = dk[m * tok : (m + 1) * tok]
                out[:, part + pair * LANES : part + (pair + 1) * LANES] = dv[m * tok : (m + 1) * tok]

        for pair in range(early // 2):
            at = 2 * pair * LANES
            write(pair, done[:, at : at + LANES], done[:, at + LANES : at + 2 * LANES])
        if rows is not None:
            pairs = range(early // 2, units // 2)
            partner_rows(
                flags, which, pairs, loader(0), loader(part), stats_in, keys, total, dq_acc, write
            )

    send_back(near, 0, near_kv, near_acc, near_done)

    def write_slots(which):
        keys, dq = apart(which, slots, side)
        send_back(keys, 1, far_kv, far_acc, far_done)
        columns = [dq_done[...]]
        if rows is not None:
            columns.append(turned_dq(dq_acc, early * part // HEAD_DIM, units * part // HEAD_DIM))
        whole = jnp.concatenate(columns, 1)
        for i, out in enumerate(dq):
            out[...] = whole[:, i * kv_width : (i + 1) * kv_width]

    by_class(write_slots)


def add_up(refs):
    totals = []
    for odd in range(2):
        total = refs[odd][...].astype(F32)
        for m in range(odd + 2, len(refs), 2):
            total = total + refs[m][...].astype(F32)
        totals.append(total)
    return totals


def join_kernel(side, dq_own, *rest):
    near, slots = rest[:side], rest[side:-3]
    gq, gk, gv = rest[-3:]
    half = dq_own.shape[1]
    part = gk.shape[1] // 2

    def write_class(which):
        keys, rows = apart(which, slots, side)
        totals = [a + b for a, b in zip(add_up(near), add_up(keys))]

        def write(mine, other):
            gq[:, mine * half : (mine + 1) * half] = dq_own[...]
            size = half // len(rows)
            for i, ref in enumerate(rows):
                gq[:, other * half + i * size : other * half + (i + 1) * size] = ref[...]
            for total, place in zip(totals, (mine, other)):
                gk[:, place * part : (place + 1) * part] = total[:, :part].astype(BF16)
                gv[:, place * part : (place + 1) * part] = total[:, part:].astype(BF16)

        by_parity(write)

    by_class(write_class)


def limit(mib):
    return pltpu.CompilerParams(vmem_limit_bytes=mib * 1024 * 1024)


def per_device(queries, key_states, value_states, attn_out, grad_out, log_sums, owners):
    n_blk, n_uly = lax.axis_size("blk"), lax.axis_size("ulysses")
    tok, width = queries.shape
    heads = log_sums.shape[1]
    kv_width = key_states.shape[1]
    half = width // 2
    side = n_uly // 2

    n_units = width // kv_width
    n_mixed = min(n_units, side)
    n_back = half // kv_width

    def flips(first, second):
        return [in_turn(which, first, second) for which in range(2)]

    def move(value, *by_kind):
        pairs = []
        for b in range(n_blk):
            for u in range(n_uly):
                step, flip = by_kind[(b + u // side) % len(by_kind)]
                pairs.append((b * n_uly + u, ((b + step) % n_blk) * n_uly + (u ^ flip)))
        return lax.ppermute(value, ("blk", "ulysses"), pairs)

    def shape(*dims, dtype=BF16):
        return jax.ShapeDtypeStruct(dims, dtype)

    def cover(flops):
        return pl.CostEstimate(flops=flops, bytes_accessed=1 << 20, transcendentals=0)

    unit = shape(tok, kv_width)
    sides = shape(side * tok, kv_width)
    sides_wide = shape(side * tok, kv_width, dtype=F32)
    dq_wide = shape(half, tok, dtype=F32)
    stats = shape(heads, tok, dtype=F32)
    whole = n_mixed == n_units
    late = [] if whole else [shape(tok, (n_units - n_mixed) * kv_width)]
    outs = [unit] * (side + n_mixed + 2) + late + [stats, stats, shape(8, LANES, dtype=jnp.int32)]
    packed = pl.pallas_call(
        functools.partial(pack_kernel, side, n_mixed),
        out_shape=outs,
        in_specs=[SMEM] + [VMEM] * 6,
        out_specs=[VMEM] * len(outs),
        compiler_params=limit(PACK_MIB),
        name="pack",
    )(owners, queries, grad_out, attn_out, jnp.transpose(log_sums), key_states, value_states)
    slots, (near_same, near_other, *rest, stat_own, stat_send, flags) = (
        packed[: side + n_mixed],
        packed[side + n_mixed :],
    )
    turns = flips([(1, d) for d in range(side, n_uly)], [(0, 1)] * n_mixed)
    slots = [move(x, one, two) for x, one, two in zip(slots, *turns)]
    stat_in = move(stat_send, (0, 1))
    near = [move(near_other if d % 2 else near_same, (1, d)) for d in range(side)]
    rest = [move(x, (0, 1)) for x in rest]
    kv_far, q_in, acc_far, dq_part = pl.pallas_call(
        functools.partial(own_far_kernel, side),
        out_shape=[sides, shape(n_mixed * tok, kv_width), sides_wide, dq_wide],
        in_specs=[VMEM] * (4 + side + n_mixed),
        out_specs=[VMEM] * 4,
        compiler_params=limit(32),
        cost_estimate=cover(SHORT),
        name="own_far",
    )(flags, queries, grad_out, stat_own, *slots)
    done = shape(side * tok, n_mixed * LANES)
    outs = [sides, sides_wide, shape(tok, half), done, done, shape(tok, n_mixed * kv_width // 2)]
    kv_near, acc_near, dq_own, near_done, far_done, dq_done = pl.pallas_call(
        functools.partial(early_kernel, side),
        out_shape=outs,
        in_specs=[VMEM] * (9 + side),
        out_specs=[VMEM] * len(outs),
        scratch_shapes=[pltpu.VMEM((half, tok), F32)],
        compiler_params=limit(32),
        cost_estimate=cover(SHORT),
        name="early",
    )(flags, queries, grad_out, stat_own, stat_in, dq_part, kv_far, q_in, acc_far, *near)
    back = pl.pallas_call(
        functools.partial(late_kernel, side),
        out_shape=[unit] * (n_uly + n_back),
        in_specs=[VMEM] * (9 + len(rest)),
        out_specs=[VMEM] * (n_uly + n_back),
        scratch_shapes=[pltpu.VMEM((half, tok), F32)],
        compiler_params=limit(32),
        cost_estimate=cover(SHORT),
        name="late",
    )(flags, stat_in, kv_near, kv_far, acc_near, acc_far, near_done, far_done, dq_done, *rest)
    near, slots = back[:side], back[side:]
    turns = flips([(-1, d) for d in range(side, n_uly)], [(0, 1)] * n_back)
    slots = [move(x, one, two) for x, one, two in zip(slots, *turns)]
    near = [move(near[d], (-1, d)) for d in reversed(range(side))][::-1]
    return tuple(
        pl.pallas_call(
            functools.partial(join_kernel, side),
            out_shape=[shape(tok, width), shape(tok, kv_width), shape(tok, kv_width)],
            in_specs=[VMEM] * (1 + n_uly + n_back),
            out_specs=[VMEM] * 3,
            compiler_params=limit(8),
            name="join",
        )(dq_own, *near, *slots)
    )


def solution(mesh):
    rows = P(("blk", "ulysses"), None)
    return jax.shard_map(
        per_device,
        mesh=mesh,
        in_specs=(rows, rows, rows, rows, rows, rows, P()),
        out_specs=(rows, rows, rows),
        check_vma=False,
    )
```

```python
import functools
import math

import jax
import jax.numpy as jnp
from jax import lax
from jax.experimental import pallas as pl
from jax.experimental.pallas import tpu as pltpu
from jax.sharding import PartitionSpec as P

HEAD_DIM = 64
LANES = 128
STAT_ROWS = 16
PACK_MIB = 60
SHORT = 1 << 31
LOG2E = math.log2(math.e)
BF16 = jnp.bfloat16
F32 = jnp.float32
VMEM = pl.BlockSpec(memory_space=pltpu.VMEM)
SMEM = pl.BlockSpec(memory_space=pltpu.SMEM)


def dot(a, b, a_dim, b_dim):
    return lax.dot_general(
        a, b, (((a_dim,), (b_dim,)), ((), ())), preferred_element_type=F32
    )


def parity():
    return lax.rem(lax.axis_index("ulysses"), 2)


def by_parity(write):
    for mine in range(2):

        @pl.when(parity() == mine)
        def _():
            write(mine, 1 - mine)


def by_class(write):
    side = lax.div(lax.axis_index("ulysses"), lax.axis_size("ulysses") // 2)
    odd = lax.rem(lax.axis_index("blk") + side, 2)
    for which in range(2):

        @pl.when(odd == which)
        def _():
            write(which)


def in_turn(which, first, second):
    return [*first, *second] if which == 0 else [*second, *first]


def apart(which, refs, n_first):
    n_second = len(refs) - n_first
    if which == 0:
        return refs[:n_first], refs[n_first:]
    return refs[n_second:], refs[:n_second]


def split3(x):
    terms = []
    for _ in range(3):
        term = x.astype(BF16).astype(F32)
        x = x - term
        terms.append(term)
    return terms


def pack_kernel(side, n_mixed, owners, q, do, o, sums, k, v, *refs):
    n_slots = side + n_mixed
    n_rest = len(refs) - n_slots - 5
    slots, near_same, near_other = refs[:n_slots], refs[n_slots], refs[n_slots + 1]
    rest = refs[n_slots + 2 : n_slots + 2 + n_rest]
    stat_own, flags, stat_rows = refs[n_slots + 2 + n_rest : n_slots + 5 + n_rest]
    tokens, width = do.shape
    heads = sums.shape[0]
    half = width // 2
    part = k.shape[1] // 2
    n = heads // 2
    group = part // HEAD_DIM
    units = half // part
    mine = parity()
    other = 1 - mine

    def cut(ref, which, size, at=0, wide=None):
        wide = size if wide is None else wide
        return ref[:, pl.ds(pl.multiple_of(which * size + at, wide), wide)]

    def put_keys(out, which):
        out[:tokens, :part] = cut(k, which, part)
        out[:tokens, part:] = cut(v, which, part)

    def put_rows(out, unit, at=0):
        out[:tokens, at : at + part] = cut(q, other, half, unit * part, part)
        out[:tokens, at + part : at + 2 * part] = cut(do, other, half, unit * part, part)
        out[tokens:, at : at + 2 * part] = stat_rows[unit * STAT_ROWS : (unit + 1) * STAT_ROWS, :]

    row = lax.broadcasted_iota(jnp.int32, (heads, width), 0)
    col = lax.broadcasted_iota(jnp.int32, (heads, width), 1)
    pick = jnp.where(col // HEAD_DIM == row, 1.0, 0.0).astype(BF16)
    prod = do[...].astype(F32) * o[...].astype(F32)
    high = prod.astype(BF16)
    low = (prod - high.astype(F32)).astype(BF16)
    delta = dot(pick, high, 1, 1) + dot(pick, low, 1, 1)
    lse = sums[...] * LOG2E

    def write_stats(mine, other):
        stat_own[:n, :] = lse[mine * n : (mine + 1) * n, :]
        stat_own[n:, :] = delta[mine * n : (mine + 1) * n, :]
        stat_rows[...] = jnp.zeros_like(stat_rows)
        for unit in range(units):
            first = other * n + unit * group
            both = jnp.concatenate([x[first : first + group, :] for x in (lse, delta)], 0)
            high, middle, low = split3(both)
            rows = slice(unit * STAT_ROWS, (unit + 1) * STAT_ROWS)
            stat_rows[rows, :tokens] = jnp.concatenate([high, middle], 0).astype(BF16)
            low = jnp.concatenate([low, jnp.zeros_like(low)], 0)
            stat_rows[rows, tokens : 2 * tokens] = low.astype(BF16)

    by_parity(write_stats)

    def write(which):
        keys, rows = apart(which, slots, side)
        for d in range(side):
            put_keys(keys[d], mine if d % 2 == 0 else other)
            keys[d][tokens:, :] = jnp.zeros((STAT_ROWS, 2 * part), BF16)
        for unit in range(n_mixed):
            put_rows(rows[unit], unit)

    by_class(write)
    put_keys(near_same, mine)
    put_keys(near_other, other)
    for unit in range(n_mixed, units):
        put_rows(rest[0], unit, (unit - n_mixed) * 2 * part)
    near, far = seen_sides(owners, 2 * side)
    line = lax.broadcasted_iota(jnp.int32, flags.shape, 0)
    flags[...] = jnp.where(line == 0, near.astype(jnp.int32), far.astype(jnp.int32))


def stats_of(rows, tokens):
    rows = rows.astype(F32)
    half = STAT_ROWS // 2
    both = rows[:half, :tokens] + rows[half:, :tokens] + rows[:half, tokens : 2 * tokens]
    group = half // 2
    return stack_stats(both, 0, group), stack_stats(both, group, group)


def stack_heads(load, first, group):
    blocks = []
    for pair in range(group // 2):
        two = load((first + 2 * pair) * HEAD_DIM, 2 * HEAD_DIM)
        blocks += [two[:, :HEAD_DIM], two[:, HEAD_DIM:]]
    return jnp.concatenate(blocks, 0)


def stack_stats(stats, first, group):
    return jnp.concatenate([stats[first + g : first + g + 1] for g in range(group)], 1)


def head_grads(q, do, lse, delta, k, v):
    scores = dot(k, q, 1, 1)
    dprobs = dot(v, do, 1, 1)
    probs = jnp.exp2(scores * (LOG2E / math.sqrt(HEAD_DIM)) - lse)
    dscores = (probs * (dprobs - delta)).astype(BF16)
    dv = dot(probs.astype(BF16), do, 1, 0)
    dk = dot(dscores, q, 1, 0)
    dq = dot(k, dscores, 0, 0)
    return dk, dv, dq


def side_grads(pairs, load_q, load_do, load_stats, kv, put):
    part = kv.shape[1] // 2
    width = 2 * HEAD_DIM
    for pair in pairs:
        at = pair * width
        k_two, v_two = kv[:, at : at + width], kv[:, part + at : part + at + width]
        dks, dvs = [], []
        for odd in range(2):
            first = (2 * pair + odd) * put.group
            lanes = slice(odd * HEAD_DIM, (odd + 1) * HEAD_DIM)
            dk, dv, dq = head_grads(
                stack_heads(load_q, first, put.group),
                stack_heads(load_do, first, put.group),
                *load_stats(first),
                k_two[:, lanes],
                v_two[:, lanes],
            )
            dks.append(dk)
            dvs.append(dv)
            put(first, dq)
        put.store(at, jnp.concatenate(dks, 1), jnp.concatenate(dvs, 1))


class Put:
    def __init__(self, dq_acc, group, store):
        self.dq_acc, self.group, self.store = dq_acc, group, store

    def __call__(self, first, dq):
        tok = self.dq_acc.shape[1]
        for g in range(self.group):
            rows = slice((first + g) * HEAD_DIM, (first + g + 1) * HEAD_DIM)
            self.dq_acc[rows, :] += dq[:, g * tok : (g + 1) * tok]


def turned_dq(dq_acc, first, last):
    factor = 1.0 / math.sqrt(HEAD_DIM)
    blocks = [
        jnp.transpose(dq_acc[at : at + LANES, :])
        for at in range(first * HEAD_DIM, last * HEAD_DIM, LANES)
    ]
    return (jnp.concatenate(blocks, 1) * factor).astype(BF16)


def seen(flags, which):
    return jnp.max(flags[which : which + 1, :]) > 0


def seen_sides(owners, shards):
    rank, z = lax.axis_index("blk"), lax.axis_index("ulysses")
    n_blk = lax.axis_size("blk")
    before = lax.rem(rank + n_blk - 1, n_blk)
    place = lax.div(z, shards // 2)
    mine = owners[2 * rank + place]
    return mine > owners[2 * before + place], mine > owners[2 * before + 1 - place]


def own_rows(flags, which, q, do, stats, kv, acc, dq_acc):
    heads = stats.shape[0] // 2
    half = heads * HEAD_DIM
    part = kv.shape[1] // 2
    mine = parity()

    def from_half(ref):
        def load(at, size):
            return ref[:, pl.ds(pl.multiple_of(mine * half + at, size), size)]

        return load

    def load_stats(first):
        group = part // HEAD_DIM
        every = stats[...]
        return stack_stats(every, first, group), stack_stats(every, heads + first, group)

    def store(at, dk, dv):
        acc[:, at : at + dk.shape[1]] = dk
        acc[:, part + at : part + at + dv.shape[1]] = dv

    @pl.when(seen(flags, which))
    def _():
        pairs = range(part // LANES)
        put = Put(dq_acc, part // HEAD_DIM, store)
        side_grads(pairs, from_half(q), from_half(do), load_stats, kv, put)


def own_far_kernel(side, flags, q, do, stats, *rest):
    slots = rest[:-4]
    kv, q_in, acc, dq_acc = rest[-4:]
    tok, high = q.shape[0], slots[0].shape[0]

    def sort(which):
        keys, rows = apart(which, slots, side)
        for d in range(side):
            kv[d * tok : (d + 1) * tok, :] = keys[d][:tok, :]
        for unit in range(len(rows)):
            q_in[unit * high : (unit + 1) * high, :] = rows[unit][...]

    by_class(sort)
    dq_acc[...] = jnp.zeros_like(dq_acc)
    own_rows(flags, 1, q, do, stats, kv, acc, dq_acc)


def partner_rows(flags, which, pairs, load_q, load_do, load_stats, kv, acc, dq_acc, write):
    part = kv.shape[1] // 2
    factor = 1.0 / math.sqrt(HEAD_DIM)

    @pl.when(seen(flags, which))
    def _():
        def store(at, dk, dv):
            dk = (dk + acc[:, at : at + dk.shape[1]]) * factor
            dv = dv + acc[:, part + at : part + at + dv.shape[1]]
            write(at // LANES, dk.astype(BF16), dv.astype(BF16))

        side_grads(pairs, load_q, load_do, load_stats, kv, Put(dq_acc, part // HEAD_DIM, store))

    @pl.when(jnp.logical_not(seen(flags, which)))
    def _():
        for pair in pairs:
            zero = jnp.zeros((kv.shape[0], LANES), BF16)
            write(pair, zero, zero)


def early_kernel(side, flags, q, do, stats, dq_before, kv_far, q_in, acc_far, *rest):
    slots = rest[:side]
    kv, acc, dq_own, near_done, far_done, dq_done, dq_acc = rest[side:]
    tok, part = q.shape[0], kv.shape[1] // 2
    heads = stats.shape[0] // 2
    for d in range(side):
        kv[d * tok : (d + 1) * tok, :] = slots[d][...]
    dq_acc[...] = dq_before[...]
    own_rows(flags, 0, q, do, stats, kv, acc, dq_acc)
    dq_own[...] = turned_dq(dq_acc, 0, heads)
    high = tok + STAT_ROWS
    n_units = q_in.shape[0] // high
    pairs = range(n_units // 2)
    dq_acc[...] = jnp.zeros_like(dq_acc)

    def loader(offset):
        def load(at, size):
            unit, lane = at // part, offset + at % part
            return q_in[unit * high : unit * high + tok, lane : lane + size]

        return load

    def load_stats(first):
        unit = first * HEAD_DIM // part
        return stats_of(q_in[unit * high + tok : (unit + 1) * high, :], tok)

    for which, keys, total, done in ((0, kv, acc, near_done), (1, kv_far, acc_far, far_done)):

        def write(pair, dk, dv, done=done):
            done[:, 2 * pair * LANES : (2 * pair + 1) * LANES] = dk
            done[:, (2 * pair + 1) * LANES : (2 * pair + 2) * LANES] = dv

        partner_rows(
            flags, which, pairs, loader(0), loader(part), load_stats, keys, total, dq_acc, write
        )
    dq_done[...] = turned_dq(dq_acc, 0, n_units * part // HEAD_DIM)


def late_kernel(side, flags, near_kv, far_kv, near_acc, far_acc, near_done, far_done, dq_done, *rest):
    dq_acc = rest[-1]
    kv_width = near_kv.shape[1]
    part = kv_width // 2
    tok = dq_acc.shape[1]
    units = dq_acc.shape[0] // part
    early = dq_done.shape[1] // part
    rows = None
    if early < units:
        rows, rest = rest[0], rest[1:]
    near, slots = rest[:side], rest[side:-1]
    if rows is not None:
        dq_acc[...] = jnp.zeros_like(dq_acc)

    def loader(offset):
        def load(at, size):
            lane = (at // part - early) * kv_width + offset + at % part
            return rows[:tok, lane : lane + size]

        return load

    def load_stats(first):
        at = (first * HEAD_DIM // part - early) * kv_width
        return stats_of(rows[tok:, at : at + kv_width], tok)

    def send_back(outs, which, keys, total, done):
        def write(pair, dk, dv):
            for m, out in enumerate(outs):
                out[:, pair * LANES : (pair + 1) * LANES] = dk[m * tok : (m + 1) * tok]
                out[:, part + pair * LANES : part + (pair + 1) * LANES] = dv[m * tok : (m + 1) * tok]

        for pair in range(early // 2):
            at = 2 * pair * LANES
            write(pair, done[:, at : at + LANES], done[:, at + LANES : at + 2 * LANES])
        if rows is not None:
            pairs = range(early // 2, units // 2)
            partner_rows(
                flags, which, pairs, loader(0), loader(part), load_stats, keys, total, dq_acc, write
            )

    send_back(near, 0, near_kv, near_acc, near_done)

    def write_slots(which):
        keys, dq = apart(which, slots, side)
        send_back(keys, 1, far_kv, far_acc, far_done)
        columns = [dq_done[...]]
        if rows is not None:
            columns.append(turned_dq(dq_acc, early * part // HEAD_DIM, units * part // HEAD_DIM))
        whole = jnp.concatenate(columns, 1)
        for i, out in enumerate(dq):
            out[...] = whole[:, i * kv_width : (i + 1) * kv_width]

    by_class(write_slots)


def add_up(refs):
    totals = []
    for odd in range(2):
        total = refs[odd][...].astype(F32)
        for m in range(odd + 2, len(refs), 2):
            total = total + refs[m][...].astype(F32)
        totals.append(total)
    return totals


def join_kernel(side, dq_own, *rest):
    near, slots = rest[:side], rest[side:-3]
    gq, gk, gv = rest[-3:]
    half = dq_own.shape[1]
    part = gk.shape[1] // 2

    def write_class(which):
        keys, rows = apart(which, slots, side)
        totals = [a + b for a, b in zip(add_up(near), add_up(keys))]

        def write(mine, other):
            gq[:, mine * half : (mine + 1) * half] = dq_own[...]
            size = half // len(rows)
            for i, ref in enumerate(rows):
                gq[:, other * half + i * size : other * half + (i + 1) * size] = ref[...]
            for total, place in zip(totals, (mine, other)):
                gk[:, place * part : (place + 1) * part] = total[:, :part].astype(BF16)
                gv[:, place * part : (place + 1) * part] = total[:, part:].astype(BF16)

        by_parity(write)

    by_class(write_class)


def limit(mib):
    return pltpu.CompilerParams(vmem_limit_bytes=mib * 1024 * 1024)


def per_device(queries, key_states, value_states, attn_out, grad_out, log_sums, owners):
    n_blk, n_uly = lax.axis_size("blk"), lax.axis_size("ulysses")
    tok, width = queries.shape
    heads = log_sums.shape[1]
    kv_width = key_states.shape[1]
    half = width // 2
    side = n_uly // 2

    n_units = width // kv_width
    n_mixed = min(n_units, side)
    n_back = half // kv_width

    def flips(first, second):
        return [in_turn(which, first, second) for which in range(2)]

    def move(value, *by_kind):
        pairs = []
        for b in range(n_blk):
            for u in range(n_uly):
                step, flip = by_kind[(b + u // side) % len(by_kind)]
                pairs.append((b * n_uly + u, ((b + step) % n_blk) * n_uly + (u ^ flip)))
        return lax.ppermute(value, ("blk", "ulysses"), pairs)

    def shape(*dims, dtype=BF16):
        return jax.ShapeDtypeStruct(dims, dtype)

    def cover(flops):
        return pl.CostEstimate(flops=flops, bytes_accessed=1 << 20, transcendentals=0)

    unit = shape(tok, kv_width)
    sides = shape(side * tok, kv_width)
    sides_wide = shape(side * tok, kv_width, dtype=F32)
    dq_wide = shape(half, tok, dtype=F32)
    whole = n_mixed == n_units
    high = tok + STAT_ROWS
    late = [] if whole else [shape(high, (n_units - n_mixed) * kv_width)]
    outs = [shape(high, kv_width)] * (side + n_mixed) + [unit] * 2 + late
    outs += [shape(heads, tok, dtype=F32), shape(8, LANES, dtype=jnp.int32)]
    packed = pl.pallas_call(
        functools.partial(pack_kernel, side, n_mixed),
        out_shape=outs,
        in_specs=[SMEM] + [VMEM] * 6,
        out_specs=[VMEM] * len(outs),
        scratch_shapes=[pltpu.VMEM((n_units * STAT_ROWS, kv_width), BF16)],
        compiler_params=limit(PACK_MIB),
        name="pack",
    )(owners, queries, grad_out, attn_out, jnp.transpose(log_sums), key_states, value_states)
    slots, (near_same, near_other, *rest, stat_own, flags) = (
        packed[: side + n_mixed],
        packed[side + n_mixed :],
    )
    turns = flips([(1, d) for d in range(side, n_uly)], [(0, 1)] * n_mixed)
    slots = [move(x, one, two) for x, one, two in zip(slots, *turns)]
    near = [move(near_other if d % 2 else near_same, (1, d)) for d in range(side)]
    rest = [move(x, (0, 1)) for x in rest]
    kv_far, q_in, acc_far, dq_part = pl.pallas_call(
        functools.partial(own_far_kernel, side),
        out_shape=[sides, shape(n_mixed * high, kv_width), sides_wide, dq_wide],
        in_specs=[VMEM] * (4 + side + n_mixed),
        out_specs=[VMEM] * 4,
        compiler_params=limit(32),
        cost_estimate=cover(SHORT),
        name="own_far",
    )(flags, queries, grad_out, stat_own, *slots)
    done = shape(side * tok, n_mixed * LANES)
    outs = [sides, sides_wide, shape(tok, half), done, done, shape(tok, n_mixed * kv_width // 2)]
    kv_near, acc_near, dq_own, near_done, far_done, dq_done = pl.pallas_call(
        functools.partial(early_kernel, side),
        out_shape=outs,
        in_specs=[VMEM] * (8 + side),
        out_specs=[VMEM] * len(outs),
        scratch_shapes=[pltpu.VMEM((half, tok), F32)],
        compiler_params=limit(32),
        cost_estimate=cover(SHORT),
        name="early",
    )(flags, queries, grad_out, stat_own, dq_part, kv_far, q_in, acc_far, *near)
    back = pl.pallas_call(
        functools.partial(late_kernel, side),
        out_shape=[unit] * (n_uly + n_back),
        in_specs=[VMEM] * (8 + len(rest)),
        out_specs=[VMEM] * (n_uly + n_back),
        scratch_shapes=[pltpu.VMEM((half, tok), F32)],
        compiler_params=limit(32),
        cost_estimate=cover(SHORT),
        name="late",
    )(flags, kv_near, kv_far, acc_near, acc_far, near_done, far_done, dq_done, *rest)
    near, slots = back[:side], back[side:]
    turns = flips([(-1, d) for d in range(side, n_uly)], [(0, 1)] * n_back)
    slots = [move(x, one, two) for x, one, two in zip(slots, *turns)]
    near = [move(near[d], (-1, d)) for d in reversed(range(side))][::-1]
    return tuple(
        pl.pallas_call(
            functools.partial(join_kernel, side),
            out_shape=[shape(tok, width), shape(tok, kv_width), shape(tok, kv_width)],
            in_specs=[VMEM] * (1 + n_uly + n_back),
            out_specs=[VMEM] * 3,
            compiler_params=limit(8),
            name="join",
        )(dq_own, *near, *slots)
    )


def solution(mesh):
    rows = P(("blk", "ulysses"), None)
    return jax.shard_map(
        per_device,
        mesh=mesh,
        in_specs=(rows, rows, rows, rows, rows, rows, P()),
        out_specs=(rows, rows, rows),
        check_vma=False,
    )
```

```python
import functools
import math

import jax
import jax.numpy as jnp
from jax import lax
from jax.experimental import pallas as pl
from jax.experimental.pallas import tpu as pltpu
from jax.sharding import PartitionSpec as P

HEAD_DIM = 64
LANES = 128
PACK_MIB = 60
OWN, PARTNER = 1 << 31, 1 << 31
LOG2E = math.log2(math.e)
BF16 = jnp.bfloat16
F32 = jnp.float32
ANY = pl.BlockSpec(memory_space=pl.ANY)
VMEM = pl.BlockSpec(memory_space=pltpu.VMEM)
SMEM = pl.BlockSpec(memory_space=pltpu.SMEM)


def dot(a, b, a_dim, b_dim):
    return lax.dot_general(
        a, b, (((a_dim,), (b_dim,)), ((), ())), preferred_element_type=F32
    )


def parity():
    return lax.rem(lax.axis_index("ulysses"), 2)


def by_parity(write):
    for mine in range(2):

        @pl.when(parity() == mine)
        def _():
            write(mine, 1 - mine)


def by_class(write):
    side = lax.div(lax.axis_index("ulysses"), lax.axis_size("ulysses") // 2)
    odd = lax.rem(lax.axis_index("blk") + side, 2)
    for which in range(2):

        @pl.when(odd == which)
        def _():
            write(which)


def in_turn(which, first, second):
    return [*first, *second] if which == 0 else [*second, *first]


def apart(which, refs, n_first):
    n_second = len(refs) - n_first
    if which == 0:
        return refs[:n_first], refs[n_first:]
    return refs[n_second:], refs[:n_second]


def pack_kernel(side, n_mixed, owners, q, do, o, sums, k, v, *refs):
    n_slots = side + n_mixed
    slots, near_same, near_other = refs[:n_slots], refs[n_slots], refs[n_slots + 1]
    rest, stat_own, flags = refs[n_slots + 2 : n_slots + 5]
    q_v, do_v, o_v, sums_v, k_v, v_v = refs[n_slots + 5 : n_slots + 11]
    keys_v, rows_v, rest_v, stat_v, flags_v, in_sems, out_sems = refs[n_slots + 11 :]
    tokens, width = do_v.shape
    heads = sums_v.shape[0]
    half = width // 2
    part = k_v.shape[1] // 2
    n = heads // 2
    units = half // part
    mine = parity()
    other = 1 - mine

    def columns(which, size):
        return pl.ds(pl.multiple_of(which * size, size), size)

    pairs = [(k, k_v), (v, v_v), (do, do_v), (q, q_v), (o, o_v), (sums, sums_v)]
    copies = [pltpu.make_async_copy(a, b, in_sems.at[i]) for i, (a, b) in enumerate(pairs)]
    for copy in copies:
        copy.start()
    started = []

    def send(source, target):
        copy = pltpu.make_async_copy(source, target, out_sems.at[len(started)])
        copy.start()
        started.append(copy)

    def send_by_class(sources, targets):
        first = len(started)

        def start(which):
            for i, (source, target) in enumerate(zip(sources, targets[which])):
                pltpu.make_async_copy(source, target, out_sems.at[first + i]).start()

        by_class(start)
        for i, (source, target) in enumerate(zip(sources, targets[0])):
            started.append(pltpu.make_async_copy(source, target, out_sems.at[first + i]))

    sorted_slots = [apart(which, slots, side) for which in range(2)]
    for copy in copies[:2]:
        copy.wait()
    for i, which in enumerate((mine, other)):
        keys_v[i, :, :part] = k_v[:, columns(which, part)]
        keys_v[i, :, part:] = v_v[:, columns(which, part)]
    sources = [keys_v.at[d % 2] for d in range(side)]
    send_by_class(sources, [keys for keys, _ in sorted_slots])
    for copy in copies[2:4]:
        copy.wait()
    for unit in range(units):
        at = pl.ds(pl.multiple_of(other * half + unit * part, part), part)
        out, start = (rows_v.at[unit], 0) if unit < n_mixed else (rest_v, (unit - n_mixed) * 2 * part)
        out[:, start : start + part] = q_v[:, at]
        out[:, start + part : start + 2 * part] = do_v[:, at]
    sources = [rows_v.at[unit] for unit in range(n_mixed)]
    send_by_class(sources, [rows for _, rows in sorted_slots])

    row = lax.broadcasted_iota(jnp.int32, (heads, width), 0)
    col = lax.broadcasted_iota(jnp.int32, (heads, width), 1)
    pick = jnp.where(col // HEAD_DIM == row, 1.0, 0.0).astype(BF16)
    for copy in copies[4:]:
        copy.wait()
    prod = do_v[...].astype(F32) * o_v[...].astype(F32)
    high = prod.astype(BF16)
    low = (prod - high.astype(F32)).astype(BF16)
    delta = dot(pick, high, 1, 1) + dot(pick, low, 1, 1)
    lse = sums_v[...] * LOG2E

    def write_stats(mine, other):
        stat_v[:n, :] = lse[mine * n : (mine + 1) * n, :]
        stat_v[n:, :] = delta[mine * n : (mine + 1) * n, :]
        left = jnp.concatenate([x[other * n : (other + 1) * n, :] for x in (lse, delta)], 0)
        terms = []
        for _ in range(3):
            term = left.astype(BF16).astype(F32)
            left = left - term
            terms.append(term)
        terms.append(jnp.zeros((LANES - 6 * n, tokens), F32))
        at = rest_v.shape[1] - LANES
        rest_v[:, at:] = jnp.transpose(jnp.concatenate(terms, 0)).astype(BF16)

    by_parity(write_stats)
    send(rest_v, rest)
    send(stat_v, stat_own)
    near, far = seen_sides(owners, 2 * side)
    line = lax.broadcasted_iota(jnp.int32, flags_v.shape, 0)
    flags_v[...] = jnp.where(line == 0, near.astype(jnp.int32), far.astype(jnp.int32))
    send(flags_v, flags)
    send(keys_v.at[0], near_same)
    send(keys_v.at[1], near_other)
    for copy in started:
        copy.wait()


def stack_heads(load, first, group):
    blocks = []
    for pair in range(group // 2):
        two = load((first + 2 * pair) * HEAD_DIM, 2 * HEAD_DIM)
        blocks += [two[:, :HEAD_DIM], two[:, HEAD_DIM:]]
    return jnp.concatenate(blocks, 0)


def stack_stats(stats, first, group):
    return jnp.concatenate([stats[first + g : first + g + 1] for g in range(group)], 1)


def head_grads(q, do, lse, delta, k, v):
    scores = dot(k, q, 1, 1)
    dprobs = dot(v, do, 1, 1)
    probs = jnp.exp2(scores * (LOG2E / math.sqrt(HEAD_DIM)) - lse)
    dscores = (probs * (dprobs - delta)).astype(BF16)
    dv = dot(probs.astype(BF16), do, 1, 0)
    dk = dot(dscores, q, 1, 0)
    dq = dot(k, dscores, 0, 0)
    return dk, dv, dq


def side_grads(pairs, load_q, load_do, load_stats, kv, put):
    part = kv.shape[1] // 2
    width = 2 * HEAD_DIM
    for pair in pairs:
        at = pair * width
        k_two, v_two = kv[:, at : at + width], kv[:, part + at : part + at + width]
        dks, dvs = [], []
        for odd in range(2):
            first = (2 * pair + odd) * put.group
            lanes = slice(odd * HEAD_DIM, (odd + 1) * HEAD_DIM)
            dk, dv, dq = head_grads(
                stack_heads(load_q, first, put.group),
                stack_heads(load_do, first, put.group),
                *load_stats(first),
                k_two[:, lanes],
                v_two[:, lanes],
            )
            dks.append(dk)
            dvs.append(dv)
            put(first, dq)
        put.store(at, jnp.concatenate(dks, 1), jnp.concatenate(dvs, 1))


class Put:
    def __init__(self, dq_acc, group, store):
        self.dq_acc, self.group, self.store = dq_acc, group, store

    def __call__(self, first, dq):
        tok = self.dq_acc.shape[1]
        for g in range(self.group):
            rows = slice((first + g) * HEAD_DIM, (first + g + 1) * HEAD_DIM)
            self.dq_acc[rows, :] += dq[:, g * tok : (g + 1) * tok]


def turned_dq(dq_acc, first, last):
    factor = 1.0 / math.sqrt(HEAD_DIM)
    blocks = [
        jnp.transpose(dq_acc[at : at + LANES, :])
        for at in range(first * HEAD_DIM, last * HEAD_DIM, LANES)
    ]
    return (jnp.concatenate(blocks, 1) * factor).astype(BF16)


def seen(flags, which):
    return jnp.max(flags[which : which + 1, :]) > 0


def seen_sides(owners, shards):
    rank, z = lax.axis_index("blk"), lax.axis_index("ulysses")
    n_blk = lax.axis_size("blk")
    before = lax.rem(rank + n_blk - 1, n_blk)
    place = lax.div(z, shards // 2)
    mine = owners[2 * rank + place]
    return mine > owners[2 * before + place], mine > owners[2 * before + 1 - place]


def own_loaders(q, do, stats, group):
    heads = stats.shape[0] // 2
    half = heads * HEAD_DIM
    mine = parity()

    def from_half(ref):
        def load(at, size):
            return ref[:, pl.ds(pl.multiple_of(mine * half + at, size), size)]

        return load

    def load_stats(first):
        every = stats[...]
        return stack_stats(every, first, group), stack_stats(every, heads + first, group)

    return from_half(q), from_half(do), load_stats


def partner_loaders(q_in, rest, part, heads):
    tok, kv_width = rest.shape[0], 2 * part
    n_mixed = q_in.shape[0] // tok

    def loader(offset):
        def load(at, size):
            unit, lane = at // part, offset + at % part
            if unit < n_mixed:
                return q_in[unit * tok : (unit + 1) * tok, lane : lane + size]
            lane += (unit - n_mixed) * kv_width
            return rest[:, lane : lane + size]

        return load

    def load_stats(first):
        terms = jnp.transpose(rest[:, rest.shape[1] - LANES :].astype(F32))
        n = 2 * heads
        every = terms[:n] + terms[n : 2 * n] + terms[2 * n : 3 * n]
        group = part // HEAD_DIM
        return stack_stats(every, first, group), stack_stats(every, heads + first, group)

    return loader(0), loader(part), load_stats


def own_far_kernel(side, flags, q, do, stats, *rest):
    slots = rest[:-4]
    kv, q_in, acc, dq_acc = rest[-4:]
    tok, part = q.shape[0], kv.shape[1] // 2

    def sort(which):
        keys, rows = apart(which, slots, side)
        for d in range(side):
            kv[d * tok : (d + 1) * tok, :] = keys[d][...]
        for unit in range(len(rows)):
            q_in[unit * tok : (unit + 1) * tok, :] = rows[unit][...]

    by_class(sort)
    dq_acc[...] = jnp.zeros_like(dq_acc)

    def store(at, dk, dv):
        acc[:, at : at + LANES] = dk
        acc[:, part + at : part + at + LANES] = dv

    @pl.when(seen(flags, 1))
    def _():
        group = part // HEAD_DIM
        loaders = own_loaders(q, do, stats, group)
        side_grads(range(part // LANES), *loaders, kv, Put(dq_acc, group, store))


def partner_far_kernel(flags, q_in, rest, kv, acc, done, dq_acc):
    part = kv.shape[1] // 2
    factor = 1.0 / math.sqrt(HEAD_DIM)
    dq_acc[...] = jnp.zeros_like(dq_acc)

    def store(at, dk, dv):
        dk = (dk + acc[:, at : at + LANES]) * factor
        dv = dv + acc[:, part + at : part + at + LANES]
        done[:, at : at + LANES] = dk.astype(BF16)
        done[:, part + at : part + at + LANES] = dv.astype(BF16)

    @pl.when(seen(flags, 1))
    def _():
        loaders = partner_loaders(q_in, rest, part, dq_acc.shape[0] // HEAD_DIM)
        side_grads(range(part // LANES), *loaders, kv, Put(dq_acc, part // HEAD_DIM, store))

    @pl.when(jnp.logical_not(seen(flags, 1)))
    def _():
        done[...] = jnp.zeros_like(done)


def near_kernel(side, flags, q, do, stats, q_in, rest, far_done, own_dq, partner_dq, *refs):
    keys, dq_own, near = refs[:side], refs[side], refs[side + 1 : 2 * side + 1]
    slots = refs[2 * side + 1 : -4]
    kv, acc, own_acc, partner_acc = refs[-4:]
    tok, part = q.shape[0], kv.shape[1] // 2
    heads = own_acc.shape[0] // HEAD_DIM
    group = part // HEAD_DIM
    pairs = range(part // LANES)
    factor = 1.0 / math.sqrt(HEAD_DIM)
    own_acc[...] = own_dq[...]
    partner_acc[...] = partner_dq[...]

    @pl.when(seen(flags, 0))
    def _():
        for d in range(side):
            kv[d * tok : (d + 1) * tok, :] = keys[d][...]

        def keep(at, dk, dv):
            acc[:, at : at + LANES] = dk
            acc[:, part + at : part + at + LANES] = dv

        def finish(at, dk, dv):
            dk = ((dk + acc[:, at : at + LANES]) * factor).astype(BF16)
            dv = (dv + acc[:, part + at : part + at + LANES]).astype(BF16)
            for d in range(side):
                near[d][:, at : at + LANES] = dk[d * tok : (d + 1) * tok]
                near[d][:, part + at : part + at + LANES] = dv[d * tok : (d + 1) * tok]

        side_grads(pairs, *own_loaders(q, do, stats, group), kv, Put(own_acc, group, keep))
        loaders = partner_loaders(q_in, rest, part, heads)
        side_grads(pairs, *loaders, kv, Put(partner_acc, group, finish))

    @pl.when(jnp.logical_not(seen(flags, 0)))
    def _():
        for out in near:
            out[...] = jnp.zeros_like(out)

    dq_own[...] = turned_dq(own_acc, 0, heads)

    def write(which):
        far, rows = apart(which, slots, side)
        for d in range(side):
            far[d][...] = far_done[d * tok : (d + 1) * tok, :]
        each = heads // len(rows)
        for i, out in enumerate(rows):
            out[...] = turned_dq(partner_acc, i * each, (i + 1) * each)

    by_class(write)


def add_up(refs):
    totals = []
    for odd in range(2):
        total = refs[odd][...].astype(F32)
        for m in range(odd + 2, len(refs), 2):
            total = total + refs[m][...].astype(F32)
        totals.append(total)
    return totals


def join_kernel(side, dq_own, *rest):
    near, slots = rest[:side], rest[side:-3]
    gq, gk, gv = rest[-3:]
    half = dq_own.shape[1]
    part = gk.shape[1] // 2

    def write_class(which):
        keys, rows = apart(which, slots, side)
        totals = [a + b for a, b in zip(add_up(near), add_up(keys))]

        def write(mine, other):
            gq[:, mine * half : (mine + 1) * half] = dq_own[...]
            size = half // len(rows)
            for i, ref in enumerate(rows):
                gq[:, other * half + i * size : other * half + (i + 1) * size] = ref[...]
            for total, place in zip(totals, (mine, other)):
                gk[:, place * part : (place + 1) * part] = total[:, :part].astype(BF16)
                gv[:, place * part : (place + 1) * part] = total[:, part:].astype(BF16)

        by_parity(write)

    by_class(write_class)


def limit(mib):
    return pltpu.CompilerParams(vmem_limit_bytes=mib * 1024 * 1024)


def per_device(queries, key_states, value_states, attn_out, grad_out, log_sums, owners):
    n_blk, n_uly = lax.axis_size("blk"), lax.axis_size("ulysses")
    tok, width = queries.shape
    heads = log_sums.shape[1]
    kv_width = key_states.shape[1]
    half = width // 2
    side = n_uly // 2

    n_units = width // kv_width
    n_mixed = min(n_units, side)
    n_back = half // kv_width

    def flips(first, second):
        return [in_turn(which, first, second) for which in range(2)]

    def move(value, *by_kind):
        pairs = []
        for b in range(n_blk):
            for u in range(n_uly):
                step, flip = by_kind[(b + u // side) % len(by_kind)]
                pairs.append((b * n_uly + u, ((b + step) % n_blk) * n_uly + (u ^ flip)))
        return lax.ppermute(value, ("blk", "ulysses"), pairs)

    def shape(*dims, dtype=BF16):
        return jax.ShapeDtypeStruct(dims, dtype)

    def cover(flops):
        return pl.CostEstimate(flops=flops, bytes_accessed=1 << 20, transcendentals=0)

    unit = shape(tok, kv_width)
    sides = shape(side * tok, kv_width)
    sides_wide = shape(side * tok, kv_width, dtype=F32)
    dq_wide = shape(half, tok, dtype=F32)
    rest = shape(tok, (n_units - n_mixed) * kv_width + LANES)
    stats, seen_flags = shape(heads, tok, dtype=F32), shape(8, LANES, dtype=jnp.int32)
    outs = [unit] * (side + n_mixed + 2) + [rest, stats, seen_flags]

    def room(like):
        return pltpu.VMEM(like.shape, like.dtype)

    *slots, near_same, near_other, rest, stat_own, flags = pl.pallas_call(
        functools.partial(pack_kernel, side, n_mixed),
        out_shape=outs,
        in_specs=[SMEM] + [ANY] * 6,
        out_specs=[ANY] * len(outs),
        scratch_shapes=[
            room(queries),
            room(grad_out),
            room(attn_out),
            pltpu.VMEM((heads, tok), F32),
            room(key_states),
            room(value_states),
            pltpu.VMEM((2, tok, kv_width), BF16),
            pltpu.VMEM((n_mixed, tok, kv_width), BF16),
            room(rest),
            room(stats),
            room(seen_flags),
            pltpu.SemaphoreType.DMA((6,)),
            pltpu.SemaphoreType.DMA((len(outs),)),
        ],
        compiler_params=limit(PACK_MIB),
        name="pack",
    )(owners, queries, grad_out, attn_out, jnp.transpose(log_sums), key_states, value_states)
    turns = flips([(1, d) for d in range(side, n_uly)], [(0, 1)] * n_mixed)
    slots = [move(x, one, two) for x, one, two in zip(slots, *turns)]
    rest = move(rest, (0, 1))
    near = [move(near_other if d % 2 else near_same, (1, d)) for d in range(side)]
    kv_far, q_in, acc_far, own_dq = pl.pallas_call(
        functools.partial(own_far_kernel, side),
        out_shape=[sides, shape(n_mixed * tok, kv_width), sides_wide, dq_wide],
        in_specs=[VMEM] * (4 + side + n_mixed),
        out_specs=[VMEM] * 4,
        compiler_params=limit(32),
        cost_estimate=cover(OWN),
        name="own_far",
    )(flags, queries, grad_out, stat_own, *slots)
    far_done, partner_dq = pl.pallas_call(
        partner_far_kernel,
        out_shape=[sides, dq_wide],
        in_specs=[VMEM] * 5,
        out_specs=[VMEM] * 2,
        compiler_params=limit(32),
        cost_estimate=cover(PARTNER),
        name="far",
    )(flags, q_in, rest, kv_far, acc_far)
    outs = [shape(tok, half)] + [unit] * (n_uly + n_back)
    dq_own, *back = pl.pallas_call(
        functools.partial(near_kernel, side),
        out_shape=outs,
        in_specs=[VMEM] * (9 + side),
        out_specs=[VMEM] * len(outs),
        scratch_shapes=[room(sides), room(sides_wide), room(dq_wide), room(dq_wide)],
        compiler_params=limit(32),
        cost_estimate=cover(PARTNER),
        name="near",
    )(flags, queries, grad_out, stat_own, q_in, rest, far_done, own_dq, partner_dq, *near)
    near, slots = back[:side], back[side:]
    turns = flips([(-1, d) for d in range(side, n_uly)], [(0, 1)] * n_back)
    slots = [move(x, one, two) for x, one, two in zip(slots, *turns)]
    near = [move(near[d], (-1, d)) for d in reversed(range(side))][::-1]
    return tuple(
        pl.pallas_call(
            functools.partial(join_kernel, side),
            out_shape=[shape(tok, width), shape(tok, kv_width), shape(tok, kv_width)],
            in_specs=[VMEM] * (1 + n_uly + n_back),
            out_specs=[VMEM] * 3,
            compiler_params=limit(8),
            name="join",
        )(dq_own, *near, *slots)
    )


def solution(mesh):
    rows = P(("blk", "ulysses"), None)
    return jax.shard_map(
        per_device,
        mesh=mesh,
        in_specs=(rows, rows, rows, rows, rows, rows, P()),
        out_specs=(rows, rows, rows),
        check_vma=False,
    )
```

```python
import functools
import math

import jax
import jax.numpy as jnp
from jax import lax
from jax.experimental import pallas as pl
from jax.experimental.pallas import tpu as pltpu
from jax.sharding import PartitionSpec as P

HEAD_DIM = 64
LANES = 128
PACK_MIB = 60
LONG, OWN, PARTNER = 1 << 34, 1 << 31, 1 << 31
LOG2E = math.log2(math.e)
BF16 = jnp.bfloat16
F32 = jnp.float32
ANY = pl.BlockSpec(memory_space=pl.ANY)
VMEM = pl.BlockSpec(memory_space=pltpu.VMEM)
SMEM = pl.BlockSpec(memory_space=pltpu.SMEM)


def dot(a, b, a_dim, b_dim):
    return lax.dot_general(
        a, b, (((a_dim,), (b_dim,)), ((), ())), preferred_element_type=F32
    )


def parity():
    return lax.rem(lax.axis_index("ulysses"), 2)


def by_parity(write):
    for mine in range(2):

        @pl.when(parity() == mine)
        def _():
            write(mine, 1 - mine)


def by_class(write):
    side = lax.div(lax.axis_index("ulysses"), lax.axis_size("ulysses") // 2)
    odd = lax.rem(lax.axis_index("blk") + side, 2)
    for which in range(2):

        @pl.when(odd == which)
        def _():
            write(which)


def in_turn(which, first, second):
    return [*first, *second] if which == 0 else [*second, *first]


def apart(which, refs, n_first):
    n_second = len(refs) - n_first
    if which == 0:
        return refs[:n_first], refs[n_first:]
    return refs[n_second:], refs[:n_second]


def pack_kernel(side, owners, q, do, o, sums, k, v, *outs):
    near_same, near_other, rest, stat_own, flags = outs[-5:]
    slots = outs[:-5]
    tokens, width = do.shape
    heads = sums.shape[0]
    half = width // 2
    part = k.shape[1] // 2
    n = heads // 2
    mine = parity()
    other = 1 - mine

    def cut(ref, which, size, at=0, wide=None):
        wide = size if wide is None else wide
        return ref[:, pl.ds(pl.multiple_of(which * size + at, wide), wide)]

    def put_keys(out, which):
        out[:, :part] = cut(k, which, part)
        out[:, part:] = cut(v, which, part)

    def put_rows(out, unit, at=0):
        out[:, at : at + part] = cut(q, other, half, unit * part, part)
        out[:, at + part : at + 2 * part] = cut(do, other, half, unit * part, part)

    n_mixed = len(slots) - side
    units = half // part

    def write(which):
        keys, rows = apart(which, slots, side)
        for d in range(side):
            put_keys(keys[d], mine if d % 2 == 0 else other)
        for unit in range(n_mixed):
            put_rows(rows[unit], unit)

    by_class(write)
    put_keys(near_same, mine)
    put_keys(near_other, other)
    for unit in range(n_mixed, units):
        put_rows(rest, unit, (unit - n_mixed) * 2 * part)

    row = lax.broadcasted_iota(jnp.int32, (heads, width), 0)
    col = lax.broadcasted_iota(jnp.int32, (heads, width), 1)
    pick = jnp.where(col // HEAD_DIM == row, 1.0, 0.0).astype(BF16)
    prod = do[...].astype(F32) * o[...].astype(F32)
    high = prod.astype(BF16)
    low = (prod - high.astype(F32)).astype(BF16)
    delta = dot(pick, high, 1, 1) + dot(pick, low, 1, 1)
    lse = sums[...] * LOG2E

    def write_stats(mine, other):
        stat_own[:n, :] = lse[mine * n : (mine + 1) * n, :]
        stat_own[n:, :] = delta[mine * n : (mine + 1) * n, :]
        left = jnp.concatenate([x[other * n : (other + 1) * n, :] for x in (lse, delta)], 0)
        terms = []
        for _ in range(3):
            term = left.astype(BF16).astype(F32)
            left = left - term
            terms.append(term)
        terms.append(jnp.zeros((LANES - 6 * n, tokens), F32))
        rest[:, rest.shape[1] - LANES :] = jnp.transpose(jnp.concatenate(terms, 0)).astype(BF16)

    by_parity(write_stats)
    near, far = seen_sides(owners, 2 * side)
    line = lax.broadcasted_iota(jnp.int32, flags.shape, 0)
    flags[...] = jnp.where(line == 0, near.astype(jnp.int32), far.astype(jnp.int32))


def stack_heads(load, first, group):
    blocks = []
    for pair in range(group // 2):
        two = load((first + 2 * pair) * HEAD_DIM, 2 * HEAD_DIM)
        blocks += [two[:, :HEAD_DIM], two[:, HEAD_DIM:]]
    return jnp.concatenate(blocks, 0)


def stack_stats(stats, first, group):
    return jnp.concatenate([stats[first + g : first + g + 1] for g in range(group)], 1)


def head_grads(q, do, lse, delta, k, v):
    scores = dot(k, q, 1, 1)
    dprobs = dot(v, do, 1, 1)
    probs = jnp.exp2(scores * (LOG2E / math.sqrt(HEAD_DIM)) - lse)
    dscores = (probs * (dprobs - delta)).astype(BF16)
    dv = dot(probs.astype(BF16), do, 1, 0)
    dk = dot(dscores, q, 1, 0)
    dq = dot(k, dscores, 0, 0)
    return dk, dv, dq


def side_grads(pairs, load_q, load_do, load_stats, kv, put):
    part = kv.shape[1] // 2
    width = 2 * HEAD_DIM
    for pair in pairs:
        at = pair * width
        k_two, v_two = kv[:, at : at + width], kv[:, part + at : part + at + width]
        dks, dvs = [], []
        for odd in range(2):
            first = (2 * pair + odd) * put.group
            lanes = slice(odd * HEAD_DIM, (odd + 1) * HEAD_DIM)
            dk, dv, dq = head_grads(
                stack_heads(load_q, first, put.group),
                stack_heads(load_do, first, put.group),
                *load_stats(first),
                k_two[:, lanes],
                v_two[:, lanes],
            )
            dks.append(dk)
            dvs.append(dv)
            put(first, dq)
        put.store(at, jnp.concatenate(dks, 1), jnp.concatenate(dvs, 1))


class Put:
    def __init__(self, dq_acc, group, store):
        self.dq_acc, self.group, self.store = dq_acc, group, store

    def __call__(self, first, dq):
        tok = self.dq_acc.shape[1]
        for g in range(self.group):
            rows = slice((first + g) * HEAD_DIM, (first + g + 1) * HEAD_DIM)
            self.dq_acc[rows, :] += dq[:, g * tok : (g + 1) * tok]


def turned_dq(dq_acc, first, last):
    factor = 1.0 / math.sqrt(HEAD_DIM)
    blocks = [
        jnp.transpose(dq_acc[at : at + LANES, :])
        for at in range(first * HEAD_DIM, last * HEAD_DIM, LANES)
    ]
    return (jnp.concatenate(blocks, 1) * factor).astype(BF16)


def seen(flags, which):
    return jnp.max(flags[which : which + 1, :]) > 0


def seen_sides(owners, shards):
    rank, z = lax.axis_index("blk"), lax.axis_index("ulysses")
    n_blk = lax.axis_size("blk")
    before = lax.rem(rank + n_blk - 1, n_blk)
    place = lax.div(z, shards // 2)
    mine = owners[2 * rank + place]
    return mine > owners[2 * before + place], mine > owners[2 * before + 1 - place]


def own_loaders(q, do, stats, group):
    heads = stats.shape[0] // 2
    half = heads * HEAD_DIM
    mine = parity()

    def from_half(ref):
        def load(at, size):
            return ref[:, pl.ds(pl.multiple_of(mine * half + at, size), size)]

        return load

    def load_stats(first):
        every = stats[...]
        return stack_stats(every, first, group), stack_stats(every, heads + first, group)

    return from_half(q), from_half(do), load_stats


def partner_loaders(q_in, rest, part, heads):
    tok, kv_width = rest.shape[0], 2 * part
    n_mixed = q_in.shape[0] // tok

    def loader(offset):
        def load(at, size):
            unit, lane = at // part, offset + at % part
            if unit < n_mixed:
                return q_in[unit * tok : (unit + 1) * tok, lane : lane + size]
            lane += (unit - n_mixed) * kv_width
            return rest[:, lane : lane + size]

        return load

    def load_stats(first):
        terms = jnp.transpose(rest[:, rest.shape[1] - LANES :].astype(F32))
        n = 2 * heads
        every = terms[:n] + terms[n : 2 * n] + terms[2 * n : 3 * n]
        group = part // HEAD_DIM
        return stack_stats(every, first, group), stack_stats(every, heads + first, group)

    return loader(0), loader(part), load_stats


def finish(outs, acc, at, dk, dv):
    part, tok = acc.shape[1] // 2, outs[0].shape[0]
    dk = (dk + acc[:, at : at + LANES]) * (1.0 / math.sqrt(HEAD_DIM))
    dv = dv + acc[:, part + at : part + at + LANES]
    for d, out in enumerate(outs):
        rows = slice(d * tok, (d + 1) * tok)
        out[:, at : at + LANES] = dk[rows].astype(BF16)
        out[:, part + at : part + at + LANES] = dv[rows].astype(BF16)


def own_far_kernel(side, flags, q, do, stats, *rest):
    slots = rest[:-4]
    kv, q_in, acc, dq_acc = rest[-4:]
    tok, part = q.shape[0], kv.shape[1] // 2

    def sort(which):
        keys, rows = apart(which, slots, side)
        for d in range(side):
            kv[d * tok : (d + 1) * tok, :] = keys[d][...]
        for unit in range(len(rows)):
            q_in[unit * tok : (unit + 1) * tok, :] = rows[unit][...]

    by_class(sort)
    dq_acc[...] = jnp.zeros_like(dq_acc)

    def store(at, dk, dv):
        acc[:, at : at + LANES] = dk
        acc[:, part + at : part + at + LANES] = dv

    @pl.when(seen(flags, 1))
    def _():
        group = part // HEAD_DIM
        loaders = own_loaders(q, do, stats, group)
        side_grads(range(part // LANES), *loaders, kv, Put(dq_acc, group, store))


def partner_far_kernel(flags, q_in, rest, kv, acc, *outs):
    far, dq_acc = outs[:-1], outs[-1]
    tok, part = rest.shape[0], kv.shape[1] // 2
    dq_acc[...] = jnp.zeros_like(dq_acc)

    def store(at, dk, dv):
        finish(far, acc, at, dk, dv)

    @pl.when(seen(flags, 1))
    def _():
        loaders = partner_loaders(q_in, rest, part, dq_acc.shape[0] // HEAD_DIM)
        side_grads(range(part // LANES), *loaders, kv, Put(dq_acc, part // HEAD_DIM, store))

    @pl.when(jnp.logical_not(seen(flags, 1)))
    def _():
        for out in far:
            out[...] = jnp.zeros_like(out)


def near_kernel(side, flags, q, do, stats, q_in, rest, own_dq, partner_dq, *refs):
    keys, near = refs[:side], refs[side : 2 * side]
    dq_own, dq_send, kv, acc, own_acc, partner_acc = refs[2 * side :]
    tok, part = q.shape[0], kv.shape[1] // 2
    heads = own_acc.shape[0] // HEAD_DIM
    group = part // HEAD_DIM
    pairs = range(part // LANES)
    own_acc[...] = own_dq[...]
    partner_acc[...] = partner_dq[...]

    @pl.when(seen(flags, 0))
    def _():
        for d in range(side):
            kv[d * tok : (d + 1) * tok, :] = keys[d][...]

        def keep(at, dk, dv):
            acc[:, at : at + LANES] = dk
            acc[:, part + at : part + at + LANES] = dv

        def store(at, dk, dv):
            finish(near, acc, at, dk, dv)

        side_grads(pairs, *own_loaders(q, do, stats, group), kv, Put(own_acc, group, keep))
        loaders = partner_loaders(q_in, rest, part, heads)
        side_grads(pairs, *loaders, kv, Put(partner_acc, group, store))

    @pl.when(jnp.logical_not(seen(flags, 0)))
    def _():
        for out in near:
            out[...] = jnp.zeros_like(out)

    dq_send[...] = turned_dq(partner_acc, 0, heads)
    dq_own[...] = turned_dq(own_acc, 0, heads)


def add_up(refs):
    totals = []
    for odd in range(2):
        total = refs[odd][...].astype(F32)
        for m in range(odd + 2, len(refs), 2):
            total = total + refs[m][...].astype(F32)
        totals.append(total)
    return totals


def join_far_kernel(*refs):
    for out, total in zip(refs[-2:], add_up(refs[:-2])):
        out[...] = total


def join_kernel(dq_own, dq_back, far_same, far_other, *rest):
    near = rest[:-3]
    gq, gk, gv = rest[-3:]
    half = dq_own.shape[1]
    part = gk.shape[1] // 2
    totals = [a[...] + b for a, b in zip((far_same, far_other), add_up(near))]

    def write(mine, other):
        gq[:, mine * half : (mine + 1) * half] = dq_own[...]
        gq[:, other * half : (other + 1) * half] = dq_back[...]
        for total, place in zip(totals, (mine, other)):
            gk[:, place * part : (place + 1) * part] = total[:, :part].astype(BF16)
            gv[:, place * part : (place + 1) * part] = total[:, part:].astype(BF16)

    by_parity(write)


def limit(mib):
    return pltpu.CompilerParams(vmem_limit_bytes=mib * 1024 * 1024)


def per_device(queries, key_states, value_states, attn_out, grad_out, log_sums, owners):
    n_blk, n_uly = lax.axis_size("blk"), lax.axis_size("ulysses")
    tok, width = queries.shape
    heads = log_sums.shape[1]
    kv_width = key_states.shape[1]
    half = width // 2
    side = n_uly // 2

    n_units = width // kv_width
    n_mixed = min(n_units, side)

    def flips(first, second):
        return [in_turn(which, first, second) for which in range(2)]

    def move(value, *by_kind):
        pairs = []
        for b in range(n_blk):
            for u in range(n_uly):
                step, flip = by_kind[(b + u // side) % len(by_kind)]
                pairs.append((b * n_uly + u, ((b + step) % n_blk) * n_uly + (u ^ flip)))
        return lax.ppermute(value, ("blk", "ulysses"), pairs)

    def shape(*dims, dtype=BF16):
        return jax.ShapeDtypeStruct(dims, dtype)

    def cover(flops):
        return pl.CostEstimate(flops=flops, bytes_accessed=1 << 20, transcendentals=0)

    unit = shape(tok, kv_width)
    sides = shape(side * tok, kv_width)
    sides_wide = shape(side * tok, kv_width, dtype=F32)
    dq_wide = shape(half, tok, dtype=F32)
    outs = [unit] * (side + n_mixed + 2) + [
        shape(tok, (n_units - n_mixed) * kv_width + LANES),
        shape(heads, tok, dtype=F32),
        shape(8, LANES, dtype=jnp.int32),
    ]
    *slots, near_same, near_other, rest, stat_own, flags = pl.pallas_call(
        functools.partial(pack_kernel, side),
        out_shape=outs,
        in_specs=[SMEM] + [VMEM] * 6,
        out_specs=[VMEM] * len(outs),
        compiler_params=limit(PACK_MIB),
        name="pack",
    )(owners, queries, grad_out, attn_out, jnp.transpose(log_sums), key_states, value_states)
    turns = flips([(1, d) for d in range(side, n_uly)], [(0, 1)] * n_mixed)
    slots = [move(x, one, two) for x, one, two in zip(slots, *turns)]
    rest = move(rest, (0, 1))
    near = [move(near_other if d % 2 else near_same, (1, d)) for d in range(side)]
    kv_far, q_in, acc_far, own_dq = pl.pallas_call(
        functools.partial(own_far_kernel, side),
        out_shape=[sides, shape(n_mixed * tok, kv_width), sides_wide, dq_wide],
        in_specs=[VMEM] * (4 + side + n_mixed),
        out_specs=[VMEM] * 4,
        compiler_params=limit(32),
        cost_estimate=cover(OWN),
        name="own_far",
    )(flags, queries, grad_out, stat_own, *slots)
    *far, partner_dq = pl.pallas_call(
        partner_far_kernel,
        out_shape=[unit] * side + [dq_wide],
        in_specs=[VMEM] * 5,
        out_specs=[VMEM] * (side + 1),
        compiler_params=limit(32),
        cost_estimate=cover(PARTNER),
        name="far",
    )(flags, q_in, rest, kv_far, acc_far)
    far = [move(x, (-1, side + d)) for d, x in enumerate(far)]
    scratch = [sides, sides_wide, dq_wide, dq_wide]
    *back, dq_own, dq_send = pl.pallas_call(
        functools.partial(near_kernel, side),
        out_shape=[unit] * side + [shape(tok, half)] * 2,
        in_specs=[VMEM] * (8 + side),
        out_specs=[VMEM] * (side + 2),
        scratch_shapes=[pltpu.VMEM(x.shape, x.dtype) for x in scratch],
        compiler_params=limit(32),
        cost_estimate=cover(PARTNER),
        name="near",
    )(flags, queries, grad_out, stat_own, q_in, rest, own_dq, partner_dq, *near)
    dq_back = move(dq_send, (0, 1))
    near = [move(back[d], (-1, d)) for d in reversed(range(side))][::-1]
    far = pl.pallas_call(
        join_far_kernel,
        out_shape=[shape(tok, kv_width, dtype=F32)] * 2,
        in_specs=[VMEM] * side,
        out_specs=[VMEM] * 2,
        compiler_params=limit(8),
        cost_estimate=cover(LONG),
        name="join_far",
    )(*far)
    return tuple(
        pl.pallas_call(
            join_kernel,
            out_shape=[shape(tok, width), shape(tok, kv_width), shape(tok, kv_width)],
            in_specs=[VMEM] * (4 + side),
            out_specs=[VMEM] * 3,
            compiler_params=limit(8),
            name="join",
        )(dq_own, dq_back, *far, *near)
    )


def solution(mesh):
    rows = P(("blk", "ulysses"), None)
    return jax.shard_map(
        per_device,
        mesh=mesh,
        in_specs=(rows, rows, rows, rows, rows, rows, P()),
        out_specs=(rows, rows, rows),
        check_vma=False,
    )
```

```python
import functools
import math

import jax
import jax.numpy as jnp
from jax import lax
from jax.experimental import pallas as pl
from jax.experimental.pallas import tpu as pltpu
from jax.sharding import PartitionSpec as P

HEAD_DIM = 64
LANES = 128
PACK_MIB = 60
TURNS_MIB = 53.4
LONG, OWN, PARTNER = 1 << 34, 1 << 31, 1 << 31
LOG2E = math.log2(math.e)
BF16 = jnp.bfloat16
F32 = jnp.float32
ANY = pl.BlockSpec(memory_space=pl.ANY)
VMEM = pl.BlockSpec(memory_space=pltpu.VMEM)
SMEM = pl.BlockSpec(memory_space=pltpu.SMEM)


def dot(a, b, a_dim, b_dim):
    return lax.dot_general(
        a, b, (((a_dim,), (b_dim,)), ((), ())), preferred_element_type=F32
    )


def parity():
    return lax.rem(lax.axis_index("ulysses"), 2)


def by_parity(write):
    for mine in range(2):

        @pl.when(parity() == mine)
        def _():
            write(mine, 1 - mine)


def by_class(write):
    side = lax.div(lax.axis_index("ulysses"), lax.axis_size("ulysses") // 2)
    odd = lax.rem(lax.axis_index("blk") + side, 2)
    for which in range(2):

        @pl.when(odd == which)
        def _():
            write(which)


def in_turn(which, first, second):
    return [*first, *second] if which == 0 else [*second, *first]


def apart(which, refs, n_first):
    n_second = len(refs) - n_first
    if which == 0:
        return refs[:n_first], refs[n_first:]
    return refs[n_second:], refs[:n_second]


def cut(ref, which, size, at=0, wide=None):
    wide = size if wide is None else wide
    return ref[:, pl.ds(pl.multiple_of(which * size + at, wide), wide)]


def put_keys(out, k, v, which):
    part = k.shape[1] // 2
    out[:, :part] = cut(k, which, part)
    out[:, part:] = cut(v, which, part)


def put_rows(out, q, do, part, unit, at=0):
    half = q.shape[1] // 2
    other = 1 - parity()
    out[:, at : at + part] = cut(q, other, half, unit * part, part)
    out[:, at + part : at + 2 * part] = cut(do, other, half, unit * part, part)


def pack_turns_kernel(side, q, do, k, v, *slots):
    *slots, ready = slots
    ready[...] = jnp.zeros_like(ready)
    mine = parity()

    def write(which):
        keys, rows = apart(which, slots, side)
        for d in range(side):
            put_keys(keys[d], k, v, mine if d % 2 == 0 else 1 - mine)
        for unit in range(len(rows)):
            put_rows(rows[unit], q, do, k.shape[1] // 2, unit)

    by_class(write)


def pack_kernel(n_mixed, q, do, o, sums, k, v, _, near_same, near_other, rest, stat_own):
    tokens, width = do.shape
    heads = sums.shape[0]
    part = k.shape[1] // 2
    n = heads // 2
    put_keys(near_same, k, v, parity())
    put_keys(near_other, k, v, 1 - parity())
    for unit in range(n_mixed, width // 2 // part):
        put_rows(rest, q, do, part, unit, (unit - n_mixed) * 2 * part)

    row = lax.broadcasted_iota(jnp.int32, (heads, width), 0)
    col = lax.broadcasted_iota(jnp.int32, (heads, width), 1)
    pick = jnp.where(col // HEAD_DIM == row, 1.0, 0.0).astype(BF16)
    prod = do[...].astype(F32) * o[...].astype(F32)
    high = prod.astype(BF16)
    low = (prod - high.astype(F32)).astype(BF16)
    delta = dot(pick, high, 1, 1) + dot(pick, low, 1, 1)
    lse = sums[...] * LOG2E

    def write_stats(mine, other):
        stat_own[:n, :] = lse[mine * n : (mine + 1) * n, :]
        stat_own[n:, :] = delta[mine * n : (mine + 1) * n, :]
        left = jnp.concatenate([x[other * n : (other + 1) * n, :] for x in (lse, delta)], 0)
        terms = []
        for _ in range(3):
            term = left.astype(BF16).astype(F32)
            left = left - term
            terms.append(term)
        terms.append(jnp.zeros((LANES - 6 * n, tokens), F32))
        rest[:, rest.shape[1] - LANES :] = jnp.transpose(jnp.concatenate(terms, 0)).astype(BF16)

    by_parity(write_stats)


def stack_heads(load, first, group):
    blocks = []
    for pair in range(group // 2):
        two = load((first + 2 * pair) * HEAD_DIM, 2 * HEAD_DIM)
        blocks += [two[:, :HEAD_DIM], two[:, HEAD_DIM:]]
    return jnp.concatenate(blocks, 0)


def stack_stats(stats, first, group):
    return jnp.concatenate([stats[first + g : first + g + 1] for g in range(group)], 1)


def head_grads(q, do, lse, delta, k, v):
    scores = dot(k, q, 1, 1)
    dprobs = dot(v, do, 1, 1)
    probs = jnp.exp2(scores * (LOG2E / math.sqrt(HEAD_DIM)) - lse)
    dscores = (probs * (dprobs - delta)).astype(BF16)
    dv = dot(probs.astype(BF16), do, 1, 0)
    dk = dot(dscores, q, 1, 0)
    dq = dot(k, dscores, 0, 0)
    return dk, dv, dq


def side_grads(pairs, load_q, load_do, load_stats, kv, put):
    part = kv.shape[1] // 2
    width = 2 * HEAD_DIM
    for pair in pairs:
        at = pair * width
        k_two, v_two = kv[:, at : at + width], kv[:, part + at : part + at + width]
        dks, dvs = [], []
        for odd in range(2):
            first = (2 * pair + odd) * put.group
            lanes = slice(odd * HEAD_DIM, (odd + 1) * HEAD_DIM)
            dk, dv, dq = head_grads(
                stack_heads(load_q, first, put.group),
                stack_heads(load_do, first, put.group),
                *load_stats(first),
                k_two[:, lanes],
                v_two[:, lanes],
            )
            dks.append(dk)
            dvs.append(dv)
            put(first, dq)
        put.store(at, jnp.concatenate(dks, 1), jnp.concatenate(dvs, 1))


class Put:
    def __init__(self, dq_acc, group, store):
        self.dq_acc, self.group, self.store = dq_acc, group, store

    def __call__(self, first, dq):
        tok = self.dq_acc.shape[1]
        for g in range(self.group):
            rows = slice((first + g) * HEAD_DIM, (first + g + 1) * HEAD_DIM)
            self.dq_acc[rows, :] += dq[:, g * tok : (g + 1) * tok]


def turned_dq(dq_acc, first, last):
    factor = 1.0 / math.sqrt(HEAD_DIM)
    blocks = [
        jnp.transpose(dq_acc[at : at + LANES, :])
        for at in range(first * HEAD_DIM, last * HEAD_DIM, LANES)
    ]
    return (jnp.concatenate(blocks, 1) * factor).astype(BF16)


def seen(flags, which):
    return jnp.max(flags[which : which + 1, :]) > 0


def seen_sides(owners, shards):
    rank, z = lax.axis_index("blk"), lax.axis_index("ulysses")
    n_blk = lax.axis_size("blk")
    before = lax.rem(rank + n_blk - 1, n_blk)
    place = lax.div(z, shards // 2)
    mine = owners[2 * rank + place]
    return mine > owners[2 * before + place], mine > owners[2 * before + 1 - place]


def own_loaders(q, do, stats, group):
    heads = stats.shape[0] // 2
    half = heads * HEAD_DIM
    mine = parity()

    def from_half(ref):
        def load(at, size):
            return ref[:, pl.ds(pl.multiple_of(mine * half + at, size), size)]

        return load

    def load_stats(first):
        every = stats[...]
        return stack_stats(every, first, group), stack_stats(every, heads + first, group)

    return from_half(q), from_half(do), load_stats


def partner_loaders(q_in, rest, part, heads):
    tok, kv_width = rest.shape[0], 2 * part
    n_mixed = q_in.shape[0] // tok

    def loader(offset):
        def load(at, size):
            unit, lane = at // part, offset + at % part
            if unit < n_mixed:
                return q_in[unit * tok : (unit + 1) * tok, lane : lane + size]
            lane += (unit - n_mixed) * kv_width
            return rest[:, lane : lane + size]

        return load

    def load_stats(first):
        terms = jnp.transpose(rest[:, rest.shape[1] - LANES :].astype(F32))
        n = 2 * heads
        every = terms[:n] + terms[n : 2 * n] + terms[2 * n : 3 * n]
        group = part // HEAD_DIM
        return stack_stats(every, first, group), stack_stats(every, heads + first, group)

    return loader(0), loader(part), load_stats


def finish(outs, acc, at, dk, dv):
    part, tok = acc.shape[1] // 2, outs[0].shape[0]
    dk = (dk + acc[:, at : at + LANES]) * (1.0 / math.sqrt(HEAD_DIM))
    dv = dv + acc[:, part + at : part + at + LANES]
    for d, out in enumerate(outs):
        rows = slice(d * tok, (d + 1) * tok)
        out[:, at : at + LANES] = dk[rows].astype(BF16)
        out[:, part + at : part + at + LANES] = dv[rows].astype(BF16)


def own_far_kernel(side, owners, q, do, stats, *rest):
    slots = rest[:-5]
    kv, q_in, acc, dq_acc, flags = rest[-5:]
    near_seen, far_seen = seen_sides(owners, 2 * side)
    line = lax.broadcasted_iota(jnp.int32, flags.shape, 0)
    flags[...] = jnp.where(line == 0, near_seen.astype(jnp.int32), far_seen.astype(jnp.int32))
    tok, part = q.shape[0], kv.shape[1] // 2

    def sort(which):
        keys, rows = apart(which, slots, side)
        for d in range(side):
            kv[d * tok : (d + 1) * tok, :] = keys[d][...]
        for unit in range(len(rows)):
            q_in[unit * tok : (unit + 1) * tok, :] = rows[unit][...]

    by_class(sort)
    dq_acc[...] = jnp.zeros_like(dq_acc)

    def store(at, dk, dv):
        acc[:, at : at + LANES] = dk
        acc[:, part + at : part + at + LANES] = dv

    @pl.when(far_seen)
    def _():
        group = part // HEAD_DIM
        loaders = own_loaders(q, do, stats, group)
        side_grads(range(part // LANES), *loaders, kv, Put(dq_acc, group, store))


def partner_far_kernel(flags, q_in, rest, kv, acc, *outs):
    far, dq_acc = outs[:-1], outs[-1]
    tok, part = rest.shape[0], kv.shape[1] // 2
    dq_acc[...] = jnp.zeros_like(dq_acc)

    def store(at, dk, dv):
        finish(far, acc, at, dk, dv)

    @pl.when(seen(flags, 1))
    def _():
        loaders = partner_loaders(q_in, rest, part, dq_acc.shape[0] // HEAD_DIM)
        side_grads(range(part // LANES), *loaders, kv, Put(dq_acc, part // HEAD_DIM, store))

    @pl.when(jnp.logical_not(seen(flags, 1)))
    def _():
        for out in far:
            out[...] = jnp.zeros_like(out)


def near_kernel(side, flags, q, do, stats, q_in, rest, own_dq, partner_dq, *refs):
    keys, near = refs[:side], refs[side : 2 * side]
    dq_own, dq_send, kv, acc, own_acc, partner_acc = refs[2 * side :]
    tok, part = q.shape[0], kv.shape[1] // 2
    heads = own_acc.shape[0] // HEAD_DIM
    group = part // HEAD_DIM
    pairs = range(part // LANES)
    own_acc[...] = own_dq[...]
    partner_acc[...] = partner_dq[...]

    @pl.when(seen(flags, 0))
    def _():
        for d in range(side):
            kv[d * tok : (d + 1) * tok, :] = keys[d][...]

        def keep(at, dk, dv):
            acc[:, at : at + LANES] = dk
            acc[:, part + at : part + at + LANES] = dv

        def store(at, dk, dv):
            finish(near, acc, at, dk, dv)

        side_grads(pairs, *own_loaders(q, do, stats, group), kv, Put(own_acc, group, keep))
        loaders = partner_loaders(q_in, rest, part, heads)
        side_grads(pairs, *loaders, kv, Put(partner_acc, group, store))

    @pl.when(jnp.logical_not(seen(flags, 0)))
    def _():
        for out in near:
            out[...] = jnp.zeros_like(out)

    dq_send[...] = turned_dq(partner_acc, 0, heads)
    dq_own[...] = turned_dq(own_acc, 0, heads)


def add_up(refs):
    totals = []
    for odd in range(2):
        total = refs[odd][...].astype(F32)
        for m in range(odd + 2, len(refs), 2):
            total = total + refs[m][...].astype(F32)
        totals.append(total)
    return totals


def join_far_kernel(*refs):
    for out, total in zip(refs[-2:], add_up(refs[:-2])):
        out[...] = total


def join_kernel(dq_own, dq_back, far_same, far_other, *rest):
    near = rest[:-3]
    gq, gk, gv = rest[-3:]
    half = dq_own.shape[1]
    part = gk.shape[1] // 2
    totals = [a[...] + b for a, b in zip((far_same, far_other), add_up(near))]

    def write(mine, other):
        gq[:, mine * half : (mine + 1) * half] = dq_own[...]
        gq[:, other * half : (other + 1) * half] = dq_back[...]
        for total, place in zip(totals, (mine, other)):
            gk[:, place * part : (place + 1) * part] = total[:, :part].astype(BF16)
            gv[:, place * part : (place + 1) * part] = total[:, part:].astype(BF16)

    by_parity(write)


def limit(mib):
    return pltpu.CompilerParams(vmem_limit_bytes=int(mib * 1024 * 1024))


def per_device(queries, key_states, value_states, attn_out, grad_out, log_sums, owners):
    n_blk, n_uly = lax.axis_size("blk"), lax.axis_size("ulysses")
    tok, width = queries.shape
    heads = log_sums.shape[1]
    kv_width = key_states.shape[1]
    half = width // 2
    side = n_uly // 2

    n_units = width // kv_width
    n_mixed = min(n_units, side)

    def flips(first, second):
        return [in_turn(which, first, second) for which in range(2)]

    def move(value, *by_kind):
        pairs = []
        for b in range(n_blk):
            for u in range(n_uly):
                step, flip = by_kind[(b + u // side) % len(by_kind)]
                pairs.append((b * n_uly + u, ((b + step) % n_blk) * n_uly + (u ^ flip)))
        return lax.ppermute(value, ("blk", "ulysses"), pairs)

    def shape(*dims, dtype=BF16):
        return jax.ShapeDtypeStruct(dims, dtype)

    def cover(flops):
        return pl.CostEstimate(flops=flops, bytes_accessed=1 << 20, transcendentals=0)

    unit = shape(tok, kv_width)
    sides = shape(side * tok, kv_width)
    sides_wide = shape(side * tok, kv_width, dtype=F32)
    dq_wide = shape(half, tok, dtype=F32)
    *slots, ready = pl.pallas_call(
        functools.partial(pack_turns_kernel, side),
        out_shape=[unit] * (side + n_mixed) + [shape(8, LANES, dtype=F32)],
        in_specs=[VMEM] * 4,
        out_specs=[VMEM] * (side + n_mixed + 1),
        compiler_params=limit(TURNS_MIB),
        name="pack_turns",
    )(queries, grad_out, key_states, value_states)
    near_same, near_other, rest, stat_own = pl.pallas_call(
        functools.partial(pack_kernel, n_mixed),
        out_shape=[unit] * 2
        + [
            shape(tok, (n_units - n_mixed) * kv_width + LANES),
            shape(heads, tok, dtype=F32),
        ],
        in_specs=[VMEM] * 6 + [ANY],
        out_specs=[VMEM] * 4,
        compiler_params=limit(PACK_MIB),
        name="pack",
    )(
        queries, grad_out, attn_out, jnp.transpose(log_sums), key_states, value_states, ready
    )
    turns = flips([(1, d) for d in range(side, n_uly)], [(0, 1)] * n_mixed)
    slots = [move(x, one, two) for x, one, two in zip(slots, *turns)]
    rest = move(rest, (0, 1))
    near = [move(near_other if d % 2 else near_same, (1, d)) for d in range(side)]
    outs = [sides, shape(n_mixed * tok, kv_width), sides_wide, dq_wide]
    outs.append(shape(8, LANES, dtype=jnp.int32))
    kv_far, q_in, acc_far, own_dq, flags = pl.pallas_call(
        functools.partial(own_far_kernel, side),
        out_shape=outs,
        in_specs=[SMEM] + [VMEM] * (3 + side + n_mixed),
        out_specs=[VMEM] * len(outs),
        compiler_params=limit(32),
        cost_estimate=cover(OWN),
        name="own_far",
    )(owners, queries, grad_out, stat_own, *slots)
    *far, partner_dq = pl.pallas_call(
        partner_far_kernel,
        out_shape=[unit] * side + [dq_wide],
        in_specs=[VMEM] * 5,
        out_specs=[VMEM] * (side + 1),
        compiler_params=limit(32),
        cost_estimate=cover(PARTNER),
        name="far",
    )(flags, q_in, rest, kv_far, acc_far)
    far = [move(x, (-1, side + d)) for d, x in enumerate(far)]
    scratch = [sides, sides_wide, dq_wide, dq_wide]
    *back, dq_own, dq_send = pl.pallas_call(
        functools.partial(near_kernel, side),
        out_shape=[unit] * side + [shape(tok, half)] * 2,
        in_specs=[VMEM] * (8 + side),
        out_specs=[VMEM] * (side + 2),
        scratch_shapes=[pltpu.VMEM(x.shape, x.dtype) for x in scratch],
        compiler_params=limit(32),
        cost_estimate=cover(PARTNER),
        name="near",
    )(flags, queries, grad_out, stat_own, q_in, rest, own_dq, partner_dq, *near)
    dq_back = move(dq_send, (0, 1))
    near = [move(back[d], (-1, d)) for d in reversed(range(side))][::-1]
    far = pl.pallas_call(
        join_far_kernel,
        out_shape=[shape(tok, kv_width, dtype=F32)] * 2,
        in_specs=[VMEM] * side,
        out_specs=[VMEM] * 2,
        compiler_params=limit(8),
        cost_estimate=cover(LONG),
        name="join_far",
    )(*far)
    return tuple(
        pl.pallas_call(
            join_kernel,
            out_shape=[shape(tok, width), shape(tok, kv_width), shape(tok, kv_width)],
            in_specs=[VMEM] * (4 + side),
            out_specs=[VMEM] * 3,
            compiler_params=limit(8),
            name="join",
        )(dq_own, dq_back, *far, *near)
    )


def solution(mesh):
    rows = P(("blk", "ulysses"), None)
    return jax.shard_map(
        per_device,
        mesh=mesh,
        in_specs=(rows, rows, rows, rows, rows, rows, P()),
        out_specs=(rows, rows, rows),
        check_vma=False,
    )
```

```python
import functools
import math

import jax
import jax.numpy as jnp
from jax import lax
from jax.experimental import pallas as pl
from jax.experimental.pallas import tpu as pltpu
from jax.sharding import PartitionSpec as P

HEAD_DIM = 64
LANES = 128
PACK_MIB = 60
TURNS_MIB = 53.4
LONG, OWN, PARTNER = 1 << 34, 1 << 31, 1 << 31
LOG2E = math.log2(math.e)
BF16 = jnp.bfloat16
F32 = jnp.float32
ANY = pl.BlockSpec(memory_space=pl.ANY)
VMEM = pl.BlockSpec(memory_space=pltpu.VMEM)
SMEM = pl.BlockSpec(memory_space=pltpu.SMEM)


def dot(a, b, a_dim, b_dim):
    return lax.dot_general(
        a, b, (((a_dim,), (b_dim,)), ((), ())), preferred_element_type=F32
    )


def parity():
    return lax.rem(lax.axis_index("ulysses"), 2)


def by_parity(write):
    for mine in range(2):

        @pl.when(parity() == mine)
        def _():
            write(mine, 1 - mine)


def by_class(write):
    side = lax.div(lax.axis_index("ulysses"), lax.axis_size("ulysses") // 2)
    odd = lax.rem(lax.axis_index("blk") + side, 2)
    for which in range(2):

        @pl.when(odd == which)
        def _():
            write(which)


def in_turn(which, first, second):
    return [*first, *second] if which == 0 else [*second, *first]


def apart(which, refs, n_first):
    n_second = len(refs) - n_first
    if which == 0:
        return refs[:n_first], refs[n_first:]
    return refs[n_second:], refs[:n_second]


def cut(ref, which, size, at=0, wide=None):
    wide = size if wide is None else wide
    return ref[:, pl.ds(pl.multiple_of(which * size + at, wide), wide)]


def put_keys(out, k, v, which):
    part = k.shape[1] // 2
    out[:, :part] = cut(k, which, part)
    out[:, part:] = cut(v, which, part)


def put_rows(out, q, do, part, unit, at=0):
    half = q.shape[1] // 2
    other = 1 - parity()
    out[:, at : at + part] = cut(q, other, half, unit * part, part)
    out[:, at + part : at + 2 * part] = cut(do, other, half, unit * part, part)


def pack_turns_kernel(side, q, do, k, v, *slots):
    *slots, ready = slots
    ready[...] = jnp.zeros_like(ready)
    mine = parity()

    def write(which):
        keys, rows = apart(which, slots, side)
        for d in range(side):
            put_keys(keys[d], k, v, mine if d % 2 == 0 else 1 - mine)
        for unit in range(len(rows)):
            put_rows(rows[unit], q, do, k.shape[1] // 2, unit)

    by_class(write)


def pack_kernel(n_mixed, q, do, o, sums, k, v, _, near_same, near_other, rest, stat_own):
    tokens, width = do.shape
    heads = sums.shape[0]
    part = k.shape[1] // 2
    n = heads // 2
    put_keys(near_same, k, v, parity())
    put_keys(near_other, k, v, 1 - parity())
    for unit in range(n_mixed, width // 2 // part):
        put_rows(rest, q, do, part, unit, (unit - n_mixed) * 2 * part)

    row = lax.broadcasted_iota(jnp.int32, (heads, width), 0)
    col = lax.broadcasted_iota(jnp.int32, (heads, width), 1)
    pick = jnp.where(col // HEAD_DIM == row, 1.0, 0.0).astype(BF16)
    prod = do[...].astype(F32) * o[...].astype(F32)
    high = prod.astype(BF16)
    low = (prod - high.astype(F32)).astype(BF16)
    delta = dot(pick, high, 1, 1) + dot(pick, low, 1, 1)
    lse = sums[...] * LOG2E

    def write_stats(mine, other):
        stat_own[:n, :] = lse[mine * n : (mine + 1) * n, :]
        stat_own[n:, :] = delta[mine * n : (mine + 1) * n, :]
        left = jnp.concatenate([x[other * n : (other + 1) * n, :] for x in (lse, delta)], 0)
        terms = []
        for _ in range(3):
            term = left.astype(BF16).astype(F32)
            left = left - term
            terms.append(term)
        terms.append(jnp.zeros((LANES - 6 * n, tokens), F32))
        rest[:, rest.shape[1] - LANES :] = jnp.transpose(jnp.concatenate(terms, 0)).astype(BF16)

    by_parity(write_stats)


def stack_heads(load, first, group):
    blocks = []
    for pair in range(group // 2):
        two = load((first + 2 * pair) * HEAD_DIM, 2 * HEAD_DIM)
        blocks += [two[:, :HEAD_DIM], two[:, HEAD_DIM:]]
    return jnp.concatenate(blocks, 0)


def stack_stats(stats, first, group):
    return jnp.concatenate([stats[first + g : first + g + 1] for g in range(group)], 1)


def head_grads(q, do, lse, delta, k, v):
    scores = dot(k, q, 1, 1)
    dprobs = dot(v, do, 1, 1)
    probs = jnp.exp2(scores * (LOG2E / math.sqrt(HEAD_DIM)) - lse)
    dscores = (probs * (dprobs - delta)).astype(BF16)
    dv = dot(probs.astype(BF16), do, 1, 0)
    dk = dot(dscores, q, 1, 0)
    dq = dot(k, dscores, 0, 0)
    return dk, dv, dq


def side_grads(pairs, load_q, load_do, load_stats, kv, put):
    part = kv.shape[1] // 2
    width = 2 * HEAD_DIM
    for pair in pairs:
        at = pair * width
        k_two, v_two = kv[:, at : at + width], kv[:, part + at : part + at + width]
        dks, dvs = [], []
        for odd in range(2):
            first = (2 * pair + odd) * put.group
            lanes = slice(odd * HEAD_DIM, (odd + 1) * HEAD_DIM)
            dk, dv, dq = head_grads(
                stack_heads(load_q, first, put.group),
                stack_heads(load_do, first, put.group),
                *load_stats(first),
                k_two[:, lanes],
                v_two[:, lanes],
            )
            dks.append(dk)
            dvs.append(dv)
            put(first, dq)
        put.store(at, jnp.concatenate(dks, 1), jnp.concatenate(dvs, 1))


class Put:
    def __init__(self, dq_acc, group, store):
        self.dq_acc, self.group, self.store = dq_acc, group, store

    def __call__(self, first, dq):
        tok = self.dq_acc.shape[1]
        for g in range(self.group):
            rows = slice((first + g) * HEAD_DIM, (first + g + 1) * HEAD_DIM)
            self.dq_acc[rows, :] += dq[:, g * tok : (g + 1) * tok]


def turned_dq(dq_acc, first, last):
    factor = 1.0 / math.sqrt(HEAD_DIM)
    blocks = [
        jnp.transpose(dq_acc[at : at + LANES, :])
        for at in range(first * HEAD_DIM, last * HEAD_DIM, LANES)
    ]
    return (jnp.concatenate(blocks, 1) * factor).astype(BF16)


def seen(flags, which):
    return jnp.max(flags[which : which + 1, :]) > 0


def seen_sides(owners, shards):
    rank, z = lax.axis_index("blk"), lax.axis_index("ulysses")
    n_blk = lax.axis_size("blk")
    before = lax.rem(rank + n_blk - 1, n_blk)
    place = lax.div(z, shards // 2)
    mine = owners[2 * rank + place]
    return mine > owners[2 * before + place], mine > owners[2 * before + 1 - place]


def own_loaders(q, do, stats, group):
    heads = stats.shape[0] // 2
    half = heads * HEAD_DIM
    mine = parity()

    def from_half(ref):
        def load(at, size):
            return ref[:, pl.ds(pl.multiple_of(mine * half + at, size), size)]

        return load

    def load_stats(first):
        every = stats[...]
        return stack_stats(every, first, group), stack_stats(every, heads + first, group)

    return from_half(q), from_half(do), load_stats


def partner_loaders(q_in, rest, part, heads):
    tok, kv_width = rest.shape[0], 2 * part
    n_mixed = q_in.shape[0] // tok

    def loader(offset):
        def load(at, size):
            unit, lane = at // part, offset + at % part
            if unit < n_mixed:
                return q_in[unit * tok : (unit + 1) * tok, lane : lane + size]
            lane += (unit - n_mixed) * kv_width
            return rest[:, lane : lane + size]

        return load

    def load_stats(first):
        terms = jnp.transpose(rest[:, rest.shape[1] - LANES :].astype(F32))
        n = 2 * heads
        every = terms[:n] + terms[n : 2 * n] + terms[2 * n : 3 * n]
        group = part // HEAD_DIM
        return stack_stats(every, first, group), stack_stats(every, heads + first, group)

    return loader(0), loader(part), load_stats


def finish(outs, acc, at, dk, dv):
    part, tok = acc.shape[1] // 2, outs[0].shape[0]
    dk = (dk + acc[:, at : at + LANES]) * (1.0 / math.sqrt(HEAD_DIM))
    dv = dv + acc[:, part + at : part + at + LANES]
    for d, out in enumerate(outs):
        rows = slice(d * tok, (d + 1) * tok)
        out[:, at : at + LANES] = dk[rows].astype(BF16)
        out[:, part + at : part + at + LANES] = dv[rows].astype(BF16)


def own_far_kernel(side, owners, q, do, stats, *rest):
    slots = rest[:-5]
    kv, q_in, acc, dq_acc, flags = rest[-5:]
    near_seen, far_seen = seen_sides(owners, 2 * side)
    line = lax.broadcasted_iota(jnp.int32, flags.shape, 0)
    flags[...] = jnp.where(line == 0, near_seen.astype(jnp.int32), far_seen.astype(jnp.int32))
    tok, part = q.shape[0], kv.shape[1] // 2

    def sort(which):
        keys, rows = apart(which, slots, side)
        for d in range(side):
            kv[d * tok : (d + 1) * tok, :] = keys[d][...]
        for unit in range(len(rows)):
            q_in[unit * tok : (unit + 1) * tok, :] = rows[unit][...]

    by_class(sort)
    dq_acc[...] = jnp.zeros_like(dq_acc)

    def store(at, dk, dv):
        acc[:, at : at + LANES] = dk
        acc[:, part + at : part + at + LANES] = dv

    @pl.when(far_seen)
    def _():
        group = part // HEAD_DIM
        loaders = own_loaders(q, do, stats, group)
        side_grads(range(part // LANES), *loaders, kv, Put(dq_acc, group, store))


def partner_far_kernel(flags, q_in, rest, kv, acc, *outs):
    far, dq_acc = outs[:-1], outs[-1]
    tok, part = rest.shape[0], kv.shape[1] // 2
    dq_acc[...] = jnp.zeros_like(dq_acc)

    def store(at, dk, dv):
        finish(far, acc, at, dk, dv)

    @pl.when(seen(flags, 1))
    def _():
        loaders = partner_loaders(q_in, rest, part, dq_acc.shape[0] // HEAD_DIM)
        side_grads(range(part // LANES), *loaders, kv, Put(dq_acc, part // HEAD_DIM, store))

    @pl.when(jnp.logical_not(seen(flags, 1)))
    def _():
        for out in far:
            out[...] = jnp.zeros_like(out)


def near_kernel(side, flags, q, do, stats, q_in, rest, own_dq, partner_dq, *refs):
    keys, refs = refs[:side], refs[side:]
    kv, acc, own_acc, partner_acc = refs[-4:]
    near, dq_own, refs = refs[-4 - side - 1 : -5], refs[-5], refs[: -5 - side]
    tok, part = q.shape[0], kv.shape[1] // 2
    heads = own_acc.shape[0] // HEAD_DIM
    group = part // HEAD_DIM
    pairs = range(part // LANES)
    n_back = heads * HEAD_DIM // kv.shape[1]
    n_turns = len(refs) - n_back
    n_turns //= 2
    far, slots, later = refs[:n_turns], refs[n_turns : 3 * n_turns], refs[3 * n_turns :]
    own_acc[...] = own_dq[...]
    partner_acc[...] = partner_dq[...]

    @pl.when(seen(flags, 0))
    def _():
        for d in range(side):
            kv[d * tok : (d + 1) * tok, :] = keys[d][...]

        def keep(at, dk, dv):
            acc[:, at : at + LANES] = dk
            acc[:, part + at : part + at + LANES] = dv

        def store(at, dk, dv):
            finish(near, acc, at, dk, dv)

        side_grads(pairs, *own_loaders(q, do, stats, group), kv, Put(own_acc, group, keep))
        loaders = partner_loaders(q_in, rest, part, heads)
        side_grads(pairs, *loaders, kv, Put(partner_acc, group, store))

    @pl.when(jnp.logical_not(seen(flags, 0)))
    def _():
        for out in near:
            out[...] = jnp.zeros_like(out)

    each = heads // n_back

    def write(which):
        keys, rows = apart(which, slots, n_turns)
        for out, ref in zip(keys, far):
            out[...] = ref[...]
        for i, out in enumerate(rows):
            out[...] = turned_dq(partner_acc, i * each, (i + 1) * each)

    by_class(write)
    for i, out in enumerate(later, n_turns):
        out[...] = turned_dq(partner_acc, i * each, (i + 1) * each)
    dq_own[...] = turned_dq(own_acc, 0, heads)


def widen_kernel(*refs):
    count = len(refs) // 2
    for i in range(count):
        refs[count + i][...] = refs[i][...].astype(F32)


def join_kernel(side, n_turns, dq_own, *refs):
    near, early, refs = refs[:side], refs[side : 2 * side - n_turns], refs[2 * side - n_turns :]
    slots, later, (gq, gk, gv) = refs[: 2 * n_turns], refs[2 * n_turns : -3], refs[-3:]
    half = dq_own.shape[1]
    part = gk.shape[1] // 2

    def write_class(which):
        keys, rows = apart(which, slots, n_turns)
        totals = []
        for odd in range(2):
            terms = [*near[odd::2], *[*early, *keys][odd::2]]
            totals.append(sum((ref[...].astype(F32) for ref in terms[1:]), terms[0][...].astype(F32)))

        def write(mine, other):
            gq[:, mine * half : (mine + 1) * half] = dq_own[...]
            for i, ref in enumerate([*rows, *later]):
                at = other * half + i * ref.shape[1]
                gq[:, at : at + ref.shape[1]] = ref[...]
            for total, place in zip(totals, (mine, other)):
                gk[:, place * part : (place + 1) * part] = total[:, :part].astype(BF16)
                gv[:, place * part : (place + 1) * part] = total[:, part:].astype(BF16)

        by_parity(write)

    by_class(write_class)


def limit(mib):
    return pltpu.CompilerParams(vmem_limit_bytes=int(mib * 1024 * 1024))


def per_device(queries, key_states, value_states, attn_out, grad_out, log_sums, owners):
    n_blk, n_uly = lax.axis_size("blk"), lax.axis_size("ulysses")
    tok, width = queries.shape
    heads = log_sums.shape[1]
    kv_width = key_states.shape[1]
    half = width // 2
    side = n_uly // 2

    n_units = width // kv_width
    n_mixed = min(n_units, side)

    def flips(first, second):
        return [in_turn(which, first, second) for which in range(2)]

    def move(value, *by_kind):
        pairs = []
        for b in range(n_blk):
            for u in range(n_uly):
                step, flip = by_kind[(b + u // side) % len(by_kind)]
                pairs.append((b * n_uly + u, ((b + step) % n_blk) * n_uly + (u ^ flip)))
        return lax.ppermute(value, ("blk", "ulysses"), pairs)

    def shape(*dims, dtype=BF16):
        return jax.ShapeDtypeStruct(dims, dtype)

    def cover(flops):
        return pl.CostEstimate(flops=flops, bytes_accessed=1 << 20, transcendentals=0)

    unit = shape(tok, kv_width)
    sides = shape(side * tok, kv_width)
    sides_wide = shape(side * tok, kv_width, dtype=F32)
    dq_wide = shape(half, tok, dtype=F32)
    *slots, ready = pl.pallas_call(
        functools.partial(pack_turns_kernel, side),
        out_shape=[unit] * (side + n_mixed) + [shape(8, LANES, dtype=F32)],
        in_specs=[VMEM] * 4,
        out_specs=[VMEM] * (side + n_mixed + 1),
        compiler_params=limit(TURNS_MIB),
        name="pack_turns",
    )(queries, grad_out, key_states, value_states)
    near_same, near_other, rest, stat_own = pl.pallas_call(
        functools.partial(pack_kernel, n_mixed),
        out_shape=[unit] * 2
        + [
            shape(tok, (n_units - n_mixed) * kv_width + LANES),
            shape(heads, tok, dtype=F32),
        ],
        in_specs=[VMEM] * 6 + [ANY],
        out_specs=[VMEM] * 4,
        compiler_params=limit(PACK_MIB),
        name="pack",
    )(
        queries, grad_out, attn_out, jnp.transpose(log_sums), key_states, value_states, ready
    )
    turns = flips([(1, d) for d in range(side, n_uly)], [(0, 1)] * n_mixed)
    slots = [move(x, one, two) for x, one, two in zip(slots, *turns)]
    rest = move(rest, (0, 1))
    near = [move(near_other if d % 2 else near_same, (1, d)) for d in range(side)]
    outs = [sides, shape(n_mixed * tok, kv_width), sides_wide, dq_wide]
    outs.append(shape(8, LANES, dtype=jnp.int32))
    kv_far, q_in, acc_far, own_dq, flags = pl.pallas_call(
        functools.partial(own_far_kernel, side),
        out_shape=outs,
        in_specs=[SMEM] + [VMEM] * (3 + side + n_mixed),
        out_specs=[VMEM] * len(outs),
        compiler_params=limit(32),
        cost_estimate=cover(OWN),
        name="own_far",
    )(owners, queries, grad_out, stat_own, *slots)
    *far, partner_dq = pl.pallas_call(
        partner_far_kernel,
        out_shape=[unit] * side + [dq_wide],
        in_specs=[VMEM] * 5,
        out_specs=[VMEM] * (side + 1),
        compiler_params=limit(32),
        cost_estimate=cover(PARTNER),
        name="far",
    )(flags, q_in, rest, kv_far, acc_far)
    n_back = half // kv_width
    n_turns = min(side // 2, n_back)
    n_early = side - n_turns
    early = [move(x, (-1, side + d)) for d, x in enumerate(far[:n_early])]
    outs = [unit] * (n_turns + n_back + side) + [shape(tok, half)]
    scratch = [sides, sides_wide, dq_wide, dq_wide]
    *back, dq_own = pl.pallas_call(
        functools.partial(near_kernel, side),
        out_shape=outs,
        in_specs=[VMEM] * (8 + side + n_turns),
        out_specs=[VMEM] * len(outs),
        scratch_shapes=[pltpu.VMEM(x.shape, x.dtype) for x in scratch],
        compiler_params=limit(32),
        cost_estimate=cover(PARTNER),
        name="near",
    )(flags, queries, grad_out, stat_own, q_in, rest, own_dq, partner_dq, *near, *far[n_early:])
    slots, later, near = back[: 2 * n_turns], back[2 * n_turns : -side], back[-side:]
    turns = flips([(-1, side + d) for d in range(n_early, side)], [(0, 1)] * n_turns)
    slots = [move(x, one, two) for x, one, two in zip(slots, *turns)]
    later = [move(x, (0, 1)) for x in later]
    near = [move(near[d], (-1, d)) for d in reversed(range(side))][::-1]
    early = pl.pallas_call(
        widen_kernel,
        out_shape=[shape(tok, kv_width, dtype=F32)] * n_early,
        in_specs=[VMEM] * n_early,
        out_specs=[VMEM] * n_early,
        compiler_params=limit(8),
        cost_estimate=cover(LONG),
        name="widen",
    )(*early)
    ins = [dq_own, *near, *early, *slots, *later]
    return tuple(
        pl.pallas_call(
            functools.partial(join_kernel, side, n_turns),
            out_shape=[shape(tok, width), shape(tok, kv_width), shape(tok, kv_width)],
            in_specs=[VMEM] * len(ins),
            out_specs=[VMEM] * 3,
            compiler_params=limit(8),
            name="join",
        )(*ins)
    )


def solution(mesh):
    rows = P(("blk", "ulysses"), None)
    return jax.shard_map(
        per_device,
        mesh=mesh,
        in_specs=(rows, rows, rows, rows, rows, rows, P()),
        out_specs=(rows, rows, rows),
        check_vma=False,
    )
```

```python
import functools
import math

import jax
import jax.numpy as jnp
from jax import lax
from jax.experimental import pallas as pl
from jax.experimental.pallas import tpu as pltpu
from jax.sharding import PartitionSpec as P

HEAD_DIM = 64
LANES = 128
PACK_MIB = 60
TURNS_MIB = 53.4
LONG, OWN, PARTNER = 1 << 34, 1 << 31, 1 << 31
LOG2E = math.log2(math.e)
BF16 = jnp.bfloat16
F32 = jnp.float32
ANY = pl.BlockSpec(memory_space=pl.ANY)
VMEM = pl.BlockSpec(memory_space=pltpu.VMEM)
SMEM = pl.BlockSpec(memory_space=pltpu.SMEM)


def dot(a, b, a_dim, b_dim):
    return lax.dot_general(
        a, b, (((a_dim,), (b_dim,)), ((), ())), preferred_element_type=F32
    )


def parity():
    return lax.rem(lax.axis_index("ulysses"), 2)


def by_parity(write):
    for mine in range(2):

        @pl.when(parity() == mine)
        def _():
            write(mine, 1 - mine)


def by_class(write):
    side = lax.div(lax.axis_index("ulysses"), lax.axis_size("ulysses") // 2)
    odd = lax.rem(lax.axis_index("blk") + side, 2)
    for which in range(2):

        @pl.when(odd == which)
        def _():
            write(which)


def in_turn(which, first, second):
    return [*first, *second] if which == 0 else [*second, *first]


def apart(which, refs, n_first):
    n_second = len(refs) - n_first
    if which == 0:
        return refs[:n_first], refs[n_first:]
    return refs[n_second:], refs[:n_second]


def cut(ref, which, size, at=0, wide=None):
    wide = size if wide is None else wide
    return ref[:, pl.ds(pl.multiple_of(which * size + at, wide), wide)]


def put_keys(out, k, v, which):
    part = k.shape[1] // 2
    out[:, :part] = cut(k, which, part)
    out[:, part:] = cut(v, which, part)


def put_rows(out, q, do, part, unit, at=0):
    half = q.shape[1] // 2
    other = 1 - parity()
    out[:, at : at + part] = cut(q, other, half, unit * part, part)
    out[:, at + part : at + 2 * part] = cut(do, other, half, unit * part, part)


def pack_turns_kernel(side, q, do, k, v, *slots):
    *slots, ready = slots
    ready[...] = jnp.zeros_like(ready)
    mine = parity()

    def write(which):
        keys, rows = apart(which, slots, side)
        for d in range(side):
            put_keys(keys[d], k, v, mine if d % 2 == 0 else 1 - mine)
        for unit in range(len(rows)):
            put_rows(rows[unit], q, do, k.shape[1] // 2, unit)

    by_class(write)


def pack_kernel(n_mixed, q, do, o, sums, k, v, _, near_same, near_other, rest, stat_own):
    tokens, width = do.shape
    heads = sums.shape[0]
    part = k.shape[1] // 2
    n = heads // 2
    put_keys(near_same, k, v, parity())
    put_keys(near_other, k, v, 1 - parity())
    for unit in range(n_mixed, width // 2 // part):
        put_rows(rest, q, do, part, unit, (unit - n_mixed) * 2 * part)

    row = lax.broadcasted_iota(jnp.int32, (heads, width), 0)
    col = lax.broadcasted_iota(jnp.int32, (heads, width), 1)
    pick = jnp.where(col // HEAD_DIM == row, 1.0, 0.0).astype(BF16)
    prod = do[...].astype(F32) * o[...].astype(F32)
    high = prod.astype(BF16)
    low = (prod - high.astype(F32)).astype(BF16)
    delta = dot(pick, high, 1, 1) + dot(pick, low, 1, 1)
    lse = sums[...] * LOG2E

    def write_stats(mine, other):
        stat_own[:n, :] = lse[mine * n : (mine + 1) * n, :]
        stat_own[n:, :] = delta[mine * n : (mine + 1) * n, :]
        left = jnp.concatenate([x[other * n : (other + 1) * n, :] for x in (lse, delta)], 0)
        terms = []
        for _ in range(3):
            term = left.astype(BF16).astype(F32)
            left = left - term
            terms.append(term)
        terms.append(jnp.zeros((LANES - 6 * n, tokens), F32))
        rest[:, rest.shape[1] - LANES :] = jnp.transpose(jnp.concatenate(terms, 0)).astype(BF16)

    by_parity(write_stats)


def stack_heads(load, first, group):
    blocks = []
    for pair in range(group // 2):
        two = load((first + 2 * pair) * HEAD_DIM, 2 * HEAD_DIM)
        blocks += [two[:, :HEAD_DIM], two[:, HEAD_DIM:]]
    return jnp.concatenate(blocks, 0)


def stack_stats(stats, first, group):
    return jnp.concatenate([stats[first + g : first + g + 1] for g in range(group)], 1)


def head_grads(q, do, lse, delta, k, v):
    scores = dot(k, q, 1, 1)
    dprobs = dot(v, do, 1, 1)
    probs = jnp.exp2(scores * (LOG2E / math.sqrt(HEAD_DIM)) - lse)
    dscores = (probs * (dprobs - delta)).astype(BF16)
    dv = dot(probs.astype(BF16), do, 1, 0)
    dk = dot(dscores, q, 1, 0)
    dq = dot(k, dscores, 0, 0)
    return dk, dv, dq


def side_grads(pairs, load_q, load_do, load_stats, kv, put):
    part = kv.shape[1] // 2
    width = 2 * HEAD_DIM
    for pair in pairs:
        at = pair * width
        k_two, v_two = kv[:, at : at + width], kv[:, part + at : part + at + width]
        dks, dvs = [], []
        for odd in range(2):
            first = (2 * pair + odd) * put.group
            lanes = slice(odd * HEAD_DIM, (odd + 1) * HEAD_DIM)
            dk, dv, dq = head_grads(
                stack_heads(load_q, first, put.group),
                stack_heads(load_do, first, put.group),
                *load_stats(first),
                k_two[:, lanes],
                v_two[:, lanes],
            )
            dks.append(dk)
            dvs.append(dv)
            put(first, dq)
        put.store(at, jnp.concatenate(dks, 1), jnp.concatenate(dvs, 1))


class Put:
    def __init__(self, dq_acc, group, store):
        self.dq_acc, self.group, self.store = dq_acc, group, store

    def __call__(self, first, dq):
        tok = self.dq_acc.shape[1]
        for g in range(self.group):
            rows = slice((first + g) * HEAD_DIM, (first + g + 1) * HEAD_DIM)
            self.dq_acc[rows, :] += dq[:, g * tok : (g + 1) * tok]


def turned_dq(dq_acc, first, last):
    factor = 1.0 / math.sqrt(HEAD_DIM)
    blocks = [
        jnp.transpose(dq_acc[at : at + LANES, :])
        for at in range(first * HEAD_DIM, last * HEAD_DIM, LANES)
    ]
    return (jnp.concatenate(blocks, 1) * factor).astype(BF16)


def seen(flags, which):
    return jnp.max(flags[which : which + 1, :]) > 0


def seen_sides(owners, shards):
    rank, z = lax.axis_index("blk"), lax.axis_index("ulysses")
    n_blk = lax.axis_size("blk")
    before = lax.rem(rank + n_blk - 1, n_blk)
    place = lax.div(z, shards // 2)
    mine = owners[2 * rank + place]
    return mine > owners[2 * before + place], mine > owners[2 * before + 1 - place]


def own_loaders(q, do, stats, group):
    heads = stats.shape[0] // 2
    half = heads * HEAD_DIM
    mine = parity()

    def from_half(ref):
        def load(at, size):
            return ref[:, pl.ds(pl.multiple_of(mine * half + at, size), size)]

        return load

    def load_stats(first):
        every = stats[...]
        return stack_stats(every, first, group), stack_stats(every, heads + first, group)

    return from_half(q), from_half(do), load_stats


def partner_loaders(q_in, rest, part, heads):
    tok, kv_width = rest.shape[0], 2 * part
    n_mixed = q_in.shape[0] // tok

    def loader(offset):
        def load(at, size):
            unit, lane = at // part, offset + at % part
            if unit < n_mixed:
                return q_in[unit * tok : (unit + 1) * tok, lane : lane + size]
            lane += (unit - n_mixed) * kv_width
            return rest[:, lane : lane + size]

        return load

    def load_stats(first):
        terms = jnp.transpose(rest[:, rest.shape[1] - LANES :].astype(F32))
        n = 2 * heads
        every = terms[:n] + terms[n : 2 * n] + terms[2 * n : 3 * n]
        group = part // HEAD_DIM
        return stack_stats(every, first, group), stack_stats(every, heads + first, group)

    return loader(0), loader(part), load_stats


def finish(outs, acc, at, dk, dv):
    part, tok = acc.shape[1] // 2, outs[0].shape[0]
    dk = (dk + acc[:, at : at + LANES]) * (1.0 / math.sqrt(HEAD_DIM))
    dv = dv + acc[:, part + at : part + at + LANES]
    for d, out in enumerate(outs):
        rows = slice(d * tok, (d + 1) * tok)
        out[:, at : at + LANES] = dk[rows].astype(BF16)
        out[:, part + at : part + at + LANES] = dv[rows].astype(BF16)


def own_far_kernel(side, owners, q, do, stats, *rest):
    slots = rest[:-5]
    kv, q_in, acc, dq_acc, flags = rest[-5:]
    near_seen, far_seen = seen_sides(owners, 2 * side)
    line = lax.broadcasted_iota(jnp.int32, flags.shape, 0)
    flags[...] = jnp.where(line == 0, near_seen.astype(jnp.int32), far_seen.astype(jnp.int32))
    tok, part = q.shape[0], kv.shape[1] // 2

    def sort(which):
        keys, rows = apart(which, slots, side)
        for d in range(side):
            kv[d * tok : (d + 1) * tok, :] = keys[d][...]
        for unit in range(len(rows)):
            q_in[unit * tok : (unit + 1) * tok, :] = rows[unit][...]

    by_class(sort)
    dq_acc[...] = jnp.zeros_like(dq_acc)

    def store(at, dk, dv):
        acc[:, at : at + LANES] = dk
        acc[:, part + at : part + at + LANES] = dv

    @pl.when(far_seen)
    def _():
        group = part // HEAD_DIM
        loaders = own_loaders(q, do, stats, group)
        side_grads(range(part // LANES), *loaders, kv, Put(dq_acc, group, store))


def partner_far_kernel(flags, q_in, rest, kv, acc, *outs):
    far, dq_acc = outs[:-1], outs[-1]
    tok, part = rest.shape[0], kv.shape[1] // 2
    dq_acc[...] = jnp.zeros_like(dq_acc)

    def store(at, dk, dv):
        finish(far, acc, at, dk, dv)

    @pl.when(seen(flags, 1))
    def _():
        loaders = partner_loaders(q_in, rest, part, dq_acc.shape[0] // HEAD_DIM)
        side_grads(range(part // LANES), *loaders, kv, Put(dq_acc, part // HEAD_DIM, store))

    @pl.when(jnp.logical_not(seen(flags, 1)))
    def _():
        for out in far:
            out[...] = jnp.zeros_like(out)


def near_kernel(side, flags, q, do, stats, q_in, rest, own_dq, partner_dq, *refs):
    keys, refs = refs[:side], refs[side:]
    kv, acc, own_acc, partner_acc = refs[-4:]
    near, dq_own, refs = refs[-4 - side - 1 : -5], refs[-5], refs[: -5 - side]
    tok, part = q.shape[0], kv.shape[1] // 2
    heads = own_acc.shape[0] // HEAD_DIM
    group = part // HEAD_DIM
    pairs = range(part // LANES)
    n_back = heads * HEAD_DIM // kv.shape[1]
    n_late = (len(refs) - n_back) // 2
    far, far_out, rows = refs[:n_late], refs[n_late : 2 * n_late], refs[2 * n_late :]
    own_acc[...] = own_dq[...]
    partner_acc[...] = partner_dq[...]

    @pl.when(seen(flags, 0))
    def _():
        for d in range(side):
            kv[d * tok : (d + 1) * tok, :] = keys[d][...]

        def keep(at, dk, dv):
            acc[:, at : at + LANES] = dk
            acc[:, part + at : part + at + LANES] = dv

        def store(at, dk, dv):
            finish(near, acc, at, dk, dv)

        side_grads(pairs, *own_loaders(q, do, stats, group), kv, Put(own_acc, group, keep))
        loaders = partner_loaders(q_in, rest, part, heads)
        side_grads(pairs, *loaders, kv, Put(partner_acc, group, store))

    @pl.when(jnp.logical_not(seen(flags, 0)))
    def _():
        for out in near:
            out[...] = jnp.zeros_like(out)

    for out, ref in zip(far_out, far):
        out[...] = ref[...]
    each = heads // n_back
    for i, out in enumerate(rows):
        out[...] = turned_dq(partner_acc, i * each, (i + 1) * each)
    dq_own[...] = turned_dq(own_acc, 0, heads)


def widen_kernel(*refs):
    count = len(refs) // 2
    for i in range(count):
        refs[count + i][...] = refs[i][...].astype(F32)


def join_kernel(side, dq_own, *refs):
    far, rows, near = refs[:side], refs[side : -3 - side], refs[-3 - side : -3][::-1]
    gq, gk, gv = refs[-3:]
    half = dq_own.shape[1]
    part = gk.shape[1] // 2
    totals = []
    for odd in range(2):
        terms = [*near[odd::2], *far[odd::2]]
        totals.append(sum((ref[...].astype(F32) for ref in terms[1:]), terms[0][...].astype(F32)))

    def write(mine, other):
        gq[:, mine * half : (mine + 1) * half] = dq_own[...]
        for i, ref in enumerate(rows):
            at = other * half + i * ref.shape[1]
            gq[:, at : at + ref.shape[1]] = ref[...]
        for total, place in zip(totals, (mine, other)):
            gk[:, place * part : (place + 1) * part] = total[:, :part].astype(BF16)
            gv[:, place * part : (place + 1) * part] = total[:, part:].astype(BF16)

    by_parity(write)


def limit(mib):
    return pltpu.CompilerParams(vmem_limit_bytes=int(mib * 1024 * 1024))


def per_device(queries, key_states, value_states, attn_out, grad_out, log_sums, owners):
    n_blk, n_uly = lax.axis_size("blk"), lax.axis_size("ulysses")
    tok, width = queries.shape
    heads = log_sums.shape[1]
    kv_width = key_states.shape[1]
    half = width // 2
    side = n_uly // 2

    n_units = width // kv_width
    n_mixed = min(n_units, side)

    def flips(first, second):
        return [in_turn(which, first, second) for which in range(2)]

    def move(value, *by_kind):
        pairs = []
        for b in range(n_blk):
            for u in range(n_uly):
                step, flip = by_kind[(b + u // side) % len(by_kind)]
                pairs.append((b * n_uly + u, ((b + step) % n_blk) * n_uly + (u ^ flip)))
        return lax.ppermute(value, ("blk", "ulysses"), pairs)

    def shape(*dims, dtype=BF16):
        return jax.ShapeDtypeStruct(dims, dtype)

    def cover(flops):
        return pl.CostEstimate(flops=flops, bytes_accessed=1 << 20, transcendentals=0)

    unit = shape(tok, kv_width)
    sides = shape(side * tok, kv_width)
    sides_wide = shape(side * tok, kv_width, dtype=F32)
    dq_wide = shape(half, tok, dtype=F32)
    *slots, ready = pl.pallas_call(
        functools.partial(pack_turns_kernel, side),
        out_shape=[unit] * (side + n_mixed) + [shape(8, LANES, dtype=F32)],
        in_specs=[VMEM] * 4,
        out_specs=[VMEM] * (side + n_mixed + 1),
        compiler_params=limit(TURNS_MIB),
        name="pack_turns",
    )(queries, grad_out, key_states, value_states)
    near_same, near_other, rest, stat_own = pl.pallas_call(
        functools.partial(pack_kernel, n_mixed),
        out_shape=[unit] * 2
        + [
            shape(tok, (n_units - n_mixed) * kv_width + LANES),
            shape(heads, tok, dtype=F32),
        ],
        in_specs=[VMEM] * 6 + [ANY],
        out_specs=[VMEM] * 4,
        compiler_params=limit(PACK_MIB),
        name="pack",
    )(
        queries, grad_out, attn_out, jnp.transpose(log_sums), key_states, value_states, ready
    )
    turns = flips([(1, d) for d in range(side, n_uly)], [(0, 1)] * n_mixed)
    slots = [move(x, one, two) for x, one, two in zip(slots, *turns)]
    rest = move(rest, (0, 1))
    near = [move(near_other if d % 2 else near_same, (1, d)) for d in range(side)]
    outs = [sides, shape(n_mixed * tok, kv_width), sides_wide, dq_wide]
    outs.append(shape(8, LANES, dtype=jnp.int32))
    kv_far, q_in, acc_far, own_dq, flags = pl.pallas_call(
        functools.partial(own_far_kernel, side),
        out_shape=outs,
        in_specs=[SMEM] + [VMEM] * (3 + side + n_mixed),
        out_specs=[VMEM] * len(outs),
        compiler_params=limit(32),
        cost_estimate=cover(OWN),
        name="own_far",
    )(owners, queries, grad_out, stat_own, *slots)
    *far, partner_dq = pl.pallas_call(
        partner_far_kernel,
        out_shape=[unit] * side + [dq_wide],
        in_specs=[VMEM] * 5,
        out_specs=[VMEM] * (side + 1),
        compiler_params=limit(32),
        cost_estimate=cover(PARTNER),
        name="far",
    )(flags, q_in, rest, kv_far, acc_far)
    n_back = half // kv_width
    n_early = side // 2
    n_late = side - n_early
    early = [move(x, (-1, side + d)) for d, x in enumerate(far[:n_early])]
    outs = [unit] * (n_late + n_back + side) + [shape(tok, half)]
    scratch = [sides, sides_wide, dq_wide, dq_wide]
    *back, dq_own = pl.pallas_call(
        functools.partial(near_kernel, side),
        out_shape=outs,
        in_specs=[VMEM] * (8 + side + n_late),
        out_specs=[VMEM] * len(outs),
        scratch_shapes=[pltpu.VMEM(x.shape, x.dtype) for x in scratch],
        compiler_params=limit(32),
        cost_estimate=cover(PARTNER),
        name="near",
    )(flags, queries, grad_out, stat_own, q_in, rest, own_dq, partner_dq, *near, *far[n_early:])
    late, rows, near = back[:n_late], back[n_late:-side], back[-side:]
    late = [move(x, (-1, side + n_early + d)) for d, x in enumerate(late)]
    rows = [move(x, (0, 1)) for x in rows]
    near = [move(near[d], (-1, d)) for d in reversed(range(side))][::-1]
    early = pl.pallas_call(
        widen_kernel,
        out_shape=[shape(tok, kv_width, dtype=F32)] * n_early,
        in_specs=[VMEM] * n_early,
        out_specs=[VMEM] * n_early,
        compiler_params=limit(8),
        cost_estimate=cover(LONG),
        name="widen",
    )(*early)
    ins = [dq_own, *early, *late, *rows, *near[::-1]]
    return tuple(
        pl.pallas_call(
            functools.partial(join_kernel, side),
            out_shape=[shape(tok, width), shape(tok, kv_width), shape(tok, kv_width)],
            in_specs=[VMEM] * len(ins),
            out_specs=[VMEM] * 3,
            compiler_params=limit(8),
            name="join",
        )(*ins)
    )


def solution(mesh):
    rows = P(("blk", "ulysses"), None)
    return jax.shard_map(
        per_device,
        mesh=mesh,
        in_specs=(rows, rows, rows, rows, rows, rows, P()),
        out_specs=(rows, rows, rows),
        check_vma=False,
    )
```

```python
import functools
import math

import jax
import jax.numpy as jnp
from jax import lax
from jax.experimental import pallas as pl
from jax.experimental.pallas import tpu as pltpu
from jax.sharding import PartitionSpec as P

HEAD_DIM = 64
LANES = 128
PACK_MIB = 60
TURNS_MIB = 53.4
NONE, SHORT, OWN, PARTNER, LONG = 1 << 20, 7 << 27, 1 << 31, 1 << 31, 1 << 34
LOG2E = math.log2(math.e)
BF16 = jnp.bfloat16
F32 = jnp.float32
ANY = pl.BlockSpec(memory_space=pl.ANY)
VMEM = pl.BlockSpec(memory_space=pltpu.VMEM)
SMEM = pl.BlockSpec(memory_space=pltpu.SMEM)


def dot(a, b, a_dim, b_dim):
    return lax.dot_general(
        a, b, (((a_dim,), (b_dim,)), ((), ())), preferred_element_type=F32
    )


def parity():
    return lax.rem(lax.axis_index("ulysses"), 2)


def by_parity(write):
    for mine in range(2):

        @pl.when(parity() == mine)
        def _():
            write(mine, 1 - mine)


def by_class(write):
    side = lax.div(lax.axis_index("ulysses"), lax.axis_size("ulysses") // 2)
    odd = lax.rem(lax.axis_index("blk") + side, 2)
    for which in range(2):

        @pl.when(odd == which)
        def _():
            write(which)


def in_turn(which, first, second):
    return [*first, *second] if which == 0 else [*second, *first]


def apart(which, refs, n_first):
    n_second = len(refs) - n_first
    if which == 0:
        return refs[:n_first], refs[n_first:]
    return refs[n_second:], refs[:n_second]


def cut(ref, which, size, at=0, wide=None):
    wide = size if wide is None else wide
    return ref[:, pl.ds(pl.multiple_of(which * size + at, wide), wide)]


def put_keys(out, k, v, which):
    part = k.shape[1] // 2
    out[:, :part] = cut(k, which, part)
    out[:, part:] = cut(v, which, part)


def put_rows(out, q, do, part, unit, at=0):
    half = q.shape[1] // 2
    other = 1 - parity()
    out[:, at : at + part] = cut(q, other, half, unit * part, part)
    out[:, at + part : at + 2 * part] = cut(do, other, half, unit * part, part)


def pack_turns_kernel(side, q, do, k, v, *slots):
    *slots, ready = slots
    ready[...] = jnp.zeros_like(ready)
    mine = parity()

    def write(which):
        keys, rows = apart(which, slots, side)
        for d in range(side):
            put_keys(keys[d], k, v, mine if d % 2 == 0 else 1 - mine)
        for unit in range(len(rows)):
            put_rows(rows[unit], q, do, k.shape[1] // 2, unit)

    by_class(write)


def pack_kernel(n_mixed, q, do, o, sums, k, v, _, near_same, near_other, rest, stat_own):
    tokens, width = do.shape
    heads = sums.shape[0]
    part = k.shape[1] // 2
    n = heads // 2
    put_keys(near_same, k, v, parity())
    put_keys(near_other, k, v, 1 - parity())
    for unit in range(n_mixed, width // 2 // part):
        put_rows(rest, q, do, part, unit, (unit - n_mixed) * 2 * part)

    row = lax.broadcasted_iota(jnp.int32, (heads, width), 0)
    col = lax.broadcasted_iota(jnp.int32, (heads, width), 1)
    pick = jnp.where(col // HEAD_DIM == row, 1.0, 0.0).astype(BF16)
    prod = do[...].astype(F32) * o[...].astype(F32)
    high = prod.astype(BF16)
    low = (prod - high.astype(F32)).astype(BF16)
    delta = dot(pick, high, 1, 1) + dot(pick, low, 1, 1)
    lse = sums[...] * LOG2E

    def write_stats(mine, other):
        stat_own[:n, :] = lse[mine * n : (mine + 1) * n, :]
        stat_own[n:, :] = delta[mine * n : (mine + 1) * n, :]
        left = jnp.concatenate([x[other * n : (other + 1) * n, :] for x in (lse, delta)], 0)
        terms = []
        for _ in range(3):
            term = left.astype(BF16).astype(F32)
            left = left - term
            terms.append(term)
        terms.append(jnp.zeros((LANES - 6 * n, tokens), F32))
        rest[:, rest.shape[1] - LANES :] = jnp.transpose(jnp.concatenate(terms, 0)).astype(BF16)

    by_parity(write_stats)


def stack_heads(load, first, group):
    blocks = []
    for pair in range(group // 2):
        two = load((first + 2 * pair) * HEAD_DIM, 2 * HEAD_DIM)
        blocks += [two[:, :HEAD_DIM], two[:, HEAD_DIM:]]
    return jnp.concatenate(blocks, 0)


def stack_stats(stats, first, group):
    return jnp.concatenate([stats[first + g : first + g + 1] for g in range(group)], 1)


def head_grads(q, do, lse, delta, k, v):
    scores = dot(k, q, 1, 1)
    dprobs = dot(v, do, 1, 1)
    probs = jnp.exp2(scores * (LOG2E / math.sqrt(HEAD_DIM)) - lse)
    dscores = (probs * (dprobs - delta)).astype(BF16)
    dv = dot(probs.astype(BF16), do, 1, 0)
    dk = dot(dscores, q, 1, 0)
    dq = dot(k, dscores, 0, 0)
    return dk, dv, dq


def side_grads(pairs, load_q, load_do, load_stats, kv, put):
    part = kv.shape[1] // 2
    width = 2 * HEAD_DIM
    for pair in pairs:
        at = pair * width
        k_two, v_two = kv[:, at : at + width], kv[:, part + at : part + at + width]
        dks, dvs = [], []
        for odd in range(2):
            first = (2 * pair + odd) * put.group
            lanes = slice(odd * HEAD_DIM, (odd + 1) * HEAD_DIM)
            dk, dv, dq = head_grads(
                stack_heads(load_q, first, put.group),
                stack_heads(load_do, first, put.group),
                *load_stats(first),
                k_two[:, lanes],
                v_two[:, lanes],
            )
            dks.append(dk)
            dvs.append(dv)
            put(first, dq)
        put.store(at, jnp.concatenate(dks, 1), jnp.concatenate(dvs, 1))


class Put:
    def __init__(self, dq_acc, group, store):
        self.dq_acc, self.group, self.store = dq_acc, group, store

    def __call__(self, first, dq):
        tok = self.dq_acc.shape[1]
        for g in range(self.group):
            rows = slice((first + g) * HEAD_DIM, (first + g + 1) * HEAD_DIM)
            self.dq_acc[rows, :] += dq[:, g * tok : (g + 1) * tok]


def turned_dq(dq_acc, first, last):
    factor = 1.0 / math.sqrt(HEAD_DIM)
    blocks = [
        jnp.transpose(dq_acc[at : at + LANES, :])
        for at in range(first * HEAD_DIM, last * HEAD_DIM, LANES)
    ]
    return (jnp.concatenate(blocks, 1) * factor).astype(BF16)


def seen(flags, which):
    return jnp.max(flags[which : which + 1, :]) > 0


def seen_sides(owners, shards):
    rank, z = lax.axis_index("blk"), lax.axis_index("ulysses")
    n_blk = lax.axis_size("blk")
    before = lax.rem(rank + n_blk - 1, n_blk)
    place = lax.div(z, shards // 2)
    mine = owners[2 * rank + place]
    return mine > owners[2 * before + place], mine > owners[2 * before + 1 - place]


def own_loaders(q, do, stats, group):
    heads = stats.shape[0] // 2
    half = heads * HEAD_DIM
    mine = parity()

    def from_half(ref):
        def load(at, size):
            return ref[:, pl.ds(pl.multiple_of(mine * half + at, size), size)]

        return load

    def load_stats(first):
        every = stats[...]
        return stack_stats(every, first, group), stack_stats(every, heads + first, group)

    return from_half(q), from_half(do), load_stats


def partner_loaders(q_in, rest, part, heads):
    tok, kv_width = rest.shape[0], 2 * part
    n_mixed = q_in.shape[0] // tok

    def loader(offset):
        def load(at, size):
            unit, lane = at // part, offset + at % part
            if unit < n_mixed:
                return q_in[unit * tok : (unit + 1) * tok, lane : lane + size]
            lane += (unit - n_mixed) * kv_width
            return rest[:, lane : lane + size]

        return load

    def load_stats(first):
        terms = jnp.transpose(rest[:, rest.shape[1] - LANES :].astype(F32))
        n = 2 * heads
        every = terms[:n] + terms[n : 2 * n] + terms[2 * n : 3 * n]
        group = part // HEAD_DIM
        return stack_stats(every, first, group), stack_stats(every, heads + first, group)

    return loader(0), loader(part), load_stats


def finish(outs, acc, at, dk, dv):
    part, tok = acc.shape[1] // 2, outs[0].shape[0]
    dk = (dk + acc[:, at : at + LANES]) * (1.0 / math.sqrt(HEAD_DIM))
    dv = dv + acc[:, part + at : part + at + LANES]
    for d, out in enumerate(outs):
        rows = slice(d * tok, (d + 1) * tok)
        out[:, at : at + LANES] = dk[rows].astype(BF16)
        out[:, part + at : part + at + LANES] = dv[rows].astype(BF16)


def own_far_kernel(side, owners, q, do, stats, *rest):
    slots = rest[:-5]
    kv, q_in, acc, dq_acc, flags = rest[-5:]
    near_seen, far_seen = seen_sides(owners, 2 * side)
    line = lax.broadcasted_iota(jnp.int32, flags.shape, 0)
    flags[...] = jnp.where(line == 0, near_seen.astype(jnp.int32), far_seen.astype(jnp.int32))
    tok, part = q.shape[0], kv.shape[1] // 2

    def sort(which):
        keys, rows = apart(which, slots, side)
        for d in range(side):
            kv[d * tok : (d + 1) * tok, :] = keys[d][...]
        for unit in range(len(rows)):
            q_in[unit * tok : (unit + 1) * tok, :] = rows[unit][...]

    by_class(sort)
    dq_acc[...] = jnp.zeros_like(dq_acc)

    def store(at, dk, dv):
        acc[:, at : at + LANES] = dk
        acc[:, part + at : part + at + LANES] = dv

    @pl.when(far_seen)
    def _():
        group = part // HEAD_DIM
        loaders = own_loaders(q, do, stats, group)
        side_grads(range(part // LANES), *loaders, kv, Put(dq_acc, group, store))


def partner_far_kernel(flags, q_in, rest, kv, acc, *outs):
    far, dq_acc = outs[:-1], outs[-1]
    tok, part = rest.shape[0], kv.shape[1] // 2
    dq_acc[...] = jnp.zeros_like(dq_acc)

    def store(at, dk, dv):
        finish(far, acc, at, dk, dv)

    @pl.when(seen(flags, 1))
    def _():
        loaders = partner_loaders(q_in, rest, part, dq_acc.shape[0] // HEAD_DIM)
        side_grads(range(part // LANES), *loaders, kv, Put(dq_acc, part // HEAD_DIM, store))

    @pl.when(jnp.logical_not(seen(flags, 1)))
    def _():
        for out in far:
            out[...] = jnp.zeros_like(out)


def partner_near_kernel(side, flags, q_in, rest, partner_dq, *refs):
    keys, refs = refs[:side], refs[side:]
    kv, acc, dq_acc = refs[-3:]
    tok, part = rest.shape[0], kv.shape[1] // 2
    heads = dq_acc.shape[0] // HEAD_DIM
    group = part // HEAD_DIM
    n_late = (len(refs) - 4) // 2
    far, far_out, dq_send = refs[:n_late], refs[n_late : 2 * n_late], refs[-4]
    dq_acc[...] = partner_dq[...]

    @pl.when(seen(flags, 0))
    def _():
        for d in range(side):
            kv[d * tok : (d + 1) * tok, :] = keys[d][...]

        def store(at, dk, dv):
            acc[:, at : at + LANES] = dk
            acc[:, part + at : part + at + LANES] = dv

        loaders = partner_loaders(q_in, rest, part, heads)
        side_grads(range(part // LANES), *loaders, kv, Put(dq_acc, group, store))

    for out, ref in zip(far_out, far):
        out[...] = ref[...]
    dq_send[...] = turned_dq(dq_acc, 0, heads)


def own_near_kernel(flags, q, do, stats, kv, acc, own_dq, *outs):
    *near, dq_own, dq_acc = outs
    part = kv.shape[1] // 2
    group = part // HEAD_DIM
    dq_acc[...] = own_dq[...]

    @pl.when(seen(flags, 0))
    def _():
        def store(at, dk, dv):
            finish(near, acc, at, dk, dv)

        loaders = own_loaders(q, do, stats, group)
        side_grads(range(part // LANES), *loaders, kv, Put(dq_acc, group, store))

    @pl.when(jnp.logical_not(seen(flags, 0)))
    def _():
        for out in near:
            out[...] = jnp.zeros_like(out)

    dq_own[...] = turned_dq(dq_acc, 0, dq_acc.shape[0] // HEAD_DIM)


def take_kernel(count, *refs):
    for ref, out in zip(refs[:count], refs[-count:]):
        out[...] = ref[...].astype(out.dtype)


def join_kernel(side, dq_own, *refs):
    far, dq_back, near = refs[:side], refs[side], refs[side + 1 : -3][::-1]
    gq, gk, gv = refs[-3:]
    half = dq_own.shape[1]
    part = gk.shape[1] // 2
    totals = []
    for odd in range(2):
        terms = [*near[odd::2], *far[odd::2]]
        totals.append(sum((ref[...].astype(F32) for ref in terms[1:]), terms[0][...].astype(F32)))

    def write(mine, other):
        gq[:, mine * half : (mine + 1) * half] = dq_own[...]
        gq[:, other * half : (other + 1) * half] = dq_back[...]
        for total, place in zip(totals, (mine, other)):
            gk[:, place * part : (place + 1) * part] = total[:, :part].astype(BF16)
            gv[:, place * part : (place + 1) * part] = total[:, part:].astype(BF16)

    by_parity(write)


def limit(mib):
    return pltpu.CompilerParams(vmem_limit_bytes=int(mib * 1024 * 1024))


def per_device(queries, key_states, value_states, attn_out, grad_out, log_sums, owners):
    n_blk, n_uly = lax.axis_size("blk"), lax.axis_size("ulysses")
    tok, width = queries.shape
    heads = log_sums.shape[1]
    kv_width = key_states.shape[1]
    half = width // 2
    side = n_uly // 2

    n_units = width // kv_width
    n_mixed = min(n_units, side)

    def flips(first, second):
        return [in_turn(which, first, second) for which in range(2)]

    def move(value, *by_kind):
        pairs = []
        for b in range(n_blk):
            for u in range(n_uly):
                step, flip = by_kind[(b + u // side) % len(by_kind)]
                pairs.append((b * n_uly + u, ((b + step) % n_blk) * n_uly + (u ^ flip)))
        return lax.ppermute(value, ("blk", "ulysses"), pairs)

    def shape(*dims, dtype=BF16):
        return jax.ShapeDtypeStruct(dims, dtype)

    def cover(flops):
        return pl.CostEstimate(flops=flops, bytes_accessed=1 << 20, transcendentals=0)

    unit = shape(tok, kv_width)
    sides = shape(side * tok, kv_width)
    sides_wide = shape(side * tok, kv_width, dtype=F32)
    dq_wide = shape(half, tok, dtype=F32)
    *slots, ready = pl.pallas_call(
        functools.partial(pack_turns_kernel, side),
        out_shape=[unit] * (side + n_mixed) + [shape(8, LANES, dtype=F32)],
        in_specs=[VMEM] * 4,
        out_specs=[VMEM] * (side + n_mixed + 1),
        compiler_params=limit(TURNS_MIB),
        name="pack_turns",
    )(queries, grad_out, key_states, value_states)
    near_same, near_other, rest, stat_own = pl.pallas_call(
        functools.partial(pack_kernel, n_mixed),
        out_shape=[unit] * 2
        + [
            shape(tok, (n_units - n_mixed) * kv_width + LANES),
            shape(heads, tok, dtype=F32),
        ],
        in_specs=[VMEM] * 6 + [ANY],
        out_specs=[VMEM] * 4,
        compiler_params=limit(PACK_MIB),
        name="pack",
    )(
        queries, grad_out, attn_out, jnp.transpose(log_sums), key_states, value_states, ready
    )
    turns = flips([(1, d) for d in range(side, n_uly)], [(0, 1)] * n_mixed)
    slots = [move(x, one, two) for x, one, two in zip(slots, *turns)]
    rest = move(rest, (0, 1))
    near = [move(near_other if d % 2 else near_same, (1, d)) for d in range(side)]
    outs = [sides, shape(n_mixed * tok, kv_width), sides_wide, dq_wide]
    outs.append(shape(8, LANES, dtype=jnp.int32))
    kv_far, q_in, acc_far, own_dq, flags = pl.pallas_call(
        functools.partial(own_far_kernel, side),
        out_shape=outs,
        in_specs=[SMEM] + [VMEM] * (3 + side + n_mixed),
        out_specs=[VMEM] * len(outs),
        compiler_params=limit(32),
        cost_estimate=cover(OWN),
        name="own_far",
    )(owners, queries, grad_out, stat_own, *slots)
    *far, partner_dq = pl.pallas_call(
        partner_far_kernel,
        out_shape=[unit] * side + [dq_wide],
        in_specs=[VMEM] * 5,
        out_specs=[VMEM] * (side + 1),
        compiler_params=limit(32),
        cost_estimate=cover(PARTNER),
        name="far",
    )(flags, q_in, rest, kv_far, acc_far)
    n_early = side // 2
    n_late = side - n_early
    early = [move(x, (-1, side + d)) for d, x in enumerate(far[:n_early])]
    outs = [unit] * n_late + [shape(tok, half), sides, sides_wide]
    *late, dq_back, kv_near, acc_near = pl.pallas_call(
        functools.partial(partner_near_kernel, side),
        out_shape=outs,
        in_specs=[VMEM] * (4 + side + n_late),
        out_specs=[VMEM] * len(outs),
        scratch_shapes=[pltpu.VMEM(dq_wide.shape, F32)],
        compiler_params=limit(32),
        cost_estimate=cover(PARTNER),
        name="near",
    )(flags, q_in, rest, partner_dq, *near, *far[n_early:])
    late = [move(x, (-1, side + n_early + d)) for d, x in enumerate(late)]
    dq_back = move(dq_back, (0, 1))
    outs = [unit] * side + [shape(tok, half)]
    *near, dq_own = pl.pallas_call(
        own_near_kernel,
        out_shape=outs,
        in_specs=[VMEM] * 7,
        out_specs=[VMEM] * len(outs),
        scratch_shapes=[pltpu.VMEM(dq_wide.shape, F32)],
        compiler_params=limit(32),
        cost_estimate=cover(NONE),
        name="own_near",
    )(flags, queries, grad_out, stat_own, kv_near, acc_near, own_dq)
    near = [move(near[d], (-1, d)) for d in reversed(range(side))][::-1]

    def take(first, outs, flops, *after):
        return pl.pallas_call(
            functools.partial(take_kernel, len(first)),
            out_shape=outs,
            in_specs=[VMEM] * len(first) + [ANY] * len(after),
            out_specs=[VMEM] * len(first),
            compiler_params=limit(8),
            cost_estimate=cover(flops),
            name="take",
        )(*first, *after)

    wide = shape(tok, kv_width, dtype=F32)
    early = take(early, [wide] * n_early, SHORT)
    late = take(late, [wide] * n_late, SHORT, early[0])
    (dq_back,) = take([dq_back], [shape(tok, half)], LONG, late[0])
    ins = [dq_own, *early, *late, dq_back, *near[::-1]]
    return tuple(
        pl.pallas_call(
            functools.partial(join_kernel, side),
            out_shape=[shape(tok, width), shape(tok, kv_width), shape(tok, kv_width)],
            in_specs=[VMEM] * len(ins),
            out_specs=[VMEM] * 3,
            compiler_params=limit(8),
            name="join",
        )(*ins)
    )


def solution(mesh):
    rows = P(("blk", "ulysses"), None)
    return jax.shard_map(
        per_device,
        mesh=mesh,
        in_specs=(rows, rows, rows, rows, rows, rows, P()),
        out_specs=(rows, rows, rows),
        check_vma=False,
    )
```

```python
import functools
import math

import jax
import jax.numpy as jnp
from jax import lax
from jax.experimental import pallas as pl
from jax.experimental.pallas import tpu as pltpu
from jax.sharding import PartitionSpec as P

HEAD_DIM = 64
LANES = 128
PACK_MIB = 60
TURNS_MIB = 53.4
NONE, SHORT, OWN, PARTNER, LONG = 1 << 20, 7 << 27, 1 << 31, 1 << 31, 1 << 34
LOG2E = math.log2(math.e)
BF16 = jnp.bfloat16
F32 = jnp.float32
ANY = pl.BlockSpec(memory_space=pl.ANY)
VMEM = pl.BlockSpec(memory_space=pltpu.VMEM)
SMEM = pl.BlockSpec(memory_space=pltpu.SMEM)


def dot(a, b, a_dim, b_dim):
    return lax.dot_general(
        a, b, (((a_dim,), (b_dim,)), ((), ())), preferred_element_type=F32
    )


def parity():
    return lax.rem(lax.axis_index("ulysses"), 2)


def by_parity(write):
    for mine in range(2):

        @pl.when(parity() == mine)
        def _():
            write(mine, 1 - mine)


def by_class(write):
    side = lax.div(lax.axis_index("ulysses"), lax.axis_size("ulysses") // 2)
    odd = lax.rem(lax.axis_index("blk") + side, 2)
    for which in range(2):

        @pl.when(odd == which)
        def _():
            write(which)


def in_turn(which, first, second):
    return [*first, *second] if which == 0 else [*second, *first]


def apart(which, refs, n_first):
    n_second = len(refs) - n_first
    if which == 0:
        return refs[:n_first], refs[n_first:]
    return refs[n_second:], refs[:n_second]


def cut(ref, which, size, at=0, wide=None):
    wide = size if wide is None else wide
    return ref[:, pl.ds(pl.multiple_of(which * size + at, wide), wide)]


def put_keys(out, k, v, which):
    part = k.shape[1] // 2
    out[:, :part] = cut(k, which, part)
    out[:, part:] = cut(v, which, part)


def put_rows(out, q, do, part, unit, at=0):
    half = q.shape[1] // 2
    other = 1 - parity()
    out[:, at : at + part] = cut(q, other, half, unit * part, part)
    out[:, at + part : at + 2 * part] = cut(do, other, half, unit * part, part)


def pack_turns_kernel(side, q, do, k, v, *slots):
    *slots, ready = slots
    ready[...] = jnp.zeros_like(ready)
    mine = parity()

    def write(which):
        keys, rows = apart(which, slots, side)
        for d in range(side):
            put_keys(keys[d], k, v, mine if d % 2 == 0 else 1 - mine)
        for unit in range(len(rows)):
            put_rows(rows[unit], q, do, k.shape[1] // 2, unit)

    by_class(write)


def pack_kernel(n_mixed, q, do, o, sums, k, v, _, near_same, near_other, rest, stat_own):
    tokens, width = do.shape
    heads = sums.shape[0]
    part = k.shape[1] // 2
    n = heads // 2
    put_keys(near_same, k, v, parity())
    put_keys(near_other, k, v, 1 - parity())
    for unit in range(n_mixed, width // 2 // part):
        put_rows(rest, q, do, part, unit, (unit - n_mixed) * 2 * part)

    row = lax.broadcasted_iota(jnp.int32, (heads, width), 0)
    col = lax.broadcasted_iota(jnp.int32, (heads, width), 1)
    pick = jnp.where(col // HEAD_DIM == row, 1.0, 0.0).astype(BF16)
    prod = do[...].astype(F32) * o[...].astype(F32)
    high = prod.astype(BF16)
    low = (prod - high.astype(F32)).astype(BF16)
    delta = dot(pick, high, 1, 1) + dot(pick, low, 1, 1)
    lse = sums[...] * LOG2E

    def write_stats(mine, other):
        stat_own[:n, :] = lse[mine * n : (mine + 1) * n, :]
        stat_own[n:, :] = delta[mine * n : (mine + 1) * n, :]
        left = jnp.concatenate([x[other * n : (other + 1) * n, :] for x in (lse, delta)], 0)
        terms = []
        for _ in range(3):
            term = left.astype(BF16).astype(F32)
            left = left - term
            terms.append(term)
        terms.append(jnp.zeros((LANES - 6 * n, tokens), F32))
        rest[:, rest.shape[1] - LANES :] = jnp.transpose(jnp.concatenate(terms, 0)).astype(BF16)

    by_parity(write_stats)


def stack_heads(load, first, group):
    blocks = []
    for pair in range(group // 2):
        two = load((first + 2 * pair) * HEAD_DIM, 2 * HEAD_DIM)
        blocks += [two[:, :HEAD_DIM], two[:, HEAD_DIM:]]
    return jnp.concatenate(blocks, 0)


def stack_stats(stats, first, group):
    return jnp.concatenate([stats[first + g : first + g + 1] for g in range(group)], 1)


def head_grads(q, do, lse, delta, k, v):
    scores = dot(k, q, 1, 1)
    dprobs = dot(v, do, 1, 1)
    probs = jnp.exp2(scores * (LOG2E / math.sqrt(HEAD_DIM)) - lse)
    dscores = (probs * (dprobs - delta)).astype(BF16)
    dv = dot(do, probs.astype(BF16), 0, 1)
    dk = dot(q, dscores, 0, 1)
    dq = dot(k, dscores, 0, 0)
    return dk, dv, dq


def side_grads(pairs, load_q, load_do, load_stats, kv, put):
    part = kv.shape[1] // 2
    width = 2 * HEAD_DIM
    for pair in pairs:
        at = pair * width
        k_two, v_two = kv[:, at : at + width], kv[:, part + at : part + at + width]
        dks, dvs = [], []
        for odd in range(2):
            first = (2 * pair + odd) * put.group
            lanes = slice(odd * HEAD_DIM, (odd + 1) * HEAD_DIM)
            dk, dv, dq = head_grads(
                stack_heads(load_q, first, put.group),
                stack_heads(load_do, first, put.group),
                *load_stats(first),
                k_two[:, lanes],
                v_two[:, lanes],
            )
            dks.append(dk)
            dvs.append(dv)
            put(first, dq)
        put.store(at, *(jnp.transpose(jnp.concatenate(x, 0)) for x in (dks, dvs)))


class Put:
    def __init__(self, dq_acc, group, store):
        self.dq_acc, self.group, self.store = dq_acc, group, store

    def __call__(self, first, dq):
        tok = self.dq_acc.shape[1]
        for g in range(self.group):
            rows = slice((first + g) * HEAD_DIM, (first + g + 1) * HEAD_DIM)
            self.dq_acc[rows, :] += dq[:, g * tok : (g + 1) * tok]


def turned_dq(dq_acc, first, last):
    factor = 1.0 / math.sqrt(HEAD_DIM)
    blocks = [
        jnp.transpose(dq_acc[at : at + LANES, :])
        for at in range(first * HEAD_DIM, last * HEAD_DIM, LANES)
    ]
    return (jnp.concatenate(blocks, 1) * factor).astype(BF16)


def seen(flags, which):
    return jnp.max(flags[which : which + 1, :]) > 0


def seen_sides(owners, shards):
    rank, z = lax.axis_index("blk"), lax.axis_index("ulysses")
    n_blk = lax.axis_size("blk")
    before = lax.rem(rank + n_blk - 1, n_blk)
    place = lax.div(z, shards // 2)
    mine = owners[2 * rank + place]
    return mine > owners[2 * before + place], mine > owners[2 * before + 1 - place]


def own_loaders(q, do, stats, group):
    heads = stats.shape[0] // 2
    half = heads * HEAD_DIM
    mine = parity()

    def from_half(ref):
        def load(at, size):
            return ref[:, pl.ds(pl.multiple_of(mine * half + at, size), size)]

        return load

    def load_stats(first):
        every = stats[...]
        return stack_stats(every, first, group), stack_stats(every, heads + first, group)

    return from_half(q), from_half(do), load_stats


def partner_loaders(q_in, rest, part, heads):
    tok, kv_width = rest.shape[0], 2 * part
    n_mixed = q_in.shape[0] // tok

    def loader(offset):
        def load(at, size):
            unit, lane = at // part, offset + at % part
            if unit < n_mixed:
                return q_in[unit * tok : (unit + 1) * tok, lane : lane + size]
            lane += (unit - n_mixed) * kv_width
            return rest[:, lane : lane + size]

        return load

    def load_stats(first):
        terms = jnp.transpose(rest[:, rest.shape[1] - LANES :].astype(F32))
        n = 2 * heads
        every = terms[:n] + terms[n : 2 * n] + terms[2 * n : 3 * n]
        group = part // HEAD_DIM
        return stack_stats(every, first, group), stack_stats(every, heads + first, group)

    return loader(0), loader(part), load_stats


def finish(outs, acc, at, dk, dv):
    part, tok = acc.shape[1] // 2, outs[0].shape[0]
    dk = (dk + acc[:, at : at + LANES]) * (1.0 / math.sqrt(HEAD_DIM))
    dv = dv + acc[:, part + at : part + at + LANES]
    for d, out in enumerate(outs):
        rows = slice(d * tok, (d + 1) * tok)
        out[:, at : at + LANES] = dk[rows].astype(BF16)
        out[:, part + at : part + at + LANES] = dv[rows].astype(BF16)


def own_far_kernel(side, owners, q, do, stats, *rest):
    slots = rest[:-5]
    kv, q_in, acc, dq_acc, flags = rest[-5:]
    near_seen, far_seen = seen_sides(owners, 2 * side)
    line = lax.broadcasted_iota(jnp.int32, flags.shape, 0)
    flags[...] = jnp.where(line == 0, near_seen.astype(jnp.int32), far_seen.astype(jnp.int32))
    tok, part = q.shape[0], kv.shape[1] // 2

    def sort(which):
        keys, rows = apart(which, slots, side)
        for d in range(side):
            kv[d * tok : (d + 1) * tok, :] = keys[d][...]
        for unit in range(len(rows)):
            q_in[unit * tok : (unit + 1) * tok, :] = rows[unit][...]

    by_class(sort)
    dq_acc[...] = jnp.zeros_like(dq_acc)

    def store(at, dk, dv):
        acc[:, at : at + LANES] = dk
        acc[:, part + at : part + at + LANES] = dv

    @pl.when(far_seen)
    def _():
        group = part // HEAD_DIM
        loaders = own_loaders(q, do, stats, group)
        side_grads(range(part // LANES), *loaders, kv, Put(dq_acc, group, store))


def partner_far_kernel(flags, q_in, rest, kv, acc, *outs):
    far, dq_acc = outs[:-1], outs[-1]
    tok, part = rest.shape[0], kv.shape[1] // 2
    dq_acc[...] = jnp.zeros_like(dq_acc)

    def store(at, dk, dv):
        finish(far, acc, at, dk, dv)

    @pl.when(seen(flags, 1))
    def _():
        loaders = partner_loaders(q_in, rest, part, dq_acc.shape[0] // HEAD_DIM)
        side_grads(range(part // LANES), *loaders, kv, Put(dq_acc, part // HEAD_DIM, store))

    @pl.when(jnp.logical_not(seen(flags, 1)))
    def _():
        for out in far:
            out[...] = jnp.zeros_like(out)


def partner_near_kernel(side, flags, q_in, rest, partner_dq, *refs):
    keys, refs = refs[:side], refs[side:]
    kv, acc, dq_acc = refs[-3:]
    tok, part = rest.shape[0], kv.shape[1] // 2
    heads = dq_acc.shape[0] // HEAD_DIM
    group = part // HEAD_DIM
    n_late = (len(refs) - 4) // 2
    far, far_out, dq_send = refs[:n_late], refs[n_late : 2 * n_late], refs[-4]
    dq_acc[...] = partner_dq[...]

    @pl.when(seen(flags, 0))
    def _():
        for d in range(side):
            kv[d * tok : (d + 1) * tok, :] = keys[d][...]

        def store(at, dk, dv):
            acc[:, at : at + LANES] = dk
            acc[:, part + at : part + at + LANES] = dv

        loaders = partner_loaders(q_in, rest, part, heads)
        side_grads(range(part // LANES), *loaders, kv, Put(dq_acc, group, store))

    for out, ref in zip(far_out, far):
        out[...] = ref[...]
    dq_send[...] = turned_dq(dq_acc, 0, heads)


def own_near_kernel(flags, q, do, stats, kv, acc, own_dq, *outs):
    *near, dq_own, dq_acc = outs
    part = kv.shape[1] // 2
    group = part // HEAD_DIM
    dq_acc[...] = own_dq[...]

    @pl.when(seen(flags, 0))
    def _():
        def store(at, dk, dv):
            finish(near, acc, at, dk, dv)

        loaders = own_loaders(q, do, stats, group)
        side_grads(range(part // LANES), *loaders, kv, Put(dq_acc, group, store))

    @pl.when(jnp.logical_not(seen(flags, 0)))
    def _():
        for out in near:
            out[...] = jnp.zeros_like(out)

    dq_own[...] = turned_dq(dq_acc, 0, dq_acc.shape[0] // HEAD_DIM)


def take_kernel(count, *refs):
    for ref, out in zip(refs[:count], refs[-count:]):
        out[...] = ref[...].astype(out.dtype)


def join_kernel(side, dq_own, *refs):
    far, dq_back, near = refs[:side], refs[side], refs[side + 1 : -3][::-1]
    gq, gk, gv = refs[-3:]
    half = dq_own.shape[1]
    part = gk.shape[1] // 2
    totals = []
    for odd in range(2):
        terms = [*near[odd::2], *far[odd::2]]
        totals.append(sum((ref[...].astype(F32) for ref in terms[1:]), terms[0][...].astype(F32)))

    def write(mine, other):
        gq[:, mine * half : (mine + 1) * half] = dq_own[...]
        gq[:, other * half : (other + 1) * half] = dq_back[...]
        for total, place in zip(totals, (mine, other)):
            gk[:, place * part : (place + 1) * part] = total[:, :part].astype(BF16)
            gv[:, place * part : (place + 1) * part] = total[:, part:].astype(BF16)

    by_parity(write)


def limit(mib):
    return pltpu.CompilerParams(vmem_limit_bytes=int(mib * 1024 * 1024))


def per_device(queries, key_states, value_states, attn_out, grad_out, log_sums, owners):
    n_blk, n_uly = lax.axis_size("blk"), lax.axis_size("ulysses")
    tok, width = queries.shape
    heads = log_sums.shape[1]
    kv_width = key_states.shape[1]
    half = width // 2
    side = n_uly // 2

    n_units = width // kv_width
    n_mixed = min(n_units, side)

    def flips(first, second):
        return [in_turn(which, first, second) for which in range(2)]

    def move(value, *by_kind):
        pairs = []
        for b in range(n_blk):
            for u in range(n_uly):
                step, flip = by_kind[(b + u // side) % len(by_kind)]
                pairs.append((b * n_uly + u, ((b + step) % n_blk) * n_uly + (u ^ flip)))
        return lax.ppermute(value, ("blk", "ulysses"), pairs)

    def shape(*dims, dtype=BF16):
        return jax.ShapeDtypeStruct(dims, dtype)

    def cover(flops):
        return pl.CostEstimate(flops=flops, bytes_accessed=1 << 20, transcendentals=0)

    unit = shape(tok, kv_width)
    sides = shape(side * tok, kv_width)
    sides_wide = shape(side * tok, kv_width, dtype=F32)
    dq_wide = shape(half, tok, dtype=F32)
    *slots, ready = pl.pallas_call(
        functools.partial(pack_turns_kernel, side),
        out_shape=[unit] * (side + n_mixed) + [shape(8, LANES, dtype=F32)],
        in_specs=[VMEM] * 4,
        out_specs=[VMEM] * (side + n_mixed + 1),
        compiler_params=limit(TURNS_MIB),
        name="pack_turns",
    )(queries, grad_out, key_states, value_states)
    near_same, near_other, rest, stat_own = pl.pallas_call(
        functools.partial(pack_kernel, n_mixed),
        out_shape=[unit] * 2
        + [
            shape(tok, (n_units - n_mixed) * kv_width + LANES),
            shape(heads, tok, dtype=F32),
        ],
        in_specs=[VMEM] * 6 + [ANY],
        out_specs=[VMEM] * 4,
        compiler_params=limit(PACK_MIB),
        name="pack",
    )(
        queries, grad_out, attn_out, jnp.transpose(log_sums), key_states, value_states, ready
    )
    turns = flips([(1, d) for d in range(side, n_uly)], [(0, 1)] * n_mixed)
    slots = [move(x, one, two) for x, one, two in zip(slots, *turns)]
    rest = move(rest, (0, 1))
    near = [move(near_other if d % 2 else near_same, (1, d)) for d in range(side)]
    outs = [sides, shape(n_mixed * tok, kv_width), sides_wide, dq_wide]
    outs.append(shape(8, LANES, dtype=jnp.int32))
    kv_far, q_in, acc_far, own_dq, flags = pl.pallas_call(
        functools.partial(own_far_kernel, side),
        out_shape=outs,
        in_specs=[SMEM] + [VMEM] * (3 + side + n_mixed),
        out_specs=[VMEM] * len(outs),
        compiler_params=limit(32),
        cost_estimate=cover(OWN),
        name="own_far",
    )(owners, queries, grad_out, stat_own, *slots)
    *far, partner_dq = pl.pallas_call(
        partner_far_kernel,
        out_shape=[unit] * side + [dq_wide],
        in_specs=[VMEM] * 5,
        out_specs=[VMEM] * (side + 1),
        compiler_params=limit(32),
        cost_estimate=cover(PARTNER),
        name="far",
    )(flags, q_in, rest, kv_far, acc_far)
    n_early = side // 2
    n_late = side - n_early
    early = [move(x, (-1, side + d)) for d, x in enumerate(far[:n_early])]
    outs = [unit] * n_late + [shape(tok, half), sides, sides_wide]
    *late, dq_back, kv_near, acc_near = pl.pallas_call(
        functools.partial(partner_near_kernel, side),
        out_shape=outs,
        in_specs=[VMEM] * (4 + side + n_late),
        out_specs=[VMEM] * len(outs),
        scratch_shapes=[pltpu.VMEM(dq_wide.shape, F32)],
        compiler_params=limit(32),
        cost_estimate=cover(PARTNER),
        name="near",
    )(flags, q_in, rest, partner_dq, *near, *far[n_early:])
    late = [move(x, (-1, side + n_early + d)) for d, x in enumerate(late)]
    dq_back = move(dq_back, (0, 1))
    outs = [unit] * side + [shape(tok, half)]
    *near, dq_own = pl.pallas_call(
        own_near_kernel,
        out_shape=outs,
        in_specs=[VMEM] * 7,
        out_specs=[VMEM] * len(outs),
        scratch_shapes=[pltpu.VMEM(dq_wide.shape, F32)],
        compiler_params=limit(32),
        cost_estimate=cover(NONE),
        name="own_near",
    )(flags, queries, grad_out, stat_own, kv_near, acc_near, own_dq)
    near = [move(near[d], (-1, d)) for d in reversed(range(side))][::-1]

    def take(first, outs, flops, *after):
        return pl.pallas_call(
            functools.partial(take_kernel, len(first)),
            out_shape=outs,
            in_specs=[VMEM] * len(first) + [ANY] * len(after),
            out_specs=[VMEM] * len(first),
            compiler_params=limit(8),
            cost_estimate=cover(flops),
            name="take",
        )(*first, *after)

    wide = shape(tok, kv_width, dtype=F32)
    early = take(early, [wide] * n_early, SHORT)
    late = take(late, [wide] * n_late, SHORT, early[0])
    (dq_back,) = take([dq_back], [shape(tok, half)], LONG, late[0])
    ins = [dq_own, *early, *late, dq_back, *near[::-1]]
    return tuple(
        pl.pallas_call(
            functools.partial(join_kernel, side),
            out_shape=[shape(tok, width), shape(tok, kv_width), shape(tok, kv_width)],
            in_specs=[VMEM] * len(ins),
            out_specs=[VMEM] * 3,
            compiler_params=limit(8),
            name="join",
        )(*ins)
    )


def solution(mesh):
    rows = P(("blk", "ulysses"), None)
    return jax.shard_map(
        per_device,
        mesh=mesh,
        in_specs=(rows, rows, rows, rows, rows, rows, P()),
        out_specs=(rows, rows, rows),
        check_vma=False,
    )
```

```python
import functools
import math

import jax
import jax.numpy as jnp
from jax import lax
from jax.experimental import pallas as pl
from jax.experimental.pallas import tpu as pltpu
from jax.sharding import PartitionSpec as P

HEAD_DIM = 64
LANES = 128
PACK_MIB = 60
TURNS_MIB = 53.4
NONE, SHORT, OWN, PARTNER, LONG = 1 << 20, 7 << 27, 1 << 31, 1 << 31, 1 << 34
LOG2E = math.log2(math.e)
BF16 = jnp.bfloat16
F32 = jnp.float32
ANY = pl.BlockSpec(memory_space=pl.ANY)
VMEM = pl.BlockSpec(memory_space=pltpu.VMEM)
SMEM = pl.BlockSpec(memory_space=pltpu.SMEM)


def dot(a, b, a_dim, b_dim):
    return lax.dot_general(
        a, b, (((a_dim,), (b_dim,)), ((), ())), preferred_element_type=F32
    )


def parity():
    return lax.rem(lax.axis_index("ulysses"), 2)


def by_parity(write):
    for mine in range(2):

        @pl.when(parity() == mine)
        def _():
            write(mine, 1 - mine)


def by_class(write):
    side = lax.div(lax.axis_index("ulysses"), lax.axis_size("ulysses") // 2)
    odd = lax.rem(lax.axis_index("blk") + side, 2)
    for which in range(2):

        @pl.when(odd == which)
        def _():
            write(which)


def in_turn(which, first, second):
    return [*first, *second] if which == 0 else [*second, *first]


def apart(which, refs, n_first):
    n_second = len(refs) - n_first
    if which == 0:
        return refs[:n_first], refs[n_first:]
    return refs[n_second:], refs[:n_second]


def cut(ref, which, size, at=0, wide=None):
    wide = size if wide is None else wide
    return ref[:, pl.ds(pl.multiple_of(which * size + at, wide), wide)]


def put_keys(out, k, v, which):
    part = k.shape[1] // 2
    out[:, :part] = cut(k, which, part)
    out[:, part:] = cut(v, which, part)


def put_rows(out, q, do, part, unit, at=0):
    half = q.shape[1] // 2
    other = 1 - parity()
    out[:, at : at + part] = cut(q, other, half, unit * part, part)
    out[:, at + part : at + 2 * part] = cut(do, other, half, unit * part, part)


def pack_turns_kernel(side, q, do, k, v, *slots):
    *slots, ready = slots
    ready[...] = jnp.zeros_like(ready)
    mine = parity()

    def write(which):
        keys, rows = apart(which, slots, side)
        for d in range(side):
            put_keys(keys[d], k, v, mine if d % 2 == 0 else 1 - mine)
        for unit in range(len(rows)):
            put_rows(rows[unit], q, do, k.shape[1] // 2, unit)

    by_class(write)


def pack_kernel(n_mixed, q, do, o, sums, k, v, _, near_same, near_other, rest, stat_own):
    tokens, width = do.shape
    heads = sums.shape[0]
    part = k.shape[1] // 2
    n = heads // 2
    put_keys(near_same, k, v, parity())
    put_keys(near_other, k, v, 1 - parity())
    for unit in range(n_mixed, width // 2 // part):
        put_rows(rest, q, do, part, unit, (unit - n_mixed) * 2 * part)

    row = lax.broadcasted_iota(jnp.int32, (heads, width), 0)
    col = lax.broadcasted_iota(jnp.int32, (heads, width), 1)
    pick = jnp.where(col // HEAD_DIM == row, 1.0, 0.0).astype(BF16)
    prod = do[...].astype(F32) * o[...].astype(F32)
    high = prod.astype(BF16)
    low = (prod - high.astype(F32)).astype(BF16)
    delta = dot(pick, high, 1, 1) + dot(pick, low, 1, 1)
    lse = sums[...] * LOG2E

    def write_stats(mine, other):
        stat_own[:n, :] = lse[mine * n : (mine + 1) * n, :]
        stat_own[n:, :] = delta[mine * n : (mine + 1) * n, :]
        left = jnp.concatenate([x[other * n : (other + 1) * n, :] for x in (lse, delta)], 0)
        terms = []
        for _ in range(3):
            term = left.astype(BF16).astype(F32)
            left = left - term
            terms.append(term)
        terms.append(jnp.zeros((LANES - 6 * n, tokens), F32))
        rest[:, rest.shape[1] - LANES :] = jnp.transpose(jnp.concatenate(terms, 0)).astype(BF16)

    by_parity(write_stats)


def stack_heads(load, first, group):
    blocks = []
    for pair in range(group // 2):
        two = load((first + 2 * pair) * HEAD_DIM, 2 * HEAD_DIM)
        blocks += [two[:, :HEAD_DIM], two[:, HEAD_DIM:]]
    return jnp.concatenate(blocks, 0)


def stack_stats(stats, first, group):
    return jnp.concatenate([stats[first + g : first + g + 1] for g in range(group)], 1)


def head_grads(q, do, lse, delta, k, v):
    scores = dot(k, q, 1, 1)
    dprobs = dot(v, do, 1, 1)
    probs = jnp.exp2(scores * (LOG2E / math.sqrt(HEAD_DIM)) - lse)
    dscores = (probs * (dprobs - delta)).astype(BF16)
    dv = dot(probs.astype(BF16), do, 1, 0)
    dk = dot(dscores, q, 1, 0)
    dq = dot(k, dscores, 0, 0)
    return dk, dv, dq


def side_grads(pairs, load_q, load_do, load_stats, kv, put):
    part = kv.shape[1] // 2
    width = 2 * HEAD_DIM
    for pair in pairs:
        at = pair * width
        k_two, v_two = kv[:, at : at + width], kv[:, part + at : part + at + width]
        dks, dvs = [], []
        for odd in range(2):
            first = (2 * pair + odd) * put.group
            lanes = slice(odd * HEAD_DIM, (odd + 1) * HEAD_DIM)
            dk, dv, dq = head_grads(
                stack_heads(load_q, first, put.group),
                stack_heads(load_do, first, put.group),
                *load_stats(first),
                k_two[:, lanes],
                v_two[:, lanes],
            )
            dks.append(dk)
            dvs.append(dv)
            put(first, dq)
        put.store(at, jnp.concatenate(dks, 1), jnp.concatenate(dvs, 1))


class Put:
    def __init__(self, dq_acc, group, store):
        self.dq_acc, self.group, self.store = dq_acc, group, store

    def __call__(self, first, dq):
        tok = self.dq_acc.shape[1]
        for g in range(self.group):
            rows = slice((first + g) * HEAD_DIM, (first + g + 1) * HEAD_DIM)
            self.dq_acc[rows, :] += dq[:, g * tok : (g + 1) * tok]


def turned_dq(dq_acc, first, last):
    factor = 1.0 / math.sqrt(HEAD_DIM)
    blocks = [
        jnp.transpose(dq_acc[at : at + LANES, :])
        for at in range(first * HEAD_DIM, last * HEAD_DIM, LANES)
    ]
    return (jnp.concatenate(blocks, 1) * factor).astype(BF16)


def seen(flags, which):
    return jnp.max(flags[which : which + 1, :]) > 0


def seen_sides(owners, shards):
    rank, z = lax.axis_index("blk"), lax.axis_index("ulysses")
    n_blk = lax.axis_size("blk")
    before = lax.rem(rank + n_blk - 1, n_blk)
    place = lax.div(z, shards // 2)
    mine = owners[2 * rank + place]
    return mine > owners[2 * before + place], mine > owners[2 * before + 1 - place]


def own_loaders(q, do, stats, group):
    heads = stats.shape[0] // 2
    half = heads * HEAD_DIM
    mine = parity()

    def from_half(ref):
        def load(at, size):
            return ref[:, pl.ds(pl.multiple_of(mine * half + at, size), size)]

        return load

    def load_stats(first):
        every = stats[...]
        return stack_stats(every, first, group), stack_stats(every, heads + first, group)

    return from_half(q), from_half(do), load_stats


def partner_loaders(q_in, rest, part, heads):
    tok, kv_width = rest.shape[0], 2 * part
    n_mixed = q_in.shape[0] // tok

    def loader(offset):
        def load(at, size):
            unit, lane = at // part, offset + at % part
            if unit < n_mixed:
                return q_in[unit * tok : (unit + 1) * tok, lane : lane + size]
            lane += (unit - n_mixed) * kv_width
            return rest[:, lane : lane + size]

        return load

    def load_stats(first):
        terms = jnp.transpose(rest[:, rest.shape[1] - LANES :].astype(F32))
        n = 2 * heads
        every = terms[:n] + terms[n : 2 * n] + terms[2 * n : 3 * n]
        group = part // HEAD_DIM
        return stack_stats(every, first, group), stack_stats(every, heads + first, group)

    return loader(0), loader(part), load_stats


def finish(outs, acc, at, dk, dv):
    part, tok = acc.shape[1] // 2, outs[0].shape[0]
    dk = (dk + acc[:, at : at + LANES]) * (1.0 / math.sqrt(HEAD_DIM))
    dv = dv + acc[:, part + at : part + at + LANES]
    for d, out in enumerate(outs):
        rows = slice(d * tok, (d + 1) * tok)
        out[:, at : at + LANES] = dk[rows].astype(BF16)
        out[:, part + at : part + at + LANES] = dv[rows].astype(BF16)


def own_far_kernel(side, owners, q, do, stats, *rest):
    slots = rest[:-5]
    kv, q_in, acc, dq_acc, flags = rest[-5:]
    near_seen, far_seen = seen_sides(owners, 2 * side)
    line = lax.broadcasted_iota(jnp.int32, flags.shape, 0)
    flags[...] = jnp.where(line == 0, near_seen.astype(jnp.int32), far_seen.astype(jnp.int32))
    tok, part = q.shape[0], kv.shape[1] // 2

    def sort(which):
        keys, rows = apart(which, slots, side)
        for d in range(side):
            kv[d * tok : (d + 1) * tok, :] = keys[d][...]
        for unit in range(len(rows)):
            q_in[unit * tok : (unit + 1) * tok, :] = rows[unit][...]

    by_class(sort)
    dq_acc[...] = jnp.zeros_like(dq_acc)

    def store(at, dk, dv):
        acc[:, at : at + LANES] = dk
        acc[:, part + at : part + at + LANES] = dv

    @pl.when(far_seen)
    def _():
        group = part // HEAD_DIM
        loaders = own_loaders(q, do, stats, group)
        side_grads(range(part // LANES), *loaders, kv, Put(dq_acc, group, store))


def partner_far_kernel(flags, q_in, rest, kv, acc, *outs):
    far, dq_acc = outs[:-1], outs[-1]
    tok, part = rest.shape[0], kv.shape[1] // 2
    dq_acc[...] = jnp.zeros_like(dq_acc)

    def store(at, dk, dv):
        finish(far, acc, at, dk, dv)

    @pl.when(seen(flags, 1))
    def _():
        loaders = partner_loaders(q_in, rest, part, dq_acc.shape[0] // HEAD_DIM)
        side_grads(range(part // LANES), *loaders, kv, Put(dq_acc, part // HEAD_DIM, store))

    @pl.when(jnp.logical_not(seen(flags, 1)))
    def _():
        for out in far:
            out[...] = jnp.zeros_like(out)


def partner_near_kernel(side, flags, q_in, rest, partner_dq, *refs):
    keys, refs = refs[:side], refs[side:]
    kv, acc, dq_acc = refs[-3:]
    tok, part = rest.shape[0], kv.shape[1] // 2
    heads = dq_acc.shape[0] // HEAD_DIM
    group = part // HEAD_DIM
    n_late = (len(refs) - 4) // 2
    far, far_out, dq_send = refs[:n_late], refs[n_late : 2 * n_late], refs[-4]
    dq_acc[...] = partner_dq[...]

    @pl.when(seen(flags, 0))
    def _():
        for d in range(side):
            kv[d * tok : (d + 1) * tok, :] = keys[d][...]

        def store(at, dk, dv):
            acc[:, at : at + LANES] = dk
            acc[:, part + at : part + at + LANES] = dv

        loaders = partner_loaders(q_in, rest, part, heads)
        side_grads(range(part // LANES), *loaders, kv, Put(dq_acc, group, store))

    for out, ref in zip(far_out, far):
        out[...] = ref[...]
    dq_send[...] = turned_dq(dq_acc, 0, heads)


def own_near_kernel(flags, q, do, stats, kv, acc, own_dq, *outs):
    *near, dq_own, dq_acc = outs
    part = kv.shape[1] // 2
    group = part // HEAD_DIM
    dq_acc[...] = own_dq[...]

    @pl.when(seen(flags, 0))
    def _():
        def store(at, dk, dv):
            finish(near, acc, at, dk, dv)

        loaders = own_loaders(q, do, stats, group)
        side_grads(range(part // LANES), *loaders, kv, Put(dq_acc, group, store))

    @pl.when(jnp.logical_not(seen(flags, 0)))
    def _():
        for out in near:
            out[...] = jnp.zeros_like(out)

    dq_own[...] = turned_dq(dq_acc, 0, dq_acc.shape[0] // HEAD_DIM)


def take_kernel(count, *refs):
    for ref, out in zip(refs[:count], refs[-count:]):
        out[...] = ref[...].astype(out.dtype)


def join_kernel(side, dq_own, *refs):
    far, dq_back, near = refs[: 2 * side], refs[2 * side], refs[2 * side + 1 : -3][::-1]
    gq, gk, gv = refs[-3:]
    half = dq_own.shape[1]
    part = gk.shape[1] // 2
    totals = []
    for odd in range(2):
        terms = [*near[odd::2], *far[odd::2]]
        totals.append(sum((ref[...].astype(F32) for ref in terms[1:]), terms[0][...].astype(F32)))

    def write(mine, other):
        gq[:, mine * half : (mine + 1) * half] = dq_own[...]
        gq[:, other * half : (other + 1) * half] = dq_back[...]
        for total, place in zip(totals, (mine, other)):
            gk[:, place * part : (place + 1) * part] = total[:, :part].astype(BF16)
            gv[:, place * part : (place + 1) * part] = total[:, part:].astype(BF16)

    by_parity(write)


def limit(mib):
    return pltpu.CompilerParams(vmem_limit_bytes=int(mib * 1024 * 1024))


def per_device(queries, key_states, value_states, attn_out, grad_out, log_sums, owners):
    n_blk, n_uly = lax.axis_size("blk"), lax.axis_size("ulysses")
    tok, width = queries.shape
    heads = log_sums.shape[1]
    kv_width = key_states.shape[1]
    half = width // 2
    side = n_uly // 2

    n_units = width // kv_width
    n_mixed = min(n_units, side)

    def flips(first, second):
        return [in_turn(which, first, second) for which in range(2)]

    def outer(u):
        return (u < side) == (u % 2 == 0)

    def move(value, *by_kind, places=range(n_uly)):
        pairs = []
        for b in range(n_blk):
            for u in places:
                step, flip = by_kind[(b + u // side) % len(by_kind)]
                pairs.append((b * n_uly + u, ((b + step) % n_blk) * n_uly + (u ^ flip)))
        return lax.ppermute(value, ("blk", "ulysses"), pairs)

    def shape(*dims, dtype=BF16):
        return jax.ShapeDtypeStruct(dims, dtype)

    def cover(flops):
        return pl.CostEstimate(flops=flops, bytes_accessed=1 << 20, transcendentals=0)

    unit = shape(tok, kv_width)
    sides = shape(side * tok, kv_width)
    sides_wide = shape(side * tok, kv_width, dtype=F32)
    dq_wide = shape(half, tok, dtype=F32)
    *slots, ready = pl.pallas_call(
        functools.partial(pack_turns_kernel, side),
        out_shape=[unit] * (side + n_mixed) + [shape(8, LANES, dtype=F32)],
        in_specs=[VMEM] * 4,
        out_specs=[VMEM] * (side + n_mixed + 1),
        compiler_params=limit(TURNS_MIB),
        name="pack_turns",
    )(queries, grad_out, key_states, value_states)
    near_same, near_other, rest, stat_own = pl.pallas_call(
        functools.partial(pack_kernel, n_mixed),
        out_shape=[unit] * 2
        + [
            shape(tok, (n_units - n_mixed) * kv_width + LANES),
            shape(heads, tok, dtype=F32),
        ],
        in_specs=[VMEM] * 6 + [ANY],
        out_specs=[VMEM] * 4,
        compiler_params=limit(PACK_MIB),
        name="pack",
    )(
        queries, grad_out, attn_out, jnp.transpose(log_sums), key_states, value_states, ready
    )
    turns = flips([(1, d) for d in range(side, n_uly)], [(0, 1)] * n_mixed)
    slots = [move(x, one, two) for x, one, two in zip(slots, *turns)]
    rest = move(rest, (0, 1))
    near = [move(near_other if d % 2 else near_same, (1, d)) for d in range(side)]
    outs = [sides, shape(n_mixed * tok, kv_width), sides_wide, dq_wide]
    outs.append(shape(8, LANES, dtype=jnp.int32))
    kv_far, q_in, acc_far, own_dq, flags = pl.pallas_call(
        functools.partial(own_far_kernel, side),
        out_shape=outs,
        in_specs=[SMEM] + [VMEM] * (3 + side + n_mixed),
        out_specs=[VMEM] * len(outs),
        compiler_params=limit(32),
        cost_estimate=cover(OWN),
        name="own_far",
    )(owners, queries, grad_out, stat_own, *slots)
    *far, partner_dq = pl.pallas_call(
        partner_far_kernel,
        out_shape=[unit] * side + [dq_wide],
        in_specs=[VMEM] * 5,
        out_specs=[VMEM] * (side + 1),
        compiler_params=limit(32),
        cost_estimate=cover(PARTNER),
        name="far",
    )(flags, q_in, rest, kv_far, acc_far)
    ends = [u for u in range(n_uly) if outer(u)]
    inner = [u for u in range(n_uly) if not outer(u)]
    early = [move(x, (-1, side + d), places=ends) for d, x in enumerate(far)]
    outs = [unit] * side + [shape(tok, half), sides, sides_wide]
    *late, dq_back, kv_near, acc_near = pl.pallas_call(
        functools.partial(partner_near_kernel, side),
        out_shape=outs,
        in_specs=[VMEM] * (4 + 2 * side),
        out_specs=[VMEM] * len(outs),
        scratch_shapes=[pltpu.VMEM(dq_wide.shape, F32)],
        compiler_params=limit(32),
        cost_estimate=cover(PARTNER),
        name="near",
    )(flags, q_in, rest, partner_dq, *near, *far)
    dq_back = move(dq_back, (0, 1))
    late = [move(x, (-1, side + d), places=inner) for d, x in enumerate(late)]
    outs = [unit] * side + [shape(tok, half)]
    *near, dq_own = pl.pallas_call(
        own_near_kernel,
        out_shape=outs,
        in_specs=[VMEM] * 7,
        out_specs=[VMEM] * len(outs),
        scratch_shapes=[pltpu.VMEM(dq_wide.shape, F32)],
        compiler_params=limit(32),
        cost_estimate=cover(NONE),
        name="own_near",
    )(flags, queries, grad_out, stat_own, kv_near, acc_near, own_dq)
    near = [move(near[d], (-1, d)) for d in reversed(range(side))][::-1]

    def take(first, outs, flops, *after):
        return pl.pallas_call(
            functools.partial(take_kernel, len(first)),
            out_shape=outs,
            in_specs=[VMEM] * len(first) + [ANY] * len(after),
            out_specs=[VMEM] * len(first),
            compiler_params=limit(8),
            cost_estimate=cover(flops),
            name="take",
        )(*first, *after)

    wide = shape(tok, kv_width, dtype=F32)
    early = take(early, [wide] * side, SHORT)
    late = take(late, [wide] * side, SHORT, early[0])
    (dq_back,) = take([dq_back], [shape(tok, half)], LONG, late[0])
    ins = [dq_own, *early, *late, dq_back, *near[::-1]]
    return tuple(
        pl.pallas_call(
            functools.partial(join_kernel, side),
            out_shape=[shape(tok, width), shape(tok, kv_width), shape(tok, kv_width)],
            in_specs=[VMEM] * len(ins),
            out_specs=[VMEM] * 3,
            compiler_params=limit(8),
            name="join",
        )(*ins)
    )


def solution(mesh):
    rows = P(("blk", "ulysses"), None)
    return jax.shard_map(
        per_device,
        mesh=mesh,
        in_specs=(rows, rows, rows, rows, rows, rows, P()),
        out_specs=(rows, rows, rows),
        check_vma=False,
    )
```

```python
import functools
import math

import jax
import jax.numpy as jnp
from jax import lax
from jax.experimental import pallas as pl
from jax.experimental.pallas import tpu as pltpu
from jax.sharding import PartitionSpec as P

HEAD_DIM = 64
LANES = 128
PACK_MIB = 60
FIRST_MIB = 60
NONE, SHORT, OWN, PARTNER, LONG = 1 << 20, 7 << 27, 1 << 31, 1 << 31, 1 << 34
LOG2E = math.log2(math.e)
BF16 = jnp.bfloat16
F32 = jnp.float32
ANY = pl.BlockSpec(memory_space=pl.ANY)
VMEM = pl.BlockSpec(memory_space=pltpu.VMEM)
SMEM = pl.BlockSpec(memory_space=pltpu.SMEM)


def dot(a, b, a_dim, b_dim):
    return lax.dot_general(
        a, b, (((a_dim,), (b_dim,)), ((), ())), preferred_element_type=F32
    )


def parity():
    return lax.rem(lax.axis_index("ulysses"), 2)


def by_parity(write):
    for mine in range(2):

        @pl.when(parity() == mine)
        def _():
            write(mine, 1 - mine)


def cut(ref, which, size, at=0, wide=None):
    wide = size if wide is None else wide
    return ref[:, pl.ds(pl.multiple_of(which * size + at, wide), wide)]


def put_keys(out, k, v, which):
    part = k.shape[1] // 2
    out[:, :part] = cut(k, which, part)
    out[:, part:] = cut(v, which, part)


def pack_first_kernel(q, do, o, sums, qd_send, stat_own, ready):
    tokens, width = do.shape
    heads = sums.shape[0]
    half = width // 2
    n = heads // 2
    other = 1 - parity()
    qd_send[:, :half] = cut(q, other, half)
    qd_send[:, half:width] = cut(do, other, half)
    row = lax.broadcasted_iota(jnp.int32, (heads, width), 0)
    col = lax.broadcasted_iota(jnp.int32, (heads, width), 1)
    pick = jnp.where(col // HEAD_DIM == row, 1.0, 0.0).astype(BF16)
    prod = do[...].astype(F32) * o[...].astype(F32)
    high = prod.astype(BF16)
    low = (prod - high.astype(F32)).astype(BF16)
    delta = dot(pick, high, 1, 1) + dot(pick, low, 1, 1)
    lse = sums[...] * LOG2E

    def write_stats(mine, theirs):
        stat_own[:n, :] = lse[mine * n : (mine + 1) * n, :]
        stat_own[n:, :] = delta[mine * n : (mine + 1) * n, :]
        left = jnp.concatenate([x[theirs * n : (theirs + 1) * n, :] for x in (lse, delta)], 0)
        terms = []
        for _ in range(3):
            term = left.astype(BF16).astype(F32)
            left = left - term
            terms.append(term)
        terms.append(jnp.zeros((LANES - 6 * n, tokens), F32))
        qd_send[:, width:] = jnp.transpose(jnp.concatenate(terms, 0)).astype(BF16)

    by_parity(write_stats)
    ready[...] = jnp.zeros_like(ready)


def pack_kernel(k, v, _, same, other):
    put_keys(same, k, v, parity())
    put_keys(other, k, v, 1 - parity())


def stack_heads(load, first, group):
    blocks = []
    for pair in range(group // 2):
        two = load((first + 2 * pair) * HEAD_DIM, 2 * HEAD_DIM)
        blocks += [two[:, :HEAD_DIM], two[:, HEAD_DIM:]]
    return jnp.concatenate(blocks, 0)


def stack_stats(stats, first, group):
    return jnp.concatenate([stats[first + g : first + g + 1] for g in range(group)], 1)


def head_grads(q, do, lse, delta, k, v):
    scores = dot(k, q, 1, 1)
    dprobs = dot(v, do, 1, 1)
    probs = jnp.exp2(scores * (LOG2E / math.sqrt(HEAD_DIM)) - lse)
    dscores = (probs * (dprobs - delta)).astype(BF16)
    dv = dot(probs.astype(BF16), do, 1, 0)
    dk = dot(dscores, q, 1, 0)
    dq = dot(k, dscores, 0, 0)
    return dk, dv, dq


def side_grads(pairs, load_q, load_do, load_stats, kv, put):
    part = kv.shape[1] // 2
    width = 2 * HEAD_DIM
    for pair in pairs:
        at = pair * width
        k_two, v_two = kv[:, at : at + width], kv[:, part + at : part + at + width]
        dks, dvs = [], []
        for odd in range(2):
            first = (2 * pair + odd) * put.group
            lanes = slice(odd * HEAD_DIM, (odd + 1) * HEAD_DIM)
            dk, dv, dq = head_grads(
                stack_heads(load_q, first, put.group),
                stack_heads(load_do, first, put.group),
                *load_stats(first),
                k_two[:, lanes],
                v_two[:, lanes],
            )
            dks.append(dk)
            dvs.append(dv)
            put(first, dq)
        put.store(at, jnp.concatenate(dks, 1), jnp.concatenate(dvs, 1))


class Put:
    def __init__(self, dq_acc, group, store):
        self.dq_acc, self.group, self.store = dq_acc, group, store

    def __call__(self, first, dq):
        tok = self.dq_acc.shape[1]
        for g in range(self.group):
            rows = slice((first + g) * HEAD_DIM, (first + g + 1) * HEAD_DIM)
            self.dq_acc[rows, :] += dq[:, g * tok : (g + 1) * tok]


def turned_dq(dq_acc, first, last):
    factor = 1.0 / math.sqrt(HEAD_DIM)
    blocks = [
        jnp.transpose(dq_acc[at : at + LANES, :])
        for at in range(first * HEAD_DIM, last * HEAD_DIM, LANES)
    ]
    return (jnp.concatenate(blocks, 1) * factor).astype(BF16)


def seen(flags, which):
    return jnp.max(flags[which : which + 1, :]) > 0


def seen_sides(owners, shards):
    rank, z = lax.axis_index("blk"), lax.axis_index("ulysses")
    n_blk = lax.axis_size("blk")
    before = lax.rem(rank + n_blk - 1, n_blk)
    place = lax.div(z, shards // 2)
    mine = owners[2 * rank + place]
    return mine > owners[2 * before + place], mine > owners[2 * before + 1 - place]


def loaders(q, do, stats, group, at_half=None):
    heads = stats.shape[0] // 2
    half = heads * HEAD_DIM

    def of(ref, offset):
        def load(at, size):
            if at_half is None:
                return ref[:, offset + at : offset + at + size]
            return ref[:, pl.ds(pl.multiple_of(at_half * half + at, size), size)]

        return load

    def load_stats(first):
        every = stats[...]
        return stack_stats(every, first, group), stack_stats(every, heads + first, group)

    return of(q, 0), of(do, half), load_stats


def own_loaders(q, do, stats, group):
    return loaders(q, do, stats, group, parity())


def partner_loaders(qd, group):
    terms = jnp.transpose(qd[:, qd.shape[1] - LANES :].astype(F32))
    n = (qd.shape[1] - LANES) // HEAD_DIM
    return loaders(qd, qd, terms[:n] + terms[n : 2 * n] + terms[2 * n : 3 * n], group)


def finish(outs, acc, at, dk, dv):
    part, tok = acc.shape[1] // 2, outs[0].shape[0]
    dk = (dk + acc[:, at : at + LANES]) * (1.0 / math.sqrt(HEAD_DIM))
    dv = dv + acc[:, part + at : part + at + LANES]
    for d, out in enumerate(outs):
        rows = slice(d * tok, (d + 1) * tok)
        out[:, at : at + LANES] = dk[rows].astype(BF16)
        out[:, part + at : part + at + LANES] = dv[rows].astype(BF16)


def own_far_kernel(side, owners, q, do, stats, *rest):
    keys = rest[:side]
    kv, acc, dq_acc, flags = rest[side:]
    near_seen, far_seen = seen_sides(owners, 2 * side)
    line = lax.broadcasted_iota(jnp.int32, flags.shape, 0)
    flags[...] = jnp.where(line == 0, near_seen.astype(jnp.int32), far_seen.astype(jnp.int32))
    tok, part = q.shape[0], kv.shape[1] // 2
    for d in range(side):
        kv[d * tok : (d + 1) * tok, :] = keys[d][...]
    dq_acc[...] = jnp.zeros_like(dq_acc)

    def store(at, dk, dv):
        acc[:, at : at + LANES] = dk
        acc[:, part + at : part + at + LANES] = dv

    @pl.when(far_seen)
    def _():
        group = part // HEAD_DIM
        loads = own_loaders(q, do, stats, group)
        side_grads(range(part // LANES), *loads, kv, Put(dq_acc, group, store))


def partner_far_kernel(flags, qd, kv, acc, *outs):
    far, dq_acc = outs[:-1], outs[-1]
    part = kv.shape[1] // 2
    group = part // HEAD_DIM
    dq_acc[...] = jnp.zeros_like(dq_acc)

    def store(at, dk, dv):
        finish(far, acc, at, dk, dv)

    @pl.when(seen(flags, 1))
    def _():
        loads = partner_loaders(qd, group)
        side_grads(range(part // LANES), *loads, kv, Put(dq_acc, group, store))

    @pl.when(jnp.logical_not(seen(flags, 1)))
    def _():
        for out in far:
            out[...] = jnp.zeros_like(out)


def partner_near_kernel(side, flags, qd, partner_dq, *refs):
    keys, refs = refs[:side], refs[side:]
    kv, acc, dq_acc = refs[-3:]
    tok, part = qd.shape[0], kv.shape[1] // 2
    heads = dq_acc.shape[0] // HEAD_DIM
    group = part // HEAD_DIM
    n_late = (len(refs) - 4) // 2
    far, far_out, dq_send = refs[:n_late], refs[n_late : 2 * n_late], refs[-4]
    dq_acc[...] = partner_dq[...]

    @pl.when(seen(flags, 0))
    def _():
        for d in range(side):
            kv[d * tok : (d + 1) * tok, :] = keys[d][...]

        def store(at, dk, dv):
            acc[:, at : at + LANES] = dk
            acc[:, part + at : part + at + LANES] = dv

        loads = partner_loaders(qd, group)
        side_grads(range(part // LANES), *loads, kv, Put(dq_acc, group, store))

    for out, ref in zip(far_out, far):
        out[...] = ref[...]
    dq_send[...] = turned_dq(dq_acc, 0, heads)


def own_near_kernel(flags, q, do, stats, kv, acc, own_dq, *outs):
    *near, dq_own, dq_acc = outs
    part = kv.shape[1] // 2
    group = part // HEAD_DIM
    dq_acc[...] = own_dq[...]

    @pl.when(seen(flags, 0))
    def _():
        def store(at, dk, dv):
            finish(near, acc, at, dk, dv)

        loads = own_loaders(q, do, stats, group)
        side_grads(range(part // LANES), *loads, kv, Put(dq_acc, group, store))

    @pl.when(jnp.logical_not(seen(flags, 0)))
    def _():
        for out in near:
            out[...] = jnp.zeros_like(out)

    dq_own[...] = turned_dq(dq_acc, 0, dq_acc.shape[0] // HEAD_DIM)


def take_kernel(count, *refs):
    for ref, out in zip(refs[:count], refs[-count:]):
        out[...] = ref[...].astype(out.dtype)


def join_kernel(side, dq_own, *refs):
    far, dq_back, near = refs[:side], refs[side], refs[side + 1 : -3][::-1]
    gq, gk, gv = refs[-3:]
    half = dq_own.shape[1]
    part = gk.shape[1] // 2
    totals = []
    for odd in range(2):
        terms = [*near[odd::2], *far[odd::2]]
        totals.append(sum((ref[...].astype(F32) for ref in terms[1:]), terms[0][...].astype(F32)))

    def write(mine, other):
        gq[:, mine * half : (mine + 1) * half] = dq_own[...]
        gq[:, other * half : (other + 1) * half] = dq_back[...]
        for total, place in zip(totals, (mine, other)):
            gk[:, place * part : (place + 1) * part] = total[:, :part].astype(BF16)
            gv[:, place * part : (place + 1) * part] = total[:, part:].astype(BF16)

    by_parity(write)


def limit(mib):
    return pltpu.CompilerParams(vmem_limit_bytes=int(mib * 1024 * 1024))


def per_device(queries, key_states, value_states, attn_out, grad_out, log_sums, owners):
    n_blk, n_uly = lax.axis_size("blk"), lax.axis_size("ulysses")
    tok, width = queries.shape
    heads = log_sums.shape[1]
    kv_width = key_states.shape[1]
    half = width // 2
    side = n_uly // 2

    def move(value, step, flip):
        pairs = []
        for b in range(n_blk):
            for u in range(n_uly):
                pairs.append((b * n_uly + u, ((b + step) % n_blk) * n_uly + (u ^ flip)))
        return lax.ppermute(value, ("blk", "ulysses"), pairs)

    def shape(*dims, dtype=BF16):
        return jax.ShapeDtypeStruct(dims, dtype)

    def cover(flops):
        return pl.CostEstimate(flops=flops, bytes_accessed=1 << 20, transcendentals=0)

    unit = shape(tok, kv_width)
    sides = shape(side * tok, kv_width)
    sides_wide = shape(side * tok, kv_width, dtype=F32)
    dq_wide = shape(half, tok, dtype=F32)
    qd_send, stat_own, ready = pl.pallas_call(
        pack_first_kernel,
        out_shape=[
            shape(tok, width + LANES),
            shape(heads, tok, dtype=F32),
            shape(8, LANES, dtype=F32),
        ],
        in_specs=[VMEM] * 4,
        out_specs=[VMEM] * 3,
        compiler_params=limit(FIRST_MIB),
        name="pack_first",
    )(queries, grad_out, attn_out, jnp.transpose(log_sums))
    same, other = pl.pallas_call(
        pack_kernel,
        out_shape=[unit] * 2,
        in_specs=[VMEM] * 2 + [ANY],
        out_specs=[VMEM] * 2,
        compiler_params=limit(PACK_MIB),
        name="pack",
    )(key_states, value_states, ready)
    qd_in = move(qd_send, 0, 1)
    far = [move(other if d % 2 else same, 1, d) for d in range(side, n_uly)]
    near = [move(other if d % 2 else same, 1, d) for d in range(side)]
    kv_far, acc_far, own_dq, flags = pl.pallas_call(
        functools.partial(own_far_kernel, side),
        out_shape=[sides, sides_wide, dq_wide, shape(8, LANES, dtype=jnp.int32)],
        in_specs=[SMEM] + [VMEM] * (3 + side),
        out_specs=[VMEM] * 4,
        compiler_params=limit(32),
        cost_estimate=cover(OWN),
        name="own_far",
    )(owners, queries, grad_out, stat_own, *far)
    *far, partner_dq = pl.pallas_call(
        partner_far_kernel,
        out_shape=[unit] * side + [dq_wide],
        in_specs=[VMEM] * 4,
        out_specs=[VMEM] * (side + 1),
        compiler_params=limit(32),
        cost_estimate=cover(PARTNER),
        name="far",
    )(flags, qd_in, kv_far, acc_far)
    n_early = side // 2
    n_late = side - n_early
    early = [move(x, -1, side + d) for d, x in enumerate(far[:n_early])]
    outs = [unit] * n_late + [shape(tok, half), sides, sides_wide]
    *late, dq_back, kv_near, acc_near = pl.pallas_call(
        functools.partial(partner_near_kernel, side),
        out_shape=outs,
        in_specs=[VMEM] * (3 + side + n_late),
        out_specs=[VMEM] * len(outs),
        scratch_shapes=[pltpu.VMEM(dq_wide.shape, F32)],
        compiler_params=limit(32),
        cost_estimate=cover(PARTNER),
        name="near",
    )(flags, qd_in, partner_dq, *near, *far[n_early:])
    late = [move(x, -1, side + n_early + d) for d, x in enumerate(late)]
    dq_back = move(dq_back, 0, 1)
    outs = [unit] * side + [shape(tok, half)]
    *near, dq_own = pl.pallas_call(
        own_near_kernel,
        out_shape=outs,
        in_specs=[VMEM] * 7,
        out_specs=[VMEM] * len(outs),
        scratch_shapes=[pltpu.VMEM(dq_wide.shape, F32)],
        compiler_params=limit(32),
        cost_estimate=cover(NONE),
        name="own_near",
    )(flags, queries, grad_out, stat_own, kv_near, acc_near, own_dq)
    near = [move(near[d], -1, d) for d in reversed(range(side))][::-1]

    def take(first, outs, flops, *after):
        return pl.pallas_call(
            functools.partial(take_kernel, len(first)),
            out_shape=outs,
            in_specs=[VMEM] * len(first) + [ANY] * len(after),
            out_specs=[VMEM] * len(first),
            compiler_params=limit(8),
            cost_estimate=cover(flops),
            name="take",
        )(*first, *after)

    wide = shape(tok, kv_width, dtype=F32)
    early = take(early, [wide] * n_early, SHORT)
    late = take(late, [wide] * n_late, SHORT, early[0])
    (dq_back,) = take([dq_back], [shape(tok, half)], LONG, late[0])
    ins = [dq_own, *early, *late, dq_back, *near[::-1]]
    return tuple(
        pl.pallas_call(
            functools.partial(join_kernel, side),
            out_shape=[shape(tok, width), shape(tok, kv_width), shape(tok, kv_width)],
            in_specs=[VMEM] * len(ins),
            out_specs=[VMEM] * 3,
            compiler_params=limit(8),
            name="join",
        )(*ins)
    )


def solution(mesh):
    rows = P(("blk", "ulysses"), None)
    return jax.shard_map(
        per_device,
        mesh=mesh,
        in_specs=(rows, rows, rows, rows, rows, rows, P()),
        out_specs=(rows, rows, rows),
        check_vma=False,
    )
```

```python
import functools
import math

import jax
import jax.numpy as jnp
from jax import lax
from jax.experimental import pallas as pl
from jax.experimental.pallas import tpu as pltpu
from jax.sharding import PartitionSpec as P

HEAD_DIM = 64
LANES = 128
PACK_MIB = 60
TURNS_MIB = 53.4
NONE, SHORT, OWN, PARTNER, LONG = 1 << 20, 7 << 27, 1 << 31, 1 << 31, 1 << 34
LOG2E = math.log2(math.e)
BF16 = jnp.bfloat16
F32 = jnp.float32
ANY = pl.BlockSpec(memory_space=pl.ANY)
VMEM = pl.BlockSpec(memory_space=pltpu.VMEM)
SMEM = pl.BlockSpec(memory_space=pltpu.SMEM)


def dot(a, b, a_dim, b_dim):
    return lax.dot_general(
        a, b, (((a_dim,), (b_dim,)), ((), ())), preferred_element_type=F32
    )


def parity():
    return lax.rem(lax.axis_index("ulysses"), 2)


def by_parity(write):
    for mine in range(2):

        @pl.when(parity() == mine)
        def _():
            write(mine, 1 - mine)


def by_class(write):
    side = lax.div(lax.axis_index("ulysses"), lax.axis_size("ulysses") // 2)
    odd = lax.rem(lax.axis_index("blk") + side, 2)
    for which in range(2):

        @pl.when(odd == which)
        def _():
            write(which)


def in_turn(which, first, second):
    return [*first, *second] if which == 0 else [*second, *first]


def apart(which, refs, n_first):
    n_second = len(refs) - n_first
    if which == 0:
        return refs[:n_first], refs[n_first:]
    return refs[n_second:], refs[:n_second]


def cut(ref, which, size, at=0, wide=None):
    wide = size if wide is None else wide
    return ref[:, pl.ds(pl.multiple_of(which * size + at, wide), wide)]


def put_keys(out, k, v, which):
    part = k.shape[1] // 2
    out[:, :part] = cut(k, which, part)
    out[:, part:] = cut(v, which, part)


def put_rows(out, q, do, part, unit, at=0):
    half = q.shape[1] // 2
    other = 1 - parity()
    out[:, at : at + part] = cut(q, other, half, unit * part, part)
    out[:, at + part : at + 2 * part] = cut(do, other, half, unit * part, part)


def pack_turns_kernel(side, q, do, k, v, *slots):
    *slots, ready = slots
    ready[...] = jnp.zeros_like(ready)
    mine = parity()

    def write(which):
        keys, rows = apart(which, slots, side)
        for d in range(side):
            put_keys(keys[d], k, v, mine if d % 2 == 0 else 1 - mine)
        for unit in range(len(rows)):
            put_rows(rows[unit], q, do, k.shape[1] // 2, unit)

    by_class(write)


def pack_kernel(n_mixed, q, do, o, sums, k, v, _, near_same, near_other, rest, stat_own):
    tokens, width = do.shape
    heads = sums.shape[0]
    part = k.shape[1] // 2
    n = heads // 2
    put_keys(near_same, k, v, parity())
    put_keys(near_other, k, v, 1 - parity())
    for unit in range(n_mixed, width // 2 // part):
        put_rows(rest, q, do, part, unit, (unit - n_mixed) * 2 * part)

    row = lax.broadcasted_iota(jnp.int32, (heads, width), 0)
    col = lax.broadcasted_iota(jnp.int32, (heads, width), 1)
    pick = jnp.where(col // HEAD_DIM == row, 1.0, 0.0).astype(BF16)
    prod = do[...].astype(F32) * o[...].astype(F32)
    high = prod.astype(BF16)
    low = (prod - high.astype(F32)).astype(BF16)
    delta = dot(pick, high, 1, 1) + dot(pick, low, 1, 1)
    lse = sums[...] * LOG2E

    def write_stats(mine, other):
        stat_own[:n, :] = lse[mine * n : (mine + 1) * n, :]
        stat_own[n:, :] = delta[mine * n : (mine + 1) * n, :]
        left = jnp.concatenate([x[other * n : (other + 1) * n, :] for x in (lse, delta)], 0)
        terms = []
        for _ in range(3):
            term = left.astype(BF16).astype(F32)
            left = left - term
            terms.append(term)
        terms.append(jnp.zeros((LANES - 6 * n, tokens), F32))
        rest[:, rest.shape[1] - LANES :] = jnp.transpose(jnp.concatenate(terms, 0)).astype(BF16)

    by_parity(write_stats)


def stack_heads(load, first, group):
    blocks = []
    for pair in range(group // 2):
        two = load((first + 2 * pair) * HEAD_DIM, 2 * HEAD_DIM)
        left = lax.broadcasted_iota(jnp.int32, two.shape, 1) < HEAD_DIM
        zero = jnp.zeros_like(two)
        blocks += [jnp.where(left, two, zero), jnp.where(left, zero, two)]
    return jnp.concatenate(blocks, 0)


def stack_stats(stats, first, group):
    return jnp.concatenate([stats[first + g : first + g + 1] for g in range(group)], 1)


def head_grads(q, do, lse, delta, k, v):
    scores = dot(jnp.concatenate([k, k], 1), q, 1, 1)
    dprobs = dot(jnp.concatenate([v, v], 1), do, 1, 1)
    probs = jnp.exp2(scores * (LOG2E / math.sqrt(HEAD_DIM)) - lse)
    dscores = (probs * (dprobs - delta)).astype(BF16)
    dv = dot(probs.astype(BF16), do, 1, 0)
    dk = dot(dscores, q, 1, 0)
    dq = dot(k, dscores, 0, 0)
    return dk, dv, dq


def fold(even, odd):
    left = lax.broadcasted_iota(jnp.int32, even.shape, 1) < HEAD_DIM
    even, odd = (x + pltpu.roll(x, HEAD_DIM, 1) for x in (even, odd))
    return jnp.where(left, even, odd)


def side_grads(pairs, load_q, load_do, load_stats, kv, put):
    part = kv.shape[1] // 2
    width = 2 * HEAD_DIM
    for pair in pairs:
        at = pair * width
        k_two, v_two = kv[:, at : at + width], kv[:, part + at : part + at + width]
        dks, dvs = [], []
        for odd in range(2):
            first = (2 * pair + odd) * put.group
            lanes = slice(odd * HEAD_DIM, (odd + 1) * HEAD_DIM)
            dk, dv, dq = head_grads(
                stack_heads(load_q, first, put.group),
                stack_heads(load_do, first, put.group),
                *load_stats(first),
                k_two[:, lanes],
                v_two[:, lanes],
            )
            dks.append(dk)
            dvs.append(dv)
            put(first, dq)
        put.store(at, fold(*dks), fold(*dvs))


class Put:
    def __init__(self, dq_acc, group, store):
        self.dq_acc, self.group, self.store = dq_acc, group, store

    def __call__(self, first, dq):
        tok = self.dq_acc.shape[1]
        for g in range(self.group):
            rows = slice((first + g) * HEAD_DIM, (first + g + 1) * HEAD_DIM)
            self.dq_acc[rows, :] += dq[:, g * tok : (g + 1) * tok]


def turned_dq(dq_acc, first, last):
    factor = 1.0 / math.sqrt(HEAD_DIM)
    blocks = [
        jnp.transpose(dq_acc[at : at + LANES, :])
        for at in range(first * HEAD_DIM, last * HEAD_DIM, LANES)
    ]
    return (jnp.concatenate(blocks, 1) * factor).astype(BF16)


def seen(flags, which):
    return jnp.max(flags[which : which + 1, :]) > 0


def seen_sides(owners, shards):
    rank, z = lax.axis_index("blk"), lax.axis_index("ulysses")
    n_blk = lax.axis_size("blk")
    before = lax.rem(rank + n_blk - 1, n_blk)
    place = lax.div(z, shards // 2)
    mine = owners[2 * rank + place]
    return mine > owners[2 * before + place], mine > owners[2 * before + 1 - place]


def own_loaders(q, do, stats, group):
    heads = stats.shape[0] // 2
    half = heads * HEAD_DIM
    mine = parity()

    def from_half(ref):
        def load(at, size):
            return ref[:, pl.ds(pl.multiple_of(mine * half + at, size), size)]

        return load

    def load_stats(first):
        every = stats[...]
        return stack_stats(every, first, group), stack_stats(every, heads + first, group)

    return from_half(q), from_half(do), load_stats


def partner_loaders(q_in, rest, part, heads):
    tok, kv_width = rest.shape[0], 2 * part
    n_mixed = q_in.shape[0] // tok

    def loader(offset):
        def load(at, size):
            unit, lane = at // part, offset + at % part
            if unit < n_mixed:
                return q_in[unit * tok : (unit + 1) * tok, lane : lane + size]
            lane += (unit - n_mixed) * kv_width
            return rest[:, lane : lane + size]

        return load

    def load_stats(first):
        terms = jnp.transpose(rest[:, rest.shape[1] - LANES :].astype(F32))
        n = 2 * heads
        every = terms[:n] + terms[n : 2 * n] + terms[2 * n : 3 * n]
        group = part // HEAD_DIM
        return stack_stats(every, first, group), stack_stats(every, heads + first, group)

    return loader(0), loader(part), load_stats


def finish(outs, acc, at, dk, dv):
    part, tok = acc.shape[1] // 2, outs[0].shape[0]
    dk = (dk + acc[:, at : at + LANES]) * (1.0 / math.sqrt(HEAD_DIM))
    dv = dv + acc[:, part + at : part + at + LANES]
    for d, out in enumerate(outs):
        rows = slice(d * tok, (d + 1) * tok)
        out[:, at : at + LANES] = dk[rows].astype(BF16)
        out[:, part + at : part + at + LANES] = dv[rows].astype(BF16)


def own_far_kernel(side, owners, q, do, stats, *rest):
    slots = rest[:-5]
    kv, q_in, acc, dq_acc, flags = rest[-5:]
    near_seen, far_seen = seen_sides(owners, 2 * side)
    line = lax.broadcasted_iota(jnp.int32, flags.shape, 0)
    flags[...] = jnp.where(line == 0, near_seen.astype(jnp.int32), far_seen.astype(jnp.int32))
    tok, part = q.shape[0], kv.shape[1] // 2

    def sort(which):
        keys, rows = apart(which, slots, side)
        for d in range(side):
            kv[d * tok : (d + 1) * tok, :] = keys[d][...]
        for unit in range(len(rows)):
            q_in[unit * tok : (unit + 1) * tok, :] = rows[unit][...]

    by_class(sort)
    dq_acc[...] = jnp.zeros_like(dq_acc)

    def store(at, dk, dv):
        acc[:, at : at + LANES] = dk
        acc[:, part + at : part + at + LANES] = dv

    @pl.when(far_seen)
    def _():
        group = part // HEAD_DIM
        loaders = own_loaders(q, do, stats, group)
        side_grads(range(part // LANES), *loaders, kv, Put(dq_acc, group, store))


def partner_far_kernel(flags, q_in, rest, kv, acc, *outs):
    far, dq_acc = outs[:-1], outs[-1]
    tok, part = rest.shape[0], kv.shape[1] // 2
    dq_acc[...] = jnp.zeros_like(dq_acc)

    def store(at, dk, dv):
        finish(far, acc, at, dk, dv)

    @pl.when(seen(flags, 1))
    def _():
        loaders = partner_loaders(q_in, rest, part, dq_acc.shape[0] // HEAD_DIM)
        side_grads(range(part // LANES), *loaders, kv, Put(dq_acc, part // HEAD_DIM, store))

    @pl.when(jnp.logical_not(seen(flags, 1)))
    def _():
        for out in far:
            out[...] = jnp.zeros_like(out)


def partner_near_kernel(side, flags, q_in, rest, partner_dq, *refs):
    keys, refs = refs[:side], refs[side:]
    kv, acc, dq_acc = refs[-3:]
    tok, part = rest.shape[0], kv.shape[1] // 2
    heads = dq_acc.shape[0] // HEAD_DIM
    group = part // HEAD_DIM
    n_late = (len(refs) - 4) // 2
    far, far_out, dq_send = refs[:n_late], refs[n_late : 2 * n_late], refs[-4]
    dq_acc[...] = partner_dq[...]

    @pl.when(seen(flags, 0))
    def _():
        for d in range(side):
            kv[d * tok : (d + 1) * tok, :] = keys[d][...]

        def store(at, dk, dv):
            acc[:, at : at + LANES] = dk
            acc[:, part + at : part + at + LANES] = dv

        loaders = partner_loaders(q_in, rest, part, heads)
        side_grads(range(part // LANES), *loaders, kv, Put(dq_acc, group, store))

    for out, ref in zip(far_out, far):
        out[...] = ref[...]
    dq_send[...] = turned_dq(dq_acc, 0, heads)


def own_near_kernel(flags, q, do, stats, kv, acc, own_dq, *outs):
    *near, dq_own, dq_acc = outs
    part = kv.shape[1] // 2
    group = part // HEAD_DIM
    dq_acc[...] = own_dq[...]

    @pl.when(seen(flags, 0))
    def _():
        def store(at, dk, dv):
            finish(near, acc, at, dk, dv)

        loaders = own_loaders(q, do, stats, group)
        side_grads(range(part // LANES), *loaders, kv, Put(dq_acc, group, store))

    @pl.when(jnp.logical_not(seen(flags, 0)))
    def _():
        for out in near:
            out[...] = jnp.zeros_like(out)

    dq_own[...] = turned_dq(dq_acc, 0, dq_acc.shape[0] // HEAD_DIM)


def take_kernel(count, *refs):
    for ref, out in zip(refs[:count], refs[-count:]):
        out[...] = ref[...].astype(out.dtype)


def join_kernel(side, dq_own, *refs):
    far, dq_back, near = refs[:side], refs[side], refs[side + 1 : -3][::-1]
    gq, gk, gv = refs[-3:]
    half = dq_own.shape[1]
    part = gk.shape[1] // 2
    totals = []
    for odd in range(2):
        terms = [*near[odd::2], *far[odd::2]]
        totals.append(sum((ref[...].astype(F32) for ref in terms[1:]), terms[0][...].astype(F32)))

    def write(mine, other):
        gq[:, mine * half : (mine + 1) * half] = dq_own[...]
        gq[:, other * half : (other + 1) * half] = dq_back[...]
        for total, place in zip(totals, (mine, other)):
            gk[:, place * part : (place + 1) * part] = total[:, :part].astype(BF16)
            gv[:, place * part : (place + 1) * part] = total[:, part:].astype(BF16)

    by_parity(write)


def limit(mib):
    return pltpu.CompilerParams(vmem_limit_bytes=int(mib * 1024 * 1024))


def per_device(queries, key_states, value_states, attn_out, grad_out, log_sums, owners):
    n_blk, n_uly = lax.axis_size("blk"), lax.axis_size("ulysses")
    tok, width = queries.shape
    heads = log_sums.shape[1]
    kv_width = key_states.shape[1]
    half = width // 2
    side = n_uly // 2

    n_units = width // kv_width
    n_mixed = min(n_units, side)

    def flips(first, second):
        return [in_turn(which, first, second) for which in range(2)]

    def move(value, *by_kind):
        pairs = []
        for b in range(n_blk):
            for u in range(n_uly):
                step, flip = by_kind[(b + u // side) % len(by_kind)]
                pairs.append((b * n_uly + u, ((b + step) % n_blk) * n_uly + (u ^ flip)))
        return lax.ppermute(value, ("blk", "ulysses"), pairs)

    def shape(*dims, dtype=BF16):
        return jax.ShapeDtypeStruct(dims, dtype)

    def cover(flops):
        return pl.CostEstimate(flops=flops, bytes_accessed=1 << 20, transcendentals=0)

    unit = shape(tok, kv_width)
    sides = shape(side * tok, kv_width)
    sides_wide = shape(side * tok, kv_width, dtype=F32)
    dq_wide = shape(half, tok, dtype=F32)
    *slots, ready = pl.pallas_call(
        functools.partial(pack_turns_kernel, side),
        out_shape=[unit] * (side + n_mixed) + [shape(8, LANES, dtype=F32)],
        in_specs=[VMEM] * 4,
        out_specs=[VMEM] * (side + n_mixed + 1),
        compiler_params=limit(TURNS_MIB),
        name="pack_turns",
    )(queries, grad_out, key_states, value_states)
    near_same, near_other, rest, stat_own = pl.pallas_call(
        functools.partial(pack_kernel, n_mixed),
        out_shape=[unit] * 2
        + [
            shape(tok, (n_units - n_mixed) * kv_width + LANES),
            shape(heads, tok, dtype=F32),
        ],
        in_specs=[VMEM] * 6 + [ANY],
        out_specs=[VMEM] * 4,
        compiler_params=limit(PACK_MIB),
        name="pack",
    )(
        queries, grad_out, attn_out, jnp.transpose(log_sums), key_states, value_states, ready
    )
    turns = flips([(1, d) for d in range(side, n_uly)], [(0, 1)] * n_mixed)
    slots = [move(x, one, two) for x, one, two in zip(slots, *turns)]
    rest = move(rest, (0, 1))
    near = [move(near_other if d % 2 else near_same, (1, d)) for d in range(side)]
    outs = [sides, shape(n_mixed * tok, kv_width), sides_wide, dq_wide]
    outs.append(shape(8, LANES, dtype=jnp.int32))
    kv_far, q_in, acc_far, own_dq, flags = pl.pallas_call(
        functools.partial(own_far_kernel, side),
        out_shape=outs,
        in_specs=[SMEM] + [VMEM] * (3 + side + n_mixed),
        out_specs=[VMEM] * len(outs),
        compiler_params=limit(32),
        cost_estimate=cover(OWN),
        name="own_far",
    )(owners, queries, grad_out, stat_own, *slots)
    *far, partner_dq = pl.pallas_call(
        partner_far_kernel,
        out_shape=[unit] * side + [dq_wide],
        in_specs=[VMEM] * 5,
        out_specs=[VMEM] * (side + 1),
        compiler_params=limit(32),
        cost_estimate=cover(PARTNER),
        name="far",
    )(flags, q_in, rest, kv_far, acc_far)
    n_early = side // 2
    n_late = side - n_early
    early = [move(x, (-1, side + d)) for d, x in enumerate(far[:n_early])]
    outs = [unit] * n_late + [shape(tok, half), sides, sides_wide]
    *late, dq_back, kv_near, acc_near = pl.pallas_call(
        functools.partial(partner_near_kernel, side),
        out_shape=outs,
        in_specs=[VMEM] * (4 + side + n_late),
        out_specs=[VMEM] * len(outs),
        scratch_shapes=[pltpu.VMEM(dq_wide.shape, F32)],
        compiler_params=limit(32),
        cost_estimate=cover(PARTNER),
        name="near",
    )(flags, q_in, rest, partner_dq, *near, *far[n_early:])
    late = [move(x, (-1, side + n_early + d)) for d, x in enumerate(late)]
    dq_back = move(dq_back, (0, 1))
    outs = [unit] * side + [shape(tok, half)]
    *near, dq_own = pl.pallas_call(
        own_near_kernel,
        out_shape=outs,
        in_specs=[VMEM] * 7,
        out_specs=[VMEM] * len(outs),
        scratch_shapes=[pltpu.VMEM(dq_wide.shape, F32)],
        compiler_params=limit(32),
        cost_estimate=cover(NONE),
        name="own_near",
    )(flags, queries, grad_out, stat_own, kv_near, acc_near, own_dq)
    near = [move(near[d], (-1, d)) for d in reversed(range(side))][::-1]

    def take(first, outs, flops, *after):
        return pl.pallas_call(
            functools.partial(take_kernel, len(first)),
            out_shape=outs,
            in_specs=[VMEM] * len(first) + [ANY] * len(after),
            out_specs=[VMEM] * len(first),
            compiler_params=limit(8),
            cost_estimate=cover(flops),
            name="take",
        )(*first, *after)

    wide = shape(tok, kv_width, dtype=F32)
    early = take(early, [wide] * n_early, SHORT)
    late = take(late, [wide] * n_late, SHORT, early[0])
    (dq_back,) = take([dq_back], [shape(tok, half)], LONG, late[0])
    ins = [dq_own, *early, *late, dq_back, *near[::-1]]
    return tuple(
        pl.pallas_call(
            functools.partial(join_kernel, side),
            out_shape=[shape(tok, width), shape(tok, kv_width), shape(tok, kv_width)],
            in_specs=[VMEM] * len(ins),
            out_specs=[VMEM] * 3,
            compiler_params=limit(8),
            name="join",
        )(*ins)
    )


def solution(mesh):
    rows = P(("blk", "ulysses"), None)
    return jax.shard_map(
        per_device,
        mesh=mesh,
        in_specs=(rows, rows, rows, rows, rows, rows, P()),
        out_specs=(rows, rows, rows),
        check_vma=False,
    )
```

```python
import functools
import math

import jax
import jax.numpy as jnp
from jax import lax
from jax.experimental import pallas as pl
from jax.experimental.pallas import tpu as pltpu
from jax.sharding import PartitionSpec as P

HEAD_DIM = 64
LANES = 128
PACK_MIB = 60
TURNS_MIB = 53.4
NONE, SHORT, OWN, PARTNER, LONG = 1 << 20, 7 << 27, 1 << 31, 1 << 31, 1 << 34
LOG2E = math.log2(math.e)
BF16 = jnp.bfloat16
F32 = jnp.float32
ANY = pl.BlockSpec(memory_space=pl.ANY)
VMEM = pl.BlockSpec(memory_space=pltpu.VMEM)
SMEM = pl.BlockSpec(memory_space=pltpu.SMEM)


def dot(a, b, a_dim, b_dim):
    return lax.dot_general(
        a, b, (((a_dim,), (b_dim,)), ((), ())), preferred_element_type=F32
    )


def parity():
    return lax.rem(lax.axis_index("ulysses"), 2)


def by_parity(write):
    for mine in range(2):

        @pl.when(parity() == mine)
        def _():
            write(mine, 1 - mine)


def by_class(write):
    side = lax.div(lax.axis_index("ulysses"), lax.axis_size("ulysses") // 2)
    odd = lax.rem(lax.axis_index("blk") + side, 2)
    for which in range(2):

        @pl.when(odd == which)
        def _():
            write(which)


def in_turn(which, first, second):
    return [*first, *second] if which == 0 else [*second, *first]


def apart(which, refs, n_first):
    n_second = len(refs) - n_first
    if which == 0:
        return refs[:n_first], refs[n_first:]
    return refs[n_second:], refs[:n_second]


def cut(ref, which, size, at=0, wide=None):
    wide = size if wide is None else wide
    return ref[:, pl.ds(pl.multiple_of(which * size + at, wide), wide)]


def put_keys(out, k, v, which):
    part = k.shape[1] // 2
    out[:, :part] = cut(k, which, part)
    out[:, part:] = cut(v, which, part)


def put_rows(out, q, do, part, unit, at=0):
    half = q.shape[1] // 2
    other = 1 - parity()
    out[:, at : at + part] = cut(q, other, half, unit * part, part)
    out[:, at + part : at + 2 * part] = cut(do, other, half, unit * part, part)


def pack_turns_kernel(side, q, do, k, v, *slots):
    *slots, ready = slots
    ready[...] = jnp.zeros_like(ready)
    mine = parity()

    def write(which):
        keys, rows = apart(which, slots, side)
        for d in range(side):
            put_keys(keys[d], k, v, mine if d % 2 == 0 else 1 - mine)
        for unit in range(len(rows)):
            put_rows(rows[unit], q, do, k.shape[1] // 2, unit)

    by_class(write)


def pack_kernel(n_mixed, q, do, o, sums, k, v, _, near_same, near_other, rest, stat_own):
    tokens, width = do.shape
    heads = sums.shape[0]
    part = k.shape[1] // 2
    n = heads // 2
    put_keys(near_same, k, v, parity())
    put_keys(near_other, k, v, 1 - parity())
    for unit in range(n_mixed, width // 2 // part):
        put_rows(rest, q, do, part, unit, (unit - n_mixed) * 2 * part)

    row = lax.broadcasted_iota(jnp.int32, (heads, width), 0)
    col = lax.broadcasted_iota(jnp.int32, (heads, width), 1)
    pick = jnp.where(col // HEAD_DIM == row, 1.0, 0.0).astype(BF16)
    prod = do[...].astype(F32) * o[...].astype(F32)
    high = prod.astype(BF16)
    low = (prod - high.astype(F32)).astype(BF16)
    delta = dot(pick, high, 1, 1) + dot(pick, low, 1, 1)
    lse = sums[...] * LOG2E

    def write_stats(mine, other):
        stat_own[:n, :] = lse[mine * n : (mine + 1) * n, :]
        stat_own[n:, :] = delta[mine * n : (mine + 1) * n, :]
        left = jnp.concatenate([x[other * n : (other + 1) * n, :] for x in (lse, delta)], 0)
        terms = []
        for _ in range(3):
            term = left.astype(BF16).astype(F32)
            left = left - term
            terms.append(term)
        terms.append(jnp.zeros((LANES - 6 * n, tokens), F32))
        rest[:, rest.shape[1] - LANES :] = jnp.transpose(jnp.concatenate(terms, 0)).astype(BF16)

    by_parity(write_stats)


def stack_heads(load, first, group):
    blocks = []
    for pair in range(group // 2):
        two = load((first + 2 * pair) * HEAD_DIM, 2 * HEAD_DIM)
        left = lax.broadcasted_iota(jnp.int32, two.shape, 1) < HEAD_DIM
        zero = jnp.zeros_like(two)
        blocks += [jnp.where(left, two, zero), jnp.where(left, zero, two)]
    return jnp.concatenate(blocks, 0)


def stack_stats(stats, first, group):
    return jnp.concatenate([stats[first + g : first + g + 1] for g in range(group)], 1)


def head_grads(q, do, lse, delta, k, v):
    scores = dot(jnp.concatenate([k, k], 1), q, 1, 1)
    dprobs = dot(jnp.concatenate([v, v], 1), do, 1, 1)
    probs = jnp.exp2(scores * (LOG2E / math.sqrt(HEAD_DIM)) - lse)
    dscores = (probs * (dprobs - delta)).astype(BF16)
    dv = dot(probs.astype(BF16), do, 1, 0)
    dk = dot(dscores, q, 1, 0)
    dq = dot(k, dscores, 0, 0)
    return dk, dv, dq


def fold(even, odd):
    left = lax.broadcasted_iota(jnp.int32, even.shape, 1) < HEAD_DIM
    even, odd = (x + pltpu.roll(x, HEAD_DIM, 1) for x in (even, odd))
    return jnp.where(left, even, odd)


def side_grads(pairs, load_q, load_do, load_stats, kv, put):
    part = kv.shape[1] // 2
    width = 2 * HEAD_DIM
    for pair in pairs:
        at = pair * width
        k_two, v_two = kv[:, at : at + width], kv[:, part + at : part + at + width]
        dks, dvs = [], []
        for odd in range(2):
            first = (2 * pair + odd) * put.group
            lanes = slice(odd * HEAD_DIM, (odd + 1) * HEAD_DIM)
            dk, dv, dq = head_grads(
                stack_heads(load_q, first, put.group),
                stack_heads(load_do, first, put.group),
                *load_stats(first),
                k_two[:, lanes],
                v_two[:, lanes],
            )
            dks.append(dk)
            dvs.append(dv)
            put(first, dq)
        put.store(at, fold(*dks), fold(*dvs))


class Put:
    def __init__(self, dq_acc, group, store):
        self.dq_acc, self.group, self.store = dq_acc, group, store

    def __call__(self, first, dq):
        tok = self.dq_acc.shape[1]
        for g in range(self.group):
            rows = slice((first + g) * HEAD_DIM, (first + g + 1) * HEAD_DIM)
            self.dq_acc[rows, :] += dq[:, g * tok : (g + 1) * tok]


def turned_dq(dq_acc, first, last):
    factor = 1.0 / math.sqrt(HEAD_DIM)
    blocks = [
        jnp.transpose(dq_acc[at : at + LANES, :])
        for at in range(first * HEAD_DIM, last * HEAD_DIM, LANES)
    ]
    return (jnp.concatenate(blocks, 1) * factor).astype(BF16)


def seen(flags, which):
    return jnp.max(flags[which : which + 1, :]) > 0


def seen_sides(owners, shards):
    rank, z = lax.axis_index("blk"), lax.axis_index("ulysses")
    n_blk = lax.axis_size("blk")
    before = lax.rem(rank + n_blk - 1, n_blk)
    place = lax.div(z, shards // 2)
    mine = owners[2 * rank + place]
    return mine > owners[2 * before + place], mine > owners[2 * before + 1 - place]


def own_loaders(q, do, stats, group):
    heads = stats.shape[0] // 2
    half = heads * HEAD_DIM
    mine = parity()

    def from_half(ref):
        def load(at, size):
            return ref[:, pl.ds(pl.multiple_of(mine * half + at, size), size)]

        return load

    def load_stats(first):
        every = stats[...]
        return stack_stats(every, first, group), stack_stats(every, heads + first, group)

    return from_half(q), from_half(do), load_stats


def partner_loaders(q_in, rest, part, heads):
    tok, kv_width = rest.shape[0], 2 * part
    n_mixed = q_in.shape[0] // tok

    def loader(offset):
        def load(at, size):
            unit, lane = at // part, offset + at % part
            if unit < n_mixed:
                return q_in[unit * tok : (unit + 1) * tok, lane : lane + size]
            lane += (unit - n_mixed) * kv_width
            return rest[:, lane : lane + size]

        return load

    terms = jnp.transpose(rest[:, rest.shape[1] - LANES :].astype(F32))
    n = 2 * heads
    every = terms[:n] + terms[n : 2 * n] + terms[2 * n : 3 * n]

    def load_stats(first):
        group = part // HEAD_DIM
        return stack_stats(every, first, group), stack_stats(every, heads + first, group)

    return loader(0), loader(part), load_stats


def finish(outs, acc, at, dk, dv):
    part, tok = acc.shape[1] // 2, outs[0].shape[0]
    dk = (dk + acc[:, at : at + LANES]) * (1.0 / math.sqrt(HEAD_DIM))
    dv = dv + acc[:, part + at : part + at + LANES]
    for d, out in enumerate(outs):
        rows = slice(d * tok, (d + 1) * tok)
        out[:, at : at + LANES] = dk[rows].astype(BF16)
        out[:, part + at : part + at + LANES] = dv[rows].astype(BF16)


def own_far_kernel(side, owners, q, do, stats, *rest):
    slots = rest[:-5]
    kv, q_in, acc, dq_acc, flags = rest[-5:]
    near_seen, far_seen = seen_sides(owners, 2 * side)
    line = lax.broadcasted_iota(jnp.int32, flags.shape, 0)
    flags[...] = jnp.where(line == 0, near_seen.astype(jnp.int32), far_seen.astype(jnp.int32))
    tok, part = q.shape[0], kv.shape[1] // 2

    def sort(which):
        keys, rows = apart(which, slots, side)
        for d in range(side):
            kv[d * tok : (d + 1) * tok, :] = keys[d][...]
        for unit in range(len(rows)):
            q_in[unit * tok : (unit + 1) * tok, :] = rows[unit][...]

    by_class(sort)
    dq_acc[...] = jnp.zeros_like(dq_acc)

    def store(at, dk, dv):
        acc[:, at : at + LANES] = dk
        acc[:, part + at : part + at + LANES] = dv

    @pl.when(far_seen)
    def _():
        group = part // HEAD_DIM
        loaders = own_loaders(q, do, stats, group)
        side_grads(range(part // LANES), *loaders, kv, Put(dq_acc, group, store))


def partner_far_kernel(flags, q_in, rest, kv, acc, *outs):
    far, dq_acc = outs[:-1], outs[-1]
    tok, part = rest.shape[0], kv.shape[1] // 2
    dq_acc[...] = jnp.zeros_like(dq_acc)

    def store(at, dk, dv):
        finish(far, acc, at, dk, dv)

    @pl.when(seen(flags, 1))
    def _():
        loaders = partner_loaders(q_in, rest, part, dq_acc.shape[0] // HEAD_DIM)
        side_grads(range(part // LANES), *loaders, kv, Put(dq_acc, part // HEAD_DIM, store))

    @pl.when(jnp.logical_not(seen(flags, 1)))
    def _():
        for out in far:
            out[...] = jnp.zeros_like(out)


def partner_near_kernel(side, flags, q_in, rest, partner_dq, *refs):
    keys, refs = refs[:side], refs[side:]
    kv, acc, dq_acc = refs[-3:]
    tok, part = rest.shape[0], kv.shape[1] // 2
    heads = dq_acc.shape[0] // HEAD_DIM
    group = part // HEAD_DIM
    n_late = (len(refs) - 4) // 2
    far, far_out, dq_send = refs[:n_late], refs[n_late : 2 * n_late], refs[-4]
    dq_acc[...] = partner_dq[...]

    @pl.when(seen(flags, 0))
    def _():
        for d in range(side):
            kv[d * tok : (d + 1) * tok, :] = keys[d][...]

        def store(at, dk, dv):
            acc[:, at : at + LANES] = dk
            acc[:, part + at : part + at + LANES] = dv

        loaders = partner_loaders(q_in, rest, part, heads)
        side_grads(range(part // LANES), *loaders, kv, Put(dq_acc, group, store))

    for out, ref in zip(far_out, far):
        out[...] = ref[...]
    dq_send[...] = turned_dq(dq_acc, 0, heads)


def own_near_kernel(flags, q, do, stats, kv, acc, own_dq, *outs):
    *near, dq_own, dq_acc = outs
    part = kv.shape[1] // 2
    group = part // HEAD_DIM
    dq_acc[...] = own_dq[...]

    @pl.when(seen(flags, 0))
    def _():
        def store(at, dk, dv):
            finish(near, acc, at, dk, dv)

        loaders = own_loaders(q, do, stats, group)
        side_grads(range(part // LANES), *loaders, kv, Put(dq_acc, group, store))

    @pl.when(jnp.logical_not(seen(flags, 0)))
    def _():
        for out in near:
            out[...] = jnp.zeros_like(out)

    dq_own[...] = turned_dq(dq_acc, 0, dq_acc.shape[0] // HEAD_DIM)


def take_kernel(count, *refs):
    for ref, out in zip(refs[:count], refs[-count:]):
        out[...] = ref[...].astype(out.dtype)


def join_kernel(side, dq_own, *refs):
    far, dq_back, near = refs[:side], refs[side], refs[side + 1 : -3][::-1]
    gq, gk, gv = refs[-3:]
    half = dq_own.shape[1]
    part = gk.shape[1] // 2
    totals = []
    for odd in range(2):
        terms = [*near[odd::2], *far[odd::2]]
        totals.append(sum((ref[...].astype(F32) for ref in terms[1:]), terms[0][...].astype(F32)))

    def write(mine, other):
        gq[:, mine * half : (mine + 1) * half] = dq_own[...]
        gq[:, other * half : (other + 1) * half] = dq_back[...]
        for total, place in zip(totals, (mine, other)):
            gk[:, place * part : (place + 1) * part] = total[:, :part].astype(BF16)
            gv[:, place * part : (place + 1) * part] = total[:, part:].astype(BF16)

    by_parity(write)


def limit(mib):
    return pltpu.CompilerParams(vmem_limit_bytes=int(mib * 1024 * 1024))


def per_device(queries, key_states, value_states, attn_out, grad_out, log_sums, owners):
    n_blk, n_uly = lax.axis_size("blk"), lax.axis_size("ulysses")
    tok, width = queries.shape
    heads = log_sums.shape[1]
    kv_width = key_states.shape[1]
    half = width // 2
    side = n_uly // 2

    n_units = width // kv_width
    n_mixed = min(n_units, side)

    def flips(first, second):
        return [in_turn(which, first, second) for which in range(2)]

    def move(value, *by_kind):
        pairs = []
        for b in range(n_blk):
            for u in range(n_uly):
                step, flip = by_kind[(b + u // side) % len(by_kind)]
                pairs.append((b * n_uly + u, ((b + step) % n_blk) * n_uly + (u ^ flip)))
        return lax.ppermute(value, ("blk", "ulysses"), pairs)

    def shape(*dims, dtype=BF16):
        return jax.ShapeDtypeStruct(dims, dtype)

    def cover(flops):
        return pl.CostEstimate(flops=flops, bytes_accessed=1 << 20, transcendentals=0)

    unit = shape(tok, kv_width)
    sides = shape(side * tok, kv_width)
    sides_wide = shape(side * tok, kv_width, dtype=F32)
    dq_wide = shape(half, tok, dtype=F32)
    *slots, ready = pl.pallas_call(
        functools.partial(pack_turns_kernel, side),
        out_shape=[unit] * (side + n_mixed) + [shape(8, LANES, dtype=F32)],
        in_specs=[VMEM] * 4,
        out_specs=[VMEM] * (side + n_mixed + 1),
        compiler_params=limit(TURNS_MIB),
        name="pack_turns",
    )(queries, grad_out, key_states, value_states)
    near_same, near_other, rest, stat_own = pl.pallas_call(
        functools.partial(pack_kernel, n_mixed),
        out_shape=[unit] * 2
        + [
            shape(tok, (n_units - n_mixed) * kv_width + LANES),
            shape(heads, tok, dtype=F32),
        ],
        in_specs=[VMEM] * 6 + [ANY],
        out_specs=[VMEM] * 4,
        compiler_params=limit(PACK_MIB),
        name="pack",
    )(
        queries, grad_out, attn_out, jnp.transpose(log_sums), key_states, value_states, ready
    )
    turns = flips([(1, d) for d in range(side, n_uly)], [(0, 1)] * n_mixed)
    slots = [move(x, one, two) for x, one, two in zip(slots, *turns)]
    rest = move(rest, (0, 1))
    near = [move(near_other if d % 2 else near_same, (1, d)) for d in range(side)]
    outs = [sides, shape(n_mixed * tok, kv_width), sides_wide, dq_wide]
    outs.append(shape(8, LANES, dtype=jnp.int32))
    kv_far, q_in, acc_far, own_dq, flags = pl.pallas_call(
        functools.partial(own_far_kernel, side),
        out_shape=outs,
        in_specs=[SMEM] + [VMEM] * (3 + side + n_mixed),
        out_specs=[VMEM] * len(outs),
        compiler_params=limit(32),
        cost_estimate=cover(OWN),
        name="own_far",
    )(owners, queries, grad_out, stat_own, *slots)
    *far, partner_dq = pl.pallas_call(
        partner_far_kernel,
        out_shape=[unit] * side + [dq_wide],
        in_specs=[VMEM] * 5,
        out_specs=[VMEM] * (side + 1),
        compiler_params=limit(32),
        cost_estimate=cover(PARTNER),
        name="far",
    )(flags, q_in, rest, kv_far, acc_far)
    n_early = side // 2
    n_late = side - n_early
    early = [move(x, (-1, side + d)) for d, x in enumerate(far[:n_early])]
    outs = [unit] * n_late + [shape(tok, half), sides, sides_wide]
    *late, dq_back, kv_near, acc_near = pl.pallas_call(
        functools.partial(partner_near_kernel, side),
        out_shape=outs,
        in_specs=[VMEM] * (4 + side + n_late),
        out_specs=[VMEM] * len(outs),
        scratch_shapes=[pltpu.VMEM(dq_wide.shape, F32)],
        compiler_params=limit(32),
        cost_estimate=cover(PARTNER),
        name="near",
    )(flags, q_in, rest, partner_dq, *near, *far[n_early:])
    late = [move(x, (-1, side + n_early + d)) for d, x in enumerate(late)]
    dq_back = move(dq_back, (0, 1))
    outs = [unit] * side + [shape(tok, half)]
    *near, dq_own = pl.pallas_call(
        own_near_kernel,
        out_shape=outs,
        in_specs=[VMEM] * 7,
        out_specs=[VMEM] * len(outs),
        scratch_shapes=[pltpu.VMEM(dq_wide.shape, F32)],
        compiler_params=limit(32),
        cost_estimate=cover(NONE),
        name="own_near",
    )(flags, queries, grad_out, stat_own, kv_near, acc_near, own_dq)
    near = [move(near[d], (-1, d)) for d in reversed(range(side))][::-1]

    def take(first, outs, flops, *after):
        return pl.pallas_call(
            functools.partial(take_kernel, len(first)),
            out_shape=outs,
            in_specs=[VMEM] * len(first) + [ANY] * len(after),
            out_specs=[VMEM] * len(first),
            compiler_params=limit(8),
            cost_estimate=cover(flops),
            name="take",
        )(*first, *after)

    wide = shape(tok, kv_width, dtype=F32)
    early = take(early, [wide] * n_early, SHORT)
    late = take(late, [wide] * n_late, SHORT, early[0])
    (dq_back,) = take([dq_back], [shape(tok, half)], LONG, late[0])
    ins = [dq_own, *early, *late, dq_back, *near[::-1]]
    return tuple(
        pl.pallas_call(
            functools.partial(join_kernel, side),
            out_shape=[shape(tok, width), shape(tok, kv_width), shape(tok, kv_width)],
            in_specs=[VMEM] * len(ins),
            out_specs=[VMEM] * 3,
            compiler_params=limit(8),
            name="join",
        )(*ins)
    )


def solution(mesh):
    rows = P(("blk", "ulysses"), None)
    return jax.shard_map(
        per_device,
        mesh=mesh,
        in_specs=(rows, rows, rows, rows, rows, rows, P()),
        out_specs=(rows, rows, rows),
        check_vma=False,
    )
```
